32 devices in a mesh: dp: 8 (over y, x, core), mp: 4 (over z).
Axes of the slice: x: 2, y: 2, z: 4, core: 2. Of those that a mesh axis runs over, the one named last changes fastest.
Arguments:
- token_ids: int32 [24576], P(('dp', 'mp')), may hold values from 0 to 26
- timesteps: int32 [24], P('dp'), may hold values from 1 to 1000
- importance: float32 [24], P('dp'), may hold values from 0.5 to 2
- cotangent: bfloat16 [24576, 512], P(('dp', 'mp')), may hold values from -6 to 6
- qkv_weight: float32 [2, 512, 3, 512], P(None, 'dp', None, 'mp'), may hold values from -0.25 to 0.25
- out_weight: float32 [2, 512, 512], P(None, 'mp', 'dp'), may hold values from -0.25 to 0.25
- up_weight: float32 [2, 512, 2048], P(None, 'dp', 'mp'), may hold values from -0.25 to 0.25
- down_weight: float32 [2, 2048, 512], P(None, 'mp', 'dp'), may hold values from -0.25 to 0.25
- norm_params: float32 [2, 4, 512], replicated, may hold values from -0.5 to 1.3, as said below
- embed_table: float32 [27, 512], replicated, may hold values from -6 to 6
- qkv_first: float32 [2, 512, 3, 512], P(None, 'dp', None, 'mp'), as said below
- qkv_second: float32 [2, 512, 3, 512], P(None, 'dp', None, 'mp'), as said below
- out_first: float32 [2, 512, 512], P(None, 'mp', 'dp'), as said below
- out_second: float32 [2, 512, 512], P(None, 'mp', 'dp'), as said below
- up_first: float32 [2, 512, 2048], P(None, 'dp', 'mp'), as said below
- up_second: float32 [2, 512, 2048], P(None, 'dp', 'mp'), as said below
- down_first: float32 [2, 2048, 512], P(None, 'mp', 'dp'), as said below
- down_second: float32 [2, 2048, 512], P(None, 'mp', 'dp'), as said below
- norm_first: float32 [2, 4, 512], replicated, as said below
- norm_second: float32 [2, 4, 512], replicated, as said below
- embed_first: float32 [27, 512], replicated, as said below
- embed_second: float32 [27, 512], replicated, as said below
Outputs:
- activations: float32 [24576, 512], P(('dp', 'mp'))
- input_grad: float32 [24576, 512], P(('dp', 'mp'))
- qkv_master: float32 [2, 512, 3, 512], P(None, 'dp', None, 'mp')
- qkv_mean: float32 [2, 512, 3, 512], P(None, 'dp', None, 'mp')
- qkv_square: float32 [2, 512, 3, 512], P(None, 'dp', None, 'mp')
- qkv_copy: bfloat16 [2, 512, 3, 512], P(None, 'dp', None, 'mp')
- out_master: float32 [2, 512, 512], P(None, 'mp', 'dp')
- out_mean: float32 [2, 512, 512], P(None, 'mp', 'dp')
- out_square: float32 [2, 512, 512], P(None, 'mp', 'dp')
- out_copy: bfloat16 [2, 512, 512], P(None, 'mp', 'dp')
- up_master: float32 [2, 512, 2048], P(None, 'dp', 'mp')
- up_mean: float32 [2, 512, 2048], P(None, 'dp', 'mp')
- up_square: float32 [2, 512, 2048], P(None, 'dp', 'mp')
- up_copy: bfloat16 [2, 512, 2048], P(None, 'dp', 'mp')
- down_master: float32 [2, 2048, 512], P(None, 'mp', 'dp')
- down_mean: float32 [2, 2048, 512], P(None, 'mp', 'dp')
- down_square: float32 [2, 2048, 512], P(None, 'mp', 'dp')
- down_copy: bfloat16 [2, 2048, 512], P(None, 'mp', 'dp')
- norm_master: float32 [2, 4, 512], replicated
- norm_mean: float32 [2, 4, 512], replicated
- norm_square: float32 [2, 4, 512], replicated
- embed_master: float32 [27, 512], replicated
- embed_mean: float32 [27, 512], replicated
- embed_square: float32 [27, 512], replicated
The draws below stay inside these ranges and needn't reach their ends.
Inputs may be any that keep to these rules, and one draw needn't show every extreme that they name: `norm_params`: rows 0 and 2 of each layer are gains, rows 1 and 3 shifts. `qkv_first`: entries of either sign, none zero. `qkv_second`: positive entries. `out_first`: entries of either sign, none zero. `out_second`: positive entries. `up_first`: entries of either sign, none zero. `up_second`: positive entries. `down_first`: entries of either sign, none zero. `down_second`: positive entries. `norm_first`: entries of either sign, none zero. `norm_second`: positive entries. `embed_first`: entries of either sign, none zero. `embed_second`: positive entries.
All inputs are finite; a program needn't handle non-finite values.
Results may differ from the reference program's by a relative error of at most 0.028.
Values may be sent and summed in bfloat16 or wider, within the bound.
No kernel may reach another device: no remote copies, remote signals or barrier semaphores. Data moves between devices by JAX's collectives and lax.ppermute only.
A program may use at most 192 MiB of HBM per device.

```python
import math
import jax
import jax.numpy as jnp
from jax import lax

HEADS = 8
HEAD_DIM = 64
FF = 2048
VOCAB = 27
LAYERS = 2
LEN = 1024
STEP = 10
D = 512
SEQS = 24
TOKENS = 24576


back_scale = 1.5


def first_moment(key, layout, amount):
    magnitude = jax.random.uniform(jax.random.fold_in(key, 11), layout, jnp.float32, 0.5, 1.5)
    flips = jax.random.bernoulli(jax.random.fold_in(key, 12), 0.5, layout)
    return amount * magnitude * jnp.where(flips, 1.0, -1.0)


def second_moment(key, layout, amount):
    return amount * amount * jax.random.uniform(jax.random.fold_in(key, 13), layout, jnp.float32, 1.0, 4.0)


def qkv_amount():
    return 1.2 * back_scale * math.sqrt(TOKENS)


def out_amount():
    return back_scale * 1.6 * math.sqrt(TOKENS / LEN)


def up_amount():
    return 1.2 * back_scale * math.sqrt(D / FF) * math.sqrt(TOKENS)


def down_amount():
    return 0.6 * back_scale * math.sqrt(TOKENS)


def norm_amount():
    return jnp.array([1.6, 1.6, 0.8, 0.8], jnp.float32)[None, :, None] * back_scale * math.sqrt(TOKENS)


def embed_amount():
    return back_scale * math.sqrt(TOKENS / VOCAB)


def draw_norm_params(key, part):
    key = jax.random.fold_in(key, 31)
    gains = jax.random.uniform(jax.random.fold_in(key, 21), (LAYERS, 4, D), jnp.float32, 0.7, 1.3)
    shifts = jax.random.uniform(jax.random.fold_in(key, 22), (LAYERS, 4, D), jnp.float32, -0.5, 0.5)
    row_kind = jnp.arange(4, dtype=jnp.int32)[None, :, None]
    return jnp.where(row_kind % 2 == 0, gains, shifts)


def draw_qkv_first(key, part):
    key = jax.random.fold_in(key, 32)
    return first_moment(key, (LAYERS, D, 3, D), qkv_amount())


def draw_qkv_second(key, part):
    key = jax.random.fold_in(key, 33)
    return second_moment(key, (LAYERS, D, 3, D), qkv_amount())


def draw_out_first(key, part):
    key = jax.random.fold_in(key, 34)
    return first_moment(key, (LAYERS, D, D), out_amount())


def draw_out_second(key, part):
    key = jax.random.fold_in(key, 35)
    return second_moment(key, (LAYERS, D, D), out_amount())


def draw_up_first(key, part):
    key = jax.random.fold_in(key, 36)
    return first_moment(key, (LAYERS, D, FF), up_amount())


def draw_up_second(key, part):
    key = jax.random.fold_in(key, 37)
    return second_moment(key, (LAYERS, D, FF), up_amount())


def draw_down_first(key, part):
    key = jax.random.fold_in(key, 38)
    return first_moment(key, (LAYERS, FF, D), down_amount())


def draw_down_second(key, part):
    key = jax.random.fold_in(key, 39)
    return second_moment(key, (LAYERS, FF, D), down_amount())


def draw_norm_first(key, part):
    key = jax.random.fold_in(key, 40)
    return first_moment(key, (LAYERS, 4, D), norm_amount())


def draw_norm_second(key, part):
    key = jax.random.fold_in(key, 41)
    return second_moment(key, (LAYERS, 4, D), norm_amount())


def draw_embed_first(key, part):
    key = jax.random.fold_in(key, 42)
    return first_moment(key, (VOCAB, D), embed_amount())


def draw_embed_second(key, part):
    key = jax.random.fold_in(key, 43)
    return second_moment(key, (VOCAB, D), embed_amount())


def touch_ends(entries, rng, smallest, high):
    index_at = [jax.random.randint(jax.random.fold_in(rng, axis), (), 0, length) for axis, length in enumerate(entries.shape)]
    longest = entries.shape.index(max(entries.shape))
    neighbour = index_at[:longest] + [(index_at[longest] + 1) % entries.shape[longest]] + index_at[longest + 1:]
    return entries.at[tuple(index_at)].set(smallest).at[tuple(neighbour)].set(high)


def block_levels(own_key, dims, pieces, least, high):
    gain = 1.0
    for position, blocks in pieces:
        heights = jax.random.uniform(jax.random.fold_in(jax.random.fold_in(own_key, 6), position), (blocks,), jnp.float32, least / len(pieces), high / len(pieces))
        gain = gain * jnp.repeat(jnp.exp(heights), dims[position] // blocks).reshape((-1,) + (1,) * (len(dims) - 1 - position))
    return gain


def normal_values(stream_key, dims, deviation, bound, pieces=(), kind=jnp.bfloat16):
    values = deviation * jax.random.normal(stream_key, dims, jnp.float32)
    if pieces:
        values = values * block_levels(stream_key, dims, pieces, -0.22, 0.18)
    return jnp.clip(values, -bound, bound).astype(kind)


def setup_inputs(seed: int = 0) -> dict:
    key_of = jax.random.split(jax.random.key(seed), 23)
    token_ids = touch_ends(jax.random.randint(key_of[0], (TOKENS,), 0, VOCAB), jax.random.fold_in(key_of[0], 1), 0, VOCAB - 1).astype(jnp.int32)
    timesteps = touch_ends(jax.random.randint(key_of[1], (SEQS,), 1, 1001), jax.random.fold_in(key_of[1], 1), 1, 1000).astype(jnp.int32)
    importance = jnp.clip(jnp.exp(math.log(2.0) - 1.3862944 * jax.random.uniform(key_of[2], (SEQS,), jnp.float32) ** block_levels(key_of[2], (SEQS,), ((0, 8),), -0.2, 0.2)), 0.5, 2.0)
    cotangent = normal_values(key_of[3], (TOKENS, D), 1.0, 6.0, ((0, 32),))
    qkv_weight = normal_values(key_of[4], (LAYERS, D, 3, D), D ** -0.5, 0.25, ((1, 8), (3, 4)), jnp.float32)
    out_weight = normal_values(key_of[5], (LAYERS, D, D), D ** -0.5, 0.25, ((1, 4), (2, 8)), jnp.float32)
    up_weight = normal_values(key_of[6], (LAYERS, D, FF), D ** -0.5, 0.25, ((1, 8), (2, 4)), jnp.float32)
    down_weight = normal_values(key_of[7], (LAYERS, FF, D), (FF // 4) ** -0.5, 0.25, ((1, 4), (2, 8)), jnp.float32)
    norm_params = draw_norm_params(jax.random.fold_in(key_of[22], 71), 0)
    embed_table = normal_values(key_of[9], (VOCAB, D), 1.0, 6.0, (), jnp.float32)
    qkv_first = draw_qkv_first(jax.random.fold_in(key_of[22], 71), 0)
    qkv_second = draw_qkv_second(jax.random.fold_in(key_of[22], 71), 0)
    out_first = draw_out_first(jax.random.fold_in(key_of[22], 71), 0)
    out_second = draw_out_second(jax.random.fold_in(key_of[22], 71), 0)
    up_first = draw_up_first(jax.random.fold_in(key_of[22], 71), 0)
    up_second = draw_up_second(jax.random.fold_in(key_of[22], 71), 0)
    down_first = draw_down_first(jax.random.fold_in(key_of[22], 71), 0)
    down_second = draw_down_second(jax.random.fold_in(key_of[22], 71), 0)
    norm_first = draw_norm_first(jax.random.fold_in(key_of[22], 71), 0)
    norm_second = draw_norm_second(jax.random.fold_in(key_of[22], 71), 0)
    embed_first = draw_embed_first(jax.random.fold_in(key_of[22], 71), 0)
    embed_second = draw_embed_second(jax.random.fold_in(key_of[22], 71), 0)
    return {"token_ids": token_ids, "timesteps": timesteps, "importance": importance, "cotangent": cotangent, "qkv_weight": qkv_weight, "out_weight": out_weight, "up_weight": up_weight, "down_weight": down_weight, "norm_params": norm_params, "embed_table": embed_table, "qkv_first": qkv_first, "qkv_second": qkv_second, "out_first": out_first, "out_second": out_second, "up_first": up_first, "up_second": up_second, "down_first": down_first, "down_second": down_second, "norm_first": norm_first, "norm_second": norm_second, "embed_first": embed_first, "embed_second": embed_second}


@jax.custom_vjp
def low(v):
    return lax.optimization_barrier(v.astype(jnp.bfloat16)).astype(jnp.float32)

@jax.custom_vjp
def low_back(v):
    return v

def low_keep(v):
    return (low(v), None)

def low_pass(kept, grad):
    return (grad,)

def back_keep(v):
    return (v, None)

def back_low(kept, grad):
    return (low(grad),)
low.defvjp(low_keep, low_pass)
low_back.defvjp(back_keep, back_low)
highest = lax.Precision.HIGHEST
eps_norm = 1e-05
beta_one = 0.5
beta_two = 0.5
adam_eps = 1e-08
decay_matrix = 0.01
vector_rate = 0.6
embed_rate = 1.0

def layer_norm(values, gain_vec, shift_vec):
    row_mean = lax.optimization_barrier(jnp.mean(values, axis=-1, keepdims=True))
    centered = values - row_mean
    variance = lax.optimization_barrier(jnp.mean(centered * centered, axis=-1, keepdims=True))
    return centered * lax.rsqrt(variance + eps_norm) * gain_vec + shift_vec

def gelu_exact(hidden):
    return jax.nn.gelu(hidden, approximate=False)

def time_features(step_values):
    half_width = D // 2
    frequency = jnp.exp(-math.log(10000.0) * jnp.arange(half_width, dtype=jnp.float32) / half_width)
    angles = step_values.astype(jnp.float32)[:, None] * frequency[None, :]
    return jnp.concatenate([jnp.sin(angles), jnp.cos(angles)], axis=1)

def adamw(weight, mean_old, square_old, gradient, step_rate, decay_weight):
    mean_new = beta_one * mean_old + (1.0 - beta_one) * gradient
    square_new = beta_two * square_old + (1.0 - beta_two) * gradient * gradient
    fix_one = 1.0 - beta_one ** STEP
    fix_two = 1.0 - beta_two ** STEP
    direction = mean_new / fix_one / (jnp.sqrt(square_new / fix_two) + adam_eps)
    return (weight - step_rate * (direction + decay_weight * weight), mean_new, square_new)

def one_head(head_inputs):
    query, keys, values = head_inputs
    scores = low_back(jnp.dot(query, keys.T, precision=highest) * HEAD_DIM ** (-0.5))
    probability = jax.nn.softmax(scores, axis=-1)
    return jnp.dot(low(probability), values, precision=highest)

def forward(qkv_weight, out_weight, up_weight, down_weight, norm_params, embed_table, time_rows, letters):
    residual = jnp.dot(letters, embed_table, precision=highest) + time_rows
    for layer_index in range(LAYERS):
        normed = low(layer_norm(residual, norm_params[layer_index, 0], norm_params[layer_index, 1]))
        projected = jnp.dot(normed, low(qkv_weight[layer_index]).reshape(D, 3 * D), precision=highest)
        projected = low_back(low(projected)).reshape(LEN, 3, HEADS, HEAD_DIM).transpose(1, 2, 0, 3)
        attended = lax.map(jax.checkpoint(one_head), (projected[0], projected[1], projected[2]))
        attended = low_back(low(attended.transpose(1, 0, 2).reshape(LEN, D)))
        residual = residual + low_back(jnp.dot(attended, low(out_weight[layer_index]), precision=highest))
        normed_two = low(layer_norm(residual, norm_params[layer_index, 2], norm_params[layer_index, 3]))
        hidden = low_back(jnp.dot(normed_two, low(up_weight[layer_index]), precision=highest))
        activated = low(gelu_exact(hidden))
        residual = residual + low_back(jnp.dot(activated, low(down_weight[layer_index]), precision=highest))
    return residual

def reference(token_ids, timesteps, importance, cotangent, qkv_weight, out_weight, up_weight, down_weight, norm_params, embed_table, qkv_first, qkv_second, out_first, out_second, up_first, up_second, down_first, down_second, norm_first, norm_second, embed_first, embed_second):
    seq_total = timesteps.shape[0]
    params = (qkv_weight, out_weight, up_weight, down_weight, norm_params, embed_table)
    time_table = time_features(timesteps)

    def per_sequence(running, sequence_item):
        id_row, time_row, cot_rows, seq_weight = sequence_item
        letters = (id_row[:, None] == jnp.arange(VOCAB, dtype=jnp.int32)[None, :]).astype(jnp.float32)
        time_rows = jnp.broadcast_to(time_row[None, :], (LEN, D))

        def apply_layers(weights_all, time_input):
            return forward(weights_all[0], weights_all[1], weights_all[2], weights_all[3], weights_all[4], weights_all[5], time_input, letters)
        result, pullback = jax.vjp(apply_layers, params, time_rows)
        param_grads, time_grad = pullback(cot_rows.astype(jnp.float32) * seq_weight)
        running = jax.tree.map(jnp.add, running, param_grads)
        return (running, (result, time_grad))
    zero_grads = jax.tree.map(jnp.zeros_like, params)
    grad_totals, (outputs, input_grads) = lax.scan(per_sequence, zero_grads, (token_ids.reshape(seq_total, LEN), time_table, cotangent.reshape(seq_total, LEN, D), importance))
    qkv_grad, out_grad, up_grad, down_grad, norm_grad, embed_grad = grad_totals
    qkv_master, qkv_mean, qkv_square = adamw(qkv_weight, qkv_first, qkv_second, qkv_grad, 2.0 / math.sqrt(D), decay_matrix)
    out_master, out_mean, out_square = adamw(out_weight, out_first, out_second, out_grad, 2.0 / math.sqrt(D), decay_matrix)
    up_master, up_mean, up_square = adamw(up_weight, up_first, up_second, up_grad, 2.0 / math.sqrt(D), decay_matrix)
    down_master, down_mean, down_square = adamw(down_weight, down_first, down_second, down_grad, 2.0 / math.sqrt(FF), decay_matrix)
    norm_master, norm_mean, norm_square = adamw(norm_params, norm_first, norm_second, norm_grad, vector_rate, 0.0)
    embed_master, embed_mean, embed_square = adamw(embed_table, embed_first, embed_second, embed_grad, embed_rate, 0.0)
    return (outputs.reshape(seq_total * LEN, D), input_grads.reshape(seq_total * LEN, D), qkv_master, qkv_mean, qkv_square, qkv_master.astype(jnp.bfloat16), out_master, out_mean, out_square, out_master.astype(jnp.bfloat16), up_master, up_mean, up_square, up_master.astype(jnp.bfloat16), down_master, down_mean, down_square, down_master.astype(jnp.bfloat16), norm_master, norm_mean, norm_square, embed_master, embed_mean, embed_square)
```

```python
import functools
import math

import jax
import jax.numpy as jnp
from jax import lax
from jax.experimental import pallas as pl
from jax.experimental.pallas import tpu as pltpu
from jax.sharding import PartitionSpec as P

HEAD_DIM = 64
FF = 2048
VOCAB = 27
LAYERS = 2
LEN = 1024
STEP = 10
D = 512
PAIR = 2 * HEAD_DIM
CH = 256
SLOT = LEN // CH

bf16 = jnp.bfloat16
f32 = jnp.float32
highest = lax.Precision.HIGHEST
eps_norm = 1e-05
beta_one = 0.5
beta_two = 0.5
adam_eps = 1e-08
decay_matrix = 0.01
vector_rate = 0.6
embed_rate = 1.0
LOG2E = math.log2(math.e)
LN2 = math.log(2.0)
ALL = ("dp", "mp")

NN = (((1,), (0,)), ((), ()))
NT = (((1,), (1,)), ((), ()))


def mm(left, right, dims=NN):
    return lax.dot_general(left, right, dims, preferred_element_type=f32)


def vmem():
    return pl.BlockSpec(memory_space=pltpu.VMEM)


def smem():
    return pl.BlockSpec(memory_space=pltpu.SMEM)


def hbm():
    return pl.BlockSpec(memory_space=pl.ANY)


def after_operands(kernel, prefetched, count):
    def call(*refs):
        return kernel(*refs[:prefetched], *refs[prefetched + count :])

    return call


def params(mib):
    return pltpu.CompilerParams(
        dimension_semantics=("arbitrary",), vmem_limit_bytes=mib * 1024 * 1024
    )


def norm_parts(values):
    row_mean = jnp.mean(values, axis=-1, keepdims=True)
    centered = values - row_mean
    variance = jnp.mean(centered * centered, axis=-1, keepdims=True)
    inverse = lax.rsqrt(variance + eps_norm)
    return centered * inverse, inverse


def layer_norm(values, gain_vec, shift_vec):
    scaled, _ = norm_parts(values)
    return scaled * gain_vec + shift_vec


def norm_backward(grad_out, values, gain_vec):
    scaled, inverse = norm_parts(values)
    weighted = grad_out * gain_vec
    mean_plain = jnp.mean(weighted, axis=-1, keepdims=True)
    mean_scaled = jnp.mean(weighted * scaled, axis=-1, keepdims=True)
    grad_in = (weighted - mean_plain - scaled * mean_scaled) * inverse
    gain_grad = jnp.sum(grad_out * scaled, axis=0, keepdims=True)
    shift_grad = jnp.sum(grad_out, axis=0, keepdims=True)
    return grad_in, gain_grad, shift_grad


def gelu_pair(hidden):
    square = hidden * hidden
    bell = jnp.exp2(square * (-0.5 * LOG2E))
    ratio = 1.0 / (1.0 + (0.3275911 / math.sqrt(2.0)) * jnp.abs(hidden))
    poly = ratio * (
        0.5 * 0.254829592
        + ratio
        * (
            0.5 * -0.284496736
            + ratio * (0.5 * 1.421413741 + ratio * (0.5 * -1.453152027 + ratio * (0.5 * 1.061405429)))
        )
    )
    tail = poly * bell
    phi = jnp.where(hidden < 0.0, tail, 1.0 - tail)
    return hidden * phi, phi + hidden * bell * (1.0 / math.sqrt(2.0 * math.pi))


def time_features(step_values):
    half_width = D // 2
    frequency = jnp.exp(-math.log(10000.0) * jnp.arange(half_width, dtype=f32) / half_width)
    angles = step_values.astype(f32)[:, None] * frequency[None, :]
    return jnp.concatenate([jnp.sin(angles), jnp.cos(angles)], axis=1)


def adamw(weight, mean_old, square_old, gradient, step_rate, decay_weight):
    mean_new = beta_one * mean_old + (1.0 - beta_one) * gradient
    square_new = beta_two * square_old + (1.0 - beta_two) * gradient * gradient
    fix_one = 1.0 - beta_one**STEP
    fix_two = 1.0 - beta_two**STEP
    direction = mean_new / fix_one / (jnp.sqrt(square_new / fix_two) + adam_eps)
    return (weight - step_rate * (direction + decay_weight * weight), mean_new, square_new)


def permute_all(values, target):
    count = lax.axis_size("dp") * lax.axis_size("mp")
    return lax.ppermute(values, ALL, [(i, target(i)) for i in range(count)])


def block_places(my_dp):
    index = jnp.arange(32, dtype=jnp.int32)
    apart = (index >> 2) ^ my_dp
    place = ((apart & 1) << 4) | ((apart >> 1) << 2) | (index & 3)
    owner = my_dp ^ ((((index >> 2) & 3) << 1) | (index >> 4))
    return place, owner


def tie(values, after):
    return lax.optimization_barrier((values, after))


def flip(values, bits):
    return permute_all(values, lambda i: i ^ bits)


def gather_z(values):
    return jnp.stack([values] + [flip(values, bits) for bits in (1, 2, 3)])


def scatter_core(blocks):
    half = blocks.shape[0] // 2
    arrived = flip(blocks[half:], 4)
    return (blocks[:half].astype(f32) + arrived.astype(f32)).astype(bf16)


def scatter_four(blocks, unit):
    size = blocks.shape[0] // 4
    found = [flip(blocks[i * size : (i + 1) * size], i * unit) for i in (1, 2, 3)]
    return blocks[:size], found


def add_four(own, found, last):
    one, two, three = [part.astype(f32) for part in found]
    total = (own.astype(f32) + one) + (two + three)
    return total[0] if last else total.astype(bf16)


def gather_dp(held):
    return lax.all_gather(held, "dp", axis=0, tiled=False)


def scatter_dp(blocks, dp):
    places, rows, columns = blocks.shape
    flat = blocks.reshape(places * rows, columns)
    return lax.psum_scatter(flat, "dp", scatter_dimension=0, tiled=True).reshape(
        places // dp, rows, columns
    )


def plain_gather(values):
    dp, mp = lax.axis_size("dp"), lax.axis_size("mp")
    rows, columns = values.shape
    found = lax.all_gather(values, ALL, axis=0, tiled=True).reshape(dp, mp, rows, columns)
    if rows % 16 == 0:
        return found
    return jnp.swapaxes(found, 0, 1).reshape(1, mp, dp * rows, columns)


def plain_scatter(blocks, dp):
    places, rows, columns = blocks.shape
    mp = lax.axis_size("mp")
    if places != dp * mp:
        blocks = jnp.swapaxes(blocks.reshape(mp, dp, D // dp, columns), 0, 1)
    flat = blocks.reshape(dp * mp * (D // dp), columns)
    return lax.psum_scatter(flat, ALL, scatter_dimension=0, tiled=True).astype(f32)


def shift_right(values):
    count = lax.axis_size("mp")
    return lax.ppermute(values, "mp", [(i, i + 1) for i in range(count - 1)])


def shift_left(values):
    count = lax.axis_size("mp")
    return lax.ppermute(values, "mp", [(i + 1, i) for i in range(count - 1)])


def sum_four(values, unit):
    one, two, three = [flip(values, i * unit) for i in (1, 2, 3)]
    return (values + one) + (two + three)


def fetch_blocks(table, near, far, targets, sems):
    copies = []
    for place in range(32):
        owner = table[place]
        source = near.at[place] if place < 16 else far.at[place - 16]
        for index, (target, begin, width) in enumerate(targets):
            copies.append(
                pltpu.make_async_copy(
                    source.at[:, pl.ds(begin, width)],
                    target.at[owner, place % 4],
                    sems.at[place, index],
                )
            )
    for copy in copies:
        copy.start()
    return copies


def attn_forward_kernel(gathered, groups, meta, table, *refs):
    if gathered:
        near, far, left, own, right, resid, norm = refs[:7]
        middle, normed, q_o, k_o, v_o, o_o, lse_o, w_o = refs[7:15]
        ext, total, sems = refs[15:]
    else:
        w_in, left, own, right, resid, norm = refs[:6]
        middle, normed, q_o, k_o, v_o, o_o, lse_o = refs[6:13]
        ext, total = refs[13:]
    step = pl.program_id(0)

    @pl.when(step == 0)
    def _():
        if gathered:
            copies = fetch_blocks(table, near, far, [(w_o, 0, D)], sems)
        for index, part in enumerate((left, own, right)):
            ext[pl.ds(3 * index, 3)] = part[...].reshape(3, CH, D)
        total[...] = jnp.zeros_like(total)
        if gathered:
            for copy in copies:
                copy.wait()

    def weight(begin, end):
        found = w_o[:, step, :, begin:end] if gathered else w_in[:, 0, :, begin:end]
        return found.reshape(D, end - begin)

    for j in range(3):
        q_o[0, j] = (mm(ext[3 + j], weight(0, PAIR)) * (LOG2E / math.sqrt(HEAD_DIM))).astype(bf16)

    def project(slot, carry):
        begin = meta[slot]
        kv_w = weight(PAIR, 3 * PAIR)
        for i in range(SLOT):
            both = mm(ext[begin + i], kv_w).astype(bf16)
            k_o[0, slot * SLOT + i] = both[:, :PAIR]
            v_o[0, slot * SLOT + i] = both[:, PAIR:]
        return carry

    lax.fori_loop(0, meta[2], project, 0)
    lane = lax.broadcasted_iota(jnp.int32, (CH, PAIR), 1)

    for j in range(3):
        slot = meta[3 + j]
        query = q_o[0, j]
        keys = k_o[0, pl.ds(slot * SLOT, SLOT)].reshape(LEN, PAIR)
        values = v_o[0, pl.ds(slot * SLOT, SLOT)].reshape(LEN, PAIR)
        parts = []
        for h in range(2):
            q_h = jnp.where((lane // HEAD_DIM) == h, query, jnp.zeros_like(query))
            scores = mm(q_h, keys, NT)
            top = jnp.max(scores, axis=1, keepdims=True)
            weights = jnp.exp2(scores - top)
            denominator = jnp.sum(weights, axis=1, keepdims=True)
            mixed = mm(weights.astype(bf16), values)
            parts.append(mixed * (1.0 / denominator))
            spread = jnp.broadcast_to(top + jnp.log2(denominator), (CH, PAIR))
            lse_o[0, j, h : h + 1] = spread.T[0:1]
        out = jnp.where((lane // HEAD_DIM) == 0, parts[0], parts[1]).astype(bf16)
        o_o[0, j] = out
        total[j] += mm(out, weight(3 * PAIR, D), NT)

    @pl.when(step == groups - 1)
    def _():
        for j in range(3):
            rows = pl.ds(j * CH, CH)
            values = resid[rows] + total[j]
            middle[rows] = values
            normed[rows] = layer_norm(values, norm[2:3], norm[3:4]).astype(bf16)


def attn_forward(weights, meta, table, left, own, right, resid, norm, groups):
    rows = own.shape[0]
    gathered = isinstance(weights, tuple)
    const = lambda s, *_: (0, 0)
    pair = lambda s, *_: (s, 0, 0, 0)
    full = pl.BlockSpec((rows, D), const)
    out_shape = [
        jax.ShapeDtypeStruct((rows, D), f32),
        jax.ShapeDtypeStruct((rows, D), bf16),
        jax.ShapeDtypeStruct((groups, 3, CH, PAIR), bf16),
        jax.ShapeDtypeStruct((groups, 2 * SLOT, CH, PAIR), bf16),
        jax.ShapeDtypeStruct((groups, 2 * SLOT, CH, PAIR), bf16),
        jax.ShapeDtypeStruct((groups, 3, CH, PAIR), bf16),
        jax.ShapeDtypeStruct((groups, 3, 8, CH), f32),
    ]
    out_specs = [
        full,
        full,
        pl.BlockSpec((1, 3, CH, PAIR), pair),
        pl.BlockSpec((1, 2 * SLOT, CH, PAIR), pair),
        pl.BlockSpec((1, 2 * SLOT, CH, PAIR), pair),
        pl.BlockSpec((1, 3, CH, PAIR), pair),
        pl.BlockSpec((1, 3, 8, CH), pair),
    ]
    scratch = [
        pltpu.VMEM((9, CH, D), bf16),
        pltpu.VMEM((3, CH, D), f32),
    ]
    if gathered:
        w_args = list(weights)
        w_specs = [hbm(), hbm()]
        out_shape.append(jax.ShapeDtypeStruct((8, 4, 64, D), bf16))
        out_specs.append(pl.BlockSpec((8, 4, 64, D), pair_zero))
        scratch.append(pltpu.SemaphoreType.DMA((32, 1)))
    else:
        w_args = [weights]
        split, _, high, _ = weights.shape
        w_specs = [pl.BlockSpec((split, 1, high, D), lambda s, *_: (0, s, 0, 0))]
    outs = pl.pallas_call(
        functools.partial(attn_forward_kernel, gathered, groups),
        grid_spec=pltpu.PrefetchScalarGridSpec(
            num_scalar_prefetch=2,
            grid=(groups,),
            in_specs=w_specs
            + [full, full, full, full, pl.BlockSpec((4, D), const)],
            out_specs=out_specs,
            scratch_shapes=scratch,
        ),
        out_shape=out_shape,
        compiler_params=params(56),
        cost_estimate=pl.CostEstimate(
            flops=29_000_000_000, bytes_accessed=14_000_000, transcendentals=0
        ),
        name="attn_forward",
    )(meta, table, *w_args, left, own, right, resid, norm)
    if gathered:
        return outs[:7], outs[7]
    return outs, weights


def pair_zero(s, *_):
    return (0, 0, 0, 0)


def mlp_forward_kernel(gathered, last, groups, table, *refs):
    if gathered:
        near, far, normed, middle, norm = refs[:5]
        refs = refs[5:]
    else:
        up_in, down_in, normed, middle, norm = refs[:5]
        refs = refs[5:]
    after, act_o, slope_o = refs[:3]
    refs = refs[3:]
    if not last:
        next_o = refs[0]
        refs = refs[1:]
    if gathered:
        up_o, down_o, total, sems = refs
    else:
        (total,) = refs
    step = pl.program_id(0)

    @pl.when(step == 0)
    def _():
        if gathered:
            copies = fetch_blocks(table, near, far, [(up_o, 0, D), (down_o, D, D)], sems)
        total[...] = jnp.zeros_like(total)
        if gathered:
            for copy in copies:
                copy.wait()

    if gathered:
        up_w = up_o[:, step].reshape(D, D)
        down_w = down_o[:, step].reshape(D, D)
    else:
        up_w = up_in[:, 0].reshape(D, D)
        down_w = down_in[:, 0].reshape(D, D)
    for j in range(3):
        rows = pl.ds(j * CH, CH)
        hidden = mm(normed[rows], up_w)
        act, slope = gelu_pair(hidden)
        act = act.astype(bf16)
        act_o[0, rows] = act
        slope_o[0, rows] = slope.astype(bf16)
        total[j] += mm(act, down_w, NT)

    @pl.when(step == groups - 1)
    def _():
        for j in range(3):
            rows = pl.ds(j * CH, CH)
            values = middle[rows] + total[j]
            after[rows] = values
            if not last:
                next_o[rows] = layer_norm(values, norm[0:1], norm[1:2]).astype(bf16)


def mlp_forward(weights, table, normed, middle, norm, groups, last):
    rows = normed.shape[0]
    gathered = not isinstance(weights[0], tuple)
    const = lambda s, *_: (0, 0)
    full = pl.BlockSpec((rows, D), const)
    part = pl.BlockSpec((1, rows, D), lambda s, *_: (s, 0, 0))
    out_shape = [
        jax.ShapeDtypeStruct((rows, D), f32),
        jax.ShapeDtypeStruct((groups, rows, D), bf16),
        jax.ShapeDtypeStruct((groups, rows, D), bf16),
    ]
    out_specs = [full, part, part]
    if not last:
        out_shape.append(jax.ShapeDtypeStruct((rows, D), bf16))
        out_specs.append(full)
    scratch = [pltpu.VMEM((3, CH, D), f32)]
    if gathered:
        w_args = list(weights)
        w_specs = [hbm(), hbm()]
        for _ in range(2):
            out_shape.append(jax.ShapeDtypeStruct((8, 4, 64, D), bf16))
            out_specs.append(pl.BlockSpec((8, 4, 64, D), pair_zero))
        scratch.append(pltpu.SemaphoreType.DMA((32, 2)))
    else:
        (up_w, up_at), (down_w, down_at) = weights
        w_args = [up_w, down_w]
        w_specs = [weight_spec(up_w, up_at), weight_spec(down_w, down_at)]
    outs = pl.pallas_call(
        functools.partial(mlp_forward_kernel, gathered, last, groups),
        grid_spec=pltpu.PrefetchScalarGridSpec(
            num_scalar_prefetch=1,
            grid=(groups,),
            in_specs=w_specs + [full, full, pl.BlockSpec((4, D), const)],
            out_specs=out_specs,
            scratch_shapes=scratch,
        ),
        out_shape=out_shape,
        compiler_params=params(56),
        cost_estimate=pl.CostEstimate(
            flops=15_000_000_000, bytes_accessed=18_000_000, transcendentals=0
        ),
        name="mlp_forward",
    )(table, *w_args, normed, middle, norm)
    if gathered:
        return outs[:-2], ((outs[-2], 0), (outs[-1], 0))
    return outs, weights


def weight_spec(weight, at):
    split, _, high, _ = weight.shape
    return pl.BlockSpec((split, 1, high, D), lambda s, *_: (0, s, 0, at))


def put_blocks(out, table, step, groups, split, begin, values):
    high = D // split
    width = values.shape[1]
    for d in range(split):
        place = table[d * groups + step]
        out[place, :, begin : begin + width] = values[d * high : (d + 1) * high]


def mlp_backward_kernel(first, groups, split, meta, place, *refs):
    if first:
        scale, cot = refs[:2]
        refs = refs[2:]
    else:
        grad_in, d_own, d_left, d_right, source, norm_up = refs[:6]
        refs = refs[6:]
    up_in, down_in, act, slope, normed, middle, norm = refs[:7]
    refs = refs[7:]
    w_grad, grad_out, n_grad = refs[:3]
    refs = refs[3:]
    grad, low, low_t, norm_t, total = refs
    step = pl.program_id(0)

    @pl.when(step == 0)
    def _():
        n_grad[...] = jnp.zeros_like(n_grad)
        for j in range(3):
            rows = pl.ds(j * CH, CH)
            if first:
                values = cot[rows].astype(f32) * scale[meta[6 + j]]
            else:
                arrived = d_own[rows] + d_left[rows].astype(f32) + d_right[rows].astype(f32)
                back, gain_grad, shift_grad = norm_backward(arrived, source[rows], norm_up[0:1])
                values = grad_in[rows] + back
                n_grad[0:1] += gain_grad
                n_grad[1:2] += shift_grad
            grad[j] = values
            rounded = values.astype(bf16)
            low[rows] = rounded
            low_t[:, j * CH : (j + 1) * CH] = rounded.T
            norm_t[:, j * CH : (j + 1) * CH] = normed[rows].T
        total[...] = jnp.zeros_like(total)

    up_w = up_in[:, 0].reshape(D, D)
    down_w = down_in[:, 0].reshape(D, D)
    down_grad = mm(low_t[...], act[0]).astype(bf16)
    put_blocks(w_grad, place, step, groups, split, D, down_grad)
    pieces = []
    for j in range(3):
        rows = pl.ds(j * CH, CH)
        piece = (mm(low[rows], down_w) * slope[0, rows].astype(f32)).astype(bf16)
        pieces.append(piece)
        total[j] += mm(piece, up_w, NT)
    up_grad = mm(norm_t[...], jnp.concatenate(pieces, axis=0)).astype(bf16)
    put_blocks(w_grad, place, step, groups, split, 0, up_grad)

    @pl.when(step == groups - 1)
    def _():
        for j in range(3):
            rows = pl.ds(j * CH, CH)
            back, gain_grad, shift_grad = norm_backward(total[j], middle[rows], norm[2:3])
            grad_out[rows] = grad[j] + back
            n_grad[2:3] += gain_grad
            n_grad[3:4] += shift_grad


def mlp_backward(
    weights, meta, place, begin, act, slope, normed, middle, norm, groups, split, after=()
):
    rows = normed.shape[0]
    first = len(begin) == 2
    const = lambda s, *_: (0, 0)
    full = pl.BlockSpec((rows, D), const)
    part = pl.BlockSpec((1, rows, D), lambda s, *_: (s, 0, 0))
    vec = pl.BlockSpec((4, D), const)
    (up_w, up_at), (down_w, down_at) = weights
    begin_specs = [smem(), full] if first else [full] * 5 + [vec]
    places = split * groups
    return pl.pallas_call(
        after_operands(
            functools.partial(mlp_backward_kernel, first, groups, split), 2, len(after)
        ),
        grid_spec=pltpu.PrefetchScalarGridSpec(
            num_scalar_prefetch=2,
            grid=(groups,),
            in_specs=[hbm()] * len(after)
            + begin_specs
            + [weight_spec(up_w, up_at), weight_spec(down_w, down_at)]
            + [part, part, full, full, vec],
            out_specs=[
                pl.BlockSpec((places, D // split, 2 * D), lambda s, *_: (0, 0, 0)),
                full,
                pl.BlockSpec((8, D), const),
            ],
            scratch_shapes=[
                pltpu.VMEM((3, CH, D), f32),
                pltpu.VMEM((rows, D), bf16),
                pltpu.VMEM((D, rows), bf16),
                pltpu.VMEM((D, rows), bf16),
                pltpu.VMEM((3, CH, D), f32),
            ],
        ),
        out_shape=[
            jax.ShapeDtypeStruct((places, D // split, 2 * D), bf16),
            jax.ShapeDtypeStruct((rows, D), f32),
            jax.ShapeDtypeStruct((8, D), f32),
        ],
        compiler_params=params(56),
        cost_estimate=pl.CostEstimate(
            flops=20_000_000_000, bytes_accessed=20_000_000, transcendentals=0
        ),
        name="mlp_backward",
    )(meta, place, *after, *begin, up_w, down_w, act, slope, normed, middle, norm)


def attn_backward_kernel(groups, split, meta, place, *refs):
    w_in, left, own, right, grad_in, small, q_i, k_i, v_i, o_i, lse_i = refs[:11]
    w_grad, d_left, d_own, d_right, small_o = refs[11:16]
    ext, ext_t, low, low_t, k_t, dk, dv, d_ext, dq_all = refs[16:]
    step = pl.program_id(0)

    @pl.when(step == 0)
    def _():
        for index, part in enumerate((left, own, right)):
            for j in range(3):
                values = part[pl.ds(j * CH, CH)]
                ext[3 * index + j] = values
                ext_t[3 * index + j] = values.T
        for j in range(3):
            rounded = grad_in[pl.ds(j * CH, CH)].astype(bf16)
            low[j] = rounded
            low_t[:, j * CH : (j + 1) * CH] = rounded.T
        d_ext[...] = jnp.zeros_like(d_ext)
        small_o[...] = small[...]

    def weight(begin, end):
        return w_in[:, 0, :, begin:end].reshape(D, end - begin)

    slots = meta[2]

    def prepare(slot, carry):
        for i in range(SLOT):
            k_t[slot, :, i * CH : (i + 1) * CH] = k_i[0, slot * SLOT + i].T
        dk[slot] = jnp.zeros((LEN, PAIR), f32)
        dv[slot] = jnp.zeros((LEN, PAIR), f32)
        return carry

    lax.fori_loop(0, slots, prepare, 0)
    lane = lax.broadcasted_iota(jnp.int32, (CH, PAIR), 1)

    def chunk(j, carry):
        slot = meta[3 + j]
        query = q_i[0, j]
        out = o_i[0, j]
        keys = k_i[0, pl.ds(slot * SLOT, SLOT)].reshape(LEN, PAIR)
        values = v_i[0, pl.ds(slot * SLOT, SLOT)].reshape(LEN, PAIR)
        grad_out = mm(low[j], weight(3 * PAIR, D))
        grad_low = grad_out.astype(bf16)
        product = (grad_low.astype(f32) * out.astype(f32)).T
        delta = jnp.sum(product.reshape(2, HEAD_DIM, CH), axis=1)
        p_all = []
        ds_all = []
        q_all = []
        g_all = []
        dq_t = []
        for h in range(2):
            q_h = jnp.where((lane // HEAD_DIM) == h, query, jnp.zeros_like(query))
            g_h = jnp.where((lane // HEAD_DIM) == h, grad_low, jnp.zeros_like(grad_low))
            probability = jnp.exp2(mm(keys, q_h, NT) - lse_i[0, j, h : h + 1])
            grad_p = mm(values, g_h, NT)
            grad_s = (probability * (grad_p - delta[h : h + 1])).astype(bf16)
            dq_t.append(mm(k_t[slot, h * HEAD_DIM : (h + 1) * HEAD_DIM, :], grad_s))
            dv[slot] += mm(probability.astype(bf16), g_h)
            dk[slot] += mm(grad_s, q_h)
        dq = jnp.concatenate(dq_t, axis=0).T * (1.0 / math.sqrt(HEAD_DIM))
        dq_low = dq.astype(bf16)
        dq_all[pl.ds(j * CH, CH)] = dq_low
        d_ext[3 + j] += mm(dq_low, weight(0, PAIR), NT)
        return carry

    lax.fori_loop(0, 3, chunk, 0)
    out_grad = mm(low_t[...], o_i[0].reshape(3 * CH, PAIR)).astype(bf16)
    put_blocks(w_grad, place, step, groups, split, 3 * PAIR, out_grad)
    own_t = jnp.concatenate([ext_t[3], ext_t[4], ext_t[5]], axis=1)
    q_grad = mm(own_t, dq_all[...]).astype(bf16)
    put_blocks(w_grad, place, step, groups, split, 0, q_grad)

    def collect(slot, running):
        begin = meta[slot]
        kv_w = weight(PAIR, 3 * PAIR)
        for i in range(SLOT):
            rows = pl.ds(i * CH, CH)
            both = jnp.concatenate(
                [(dk[slot, rows] * LN2).astype(bf16), dv[slot, rows].astype(bf16)], axis=1
            )
            d_ext[begin + i] += mm(both, kv_w, NT)
            running = running + mm(ext_t[begin + i], both)
        return running

    kv_grad = lax.fori_loop(0, slots, collect, jnp.zeros((D, 2 * PAIR), f32))
    put_blocks(w_grad, place, step, groups, split, PAIR, kv_grad.astype(bf16))

    @pl.when(step == groups - 1)
    def _():
        for j in range(3):
            rows = pl.ds(j * CH, CH)
            d_left[rows] = d_ext[j].astype(bf16)
            d_own[rows] = d_ext[3 + j]
            d_right[rows] = d_ext[6 + j].astype(bf16)


def attn_backward(
    weight, meta, place, left, own, right, grad_in, kept, groups, split, small, after=()
):
    rows = own.shape[0]
    q_i, k_i, v_i, o_i, lse_i = kept
    const = lambda s, *_: (0, 0)
    pair = lambda s, *_: (s, 0, 0, 0)
    full = pl.BlockSpec((rows, D), const)
    places = split * groups
    return pl.pallas_call(
        after_operands(
            functools.partial(attn_backward_kernel, groups, split), 2, len(after)
        ),
        grid_spec=pltpu.PrefetchScalarGridSpec(
            num_scalar_prefetch=2,
            grid=(groups,),
            in_specs=[hbm()] * len(after)
            + [
                weight_spec(*weight),
                full,
                full,
                full,
                full,
                pl.BlockSpec((8, D), const),
                pl.BlockSpec((1, 3, CH, PAIR), pair),
                pl.BlockSpec((1, 2 * SLOT, CH, PAIR), pair),
                pl.BlockSpec((1, 2 * SLOT, CH, PAIR), pair),
                pl.BlockSpec((1, 3, CH, PAIR), pair),
                pl.BlockSpec((1, 3, 8, CH), pair),
            ],
            out_specs=[
                pl.BlockSpec((places, D // split, D), lambda s, *_: (0, 0, 0)),
                full,
                full,
                full,
                pl.BlockSpec((8, D), const),
            ],
            scratch_shapes=[
                pltpu.VMEM((9, CH, D), bf16),
                pltpu.VMEM((9, D, CH), bf16),
                pltpu.VMEM((3, CH, D), bf16),
                pltpu.VMEM((D, rows), bf16),
                pltpu.VMEM((2, PAIR, LEN), bf16),
                pltpu.VMEM((2, LEN, PAIR), f32),
                pltpu.VMEM((2, LEN, PAIR), f32),
                pltpu.VMEM((9, CH, D), f32),
                pltpu.VMEM((rows, PAIR), bf16),
            ],
        ),
        out_shape=[
            jax.ShapeDtypeStruct((places, D // split, D), bf16),
            jax.ShapeDtypeStruct((rows, D), bf16),
            jax.ShapeDtypeStruct((rows, D), f32),
            jax.ShapeDtypeStruct((rows, D), bf16),
            jax.ShapeDtypeStruct((8, D), f32),
        ],
        compiler_params=params(58),
        cost_estimate=pl.CostEstimate(
            flops=45_000_000_000, bytes_accessed=24_000_000, transcendentals=0
        ),
        name="attn_backward",
    )(meta, place, *after, weight[0], left, own, right, grad_in, small, q_i, k_i, v_i, o_i, lse_i)


def entry_backward_kernel(grad_in, d_own, d_left, d_right, source, norm, ids, grad_out, small):
    small[...] = jnp.zeros_like(small)
    for j in range(3):
        rows = pl.ds(j * CH, CH)
        arrived = d_own[rows] + d_left[rows].astype(f32) + d_right[rows].astype(f32)
        back, gain_grad, shift_grad = norm_backward(arrived, source[rows], norm[0:1])
        values = grad_in[rows] + back
        grad_out[rows] = values
        small[0:1] += gain_grad
        small[1:2] += shift_grad
        letter = lax.broadcasted_iota(jnp.int32, (32, CH), 0)
        chosen = (letter == ids[:, j * CH : (j + 1) * CH]).astype(bf16)
        high = values.astype(bf16)
        rest = values - high.astype(f32)
        middle = rest.astype(bf16)
        low = (rest - middle.astype(f32)).astype(bf16)
        small[8:40] += mm(chosen, high) + mm(chosen, middle) + mm(chosen, low)


def entry_backward(grad_in, d_own, d_left, d_right, source, norm, ids, after=()):
    rows = grad_in.shape[0]
    return pl.pallas_call(
        after_operands(entry_backward_kernel, 0, len(after)),
        in_specs=[hbm()] * len(after) + [vmem()] * 7,
        out_specs=[vmem()] * 2,
        out_shape=[
            jax.ShapeDtypeStruct((rows, D), f32),
            jax.ShapeDtypeStruct((40, D), f32),
        ],
        compiler_params=pltpu.CompilerParams(vmem_limit_bytes=40 * 1024 * 1024),
        cost_estimate=pl.CostEstimate(
            flops=100_000_000, bytes_accessed=9_000_000, transcendentals=0
        ),
        name="entry_backward",
    )(*after, grad_in, d_own, d_left, d_right, source, norm, ids)


def shards(
    token_ids,
    timesteps,
    importance,
    cotangent,
    qkv_weight,
    out_weight,
    up_weight,
    down_weight,
    norm_params,
    embed_table,
    qkv_first,
    qkv_second,
    out_first,
    out_second,
    up_first,
    up_second,
    down_first,
    down_second,
    norm_first,
    norm_second,
    embed_first,
    embed_second,
):
    dp, mp = lax.axis_size("dp"), lax.axis_size("mp")
    small = dp == 8 and mp == 4
    groups = mp
    split = dp if small else 1
    row_count = token_ids.shape[0]
    seq_here = timesteps.shape[0]
    high = D // dp
    my_mp = lax.axis_index("mp")
    my_dp = lax.axis_index("dp")
    row_start = my_mp * row_count

    first_seq = row_start // LEN
    last_seq = (row_start + row_count - 1) // LEN
    chunk_seq = [(row_start + CH * j) // LEN for j in range(3)]
    meta = jnp.stack(
        [
            3 + (first_seq * LEN - row_start) // CH,
            3 + (last_seq * LEN - row_start) // CH,
            last_seq - first_seq + 1,
        ]
        + [seq - first_seq for seq in chunk_seq]
        + chunk_seq
    ).astype(jnp.int32)
    in_order = jnp.arange(split * groups, dtype=jnp.int32)
    if small:
        place, owner = block_places(my_dp)
    else:
        place = owner = in_order

    attn_mine = []
    mlp_mine = []
    for layer in range(LAYERS):
        attn_mine.append(
            jnp.concatenate(
                [qkv_weight[layer].reshape(high, -1), out_weight[layer].T], axis=1
            ).astype(bf16)
        )
        mlp_mine.append(
            jnp.concatenate([up_weight[layer], down_weight[layer].T], axis=1).astype(bf16)
        )
    both_mine = jnp.concatenate([attn_mine[1], mlp_mine[1]], axis=1)
    ids_left, ids_right = shift_right(token_ids), shift_left(token_ids)
    if small:
        attn_sent = [flip(attn_mine[0], bits) for bits in (1, 2, 3)]
        attn_sent, (ids_left, ids_right) = tie(attn_sent, (ids_left, ids_right))
        attn_z = jnp.stack([attn_mine[0]] + list(attn_sent))
    ids_ext = jnp.concatenate([ids_left, token_ids, ids_right])
    seq_ext = (row_start - row_count + jnp.arange(3 * row_count, dtype=jnp.int32)) // LEN
    letters = (ids_ext[:, None] == jnp.arange(VOCAB, dtype=jnp.int32)[None, :]).astype(f32)
    member = (seq_ext[:, None] == jnp.arange(seq_here, dtype=jnp.int32)[None, :]).astype(f32)
    entry_ext = jnp.dot(letters, embed_table, precision=highest) + jnp.dot(
        member, time_features(timesteps), precision=highest
    )
    normed_ext = layer_norm(entry_ext, norm_params[0, 0], norm_params[0, 1]).astype(bf16)
    resid = entry_ext[row_count : 2 * row_count]
    ext = (
        normed_ext[:row_count],
        normed_ext[row_count : 2 * row_count],
        normed_ext[2 * row_count :],
    )

    if small:
        mlp_first, attn_z = tie(mlp_mine[0], attn_z)
        attn_sent = [flip(attn_z, bits) for bits in (8, 16, 24)]
        attn_sent, (ext, resid) = tie(attn_sent, (ext, resid))
        attn_xy = jnp.concatenate([attn_z] + list(attn_sent), axis=0)
        mlp_z = gather_z(mlp_first)
        mlp_z, attn_xy = tie(mlp_z, attn_xy)
        attn_w = [(attn_xy, flip(attn_xy, 4))]
        mlp_found = gather_dp(mlp_z)
        both_mine, mlp_z = tie(both_mine, mlp_z)
        both_sent = [flip(both_mine, bits) for bits in (1, 2, 3)]
    else:
        attn_w = [plain_gather(attn_mine[0])]
        mlp_found = plain_gather(mlp_mine[0])
        attn_w.append(plain_gather(both_mine))
        mlp_w = [((mlp_found, 0), (mlp_found, 1)), ((attn_w[1], 1), (attn_w[1], 2))]

    kept = []
    for layer in range(LAYERS):
        last = layer == LAYERS - 1
        outs, w_attn = attn_forward(
            attn_w[layer], meta, owner, *ext, resid, norm_params[layer], groups
        )
        middle, normed = outs[:2]
        if small and layer == 0:
            both_sent, normed = tie(both_sent, normed)
            both_found = gather_dp(jnp.stack([both_mine] + list(both_sent)))
            attn_w.append(both_found)
            mlp_w = [((mlp_found, 0), (mlp_found, 1)), ((both_found, 1), (both_found, 2))]
        next_norm = norm_params[min(layer + 1, LAYERS - 1)]
        mlp_outs, w_mlp = mlp_forward(
            mlp_w[layer], owner, normed, middle, next_norm, groups, last
        )
        kept.append((ext, resid, middle, normed, outs[2:], mlp_outs[1:3], (w_attn, 0), w_mlp))
        resid = mlp_outs[0]
        if not last:
            following = mlp_outs[3]
            ext = (shift_right(following), following, shift_left(following))
    activations = resid

    norm_grads = [[None] * 4 for _ in range(LAYERS)]
    attn_grads = [None] * LAYERS
    mlp_grads = [None] * LAYERS
    begin = (importance, cotangent)
    after = ()
    for layer in reversed(range(LAYERS)):
        ext, source, middle, normed, attn_kept, (act, slope), w_attn, w_mlp = kept[layer]
        mlp_grad, grad_mid, n_grad = mlp_backward(
            w_mlp,
            meta,
            in_order,
            begin,
            act,
            slope,
            normed,
            middle,
            norm_params[layer],
            groups,
            split,
            after,
        )
        after = ()
        if small:
            if layer + 1 < LAYERS:
                attn_found, (mlp_grad, grad_mid) = tie(attn_found, (mlp_grad, grad_mid))
            mlp_rows = scatter_dp(mlp_grad, dp)
            if layer + 1 < LAYERS:
                attn_rows = add_four(attn_mine_rows, attn_found, False)
                above = jnp.concatenate([attn_rows, above], axis=2)
                above_mine, above_found = scatter_four(above, 1)
                after = (above,)
        attn_grad, d_left, d_own, d_right, n_grad = attn_backward(
            w_attn, meta, place, *ext, grad_mid, attn_kept, groups, split, n_grad, after
        )
        if small and layer + 1 < LAYERS:
            above_found, (attn_grad, d_left, d_right) = tie(
                above_found, (attn_grad, d_left, d_right)
            )
        from_right = shift_left(d_left)
        from_left = shift_right(d_right)
        if small:
            attn_held = scatter_core(attn_grad)
            attn_mine_rows, attn_found = scatter_four(attn_held, 8)
            if layer + 1 < LAYERS:
                above_total = add_four(above_mine, above_found, True)
                attn_grads[1] = above_total[:, :D]
                mlp_grads[1] = above_total[:, D:]
            else:
                above = mlp_rows
            after = (attn_held,)
        else:
            mlp_grads[layer] = plain_scatter(mlp_grad, dp)
            attn_grads[layer] = plain_scatter(attn_grad, dp)
        norm_grads[layer][2:] = [n_grad[2], n_grad[3]]
        if layer + 1 < LAYERS:
            norm_grads[layer + 1][:2] = [n_grad[0], n_grad[1]]
        begin = (grad_mid, d_own, from_left, from_right, source, norm_params[layer])
    after = ()
    if small:
        attn_rows = add_four(attn_mine_rows, attn_found, False)
        below = jnp.concatenate([attn_rows, mlp_rows], axis=2)
        after = (below,)
        below_mine, below_found = scatter_four(below, 1)
    input_grad, reduced = entry_backward(*begin, token_ids[None, :], after)
    norm_grads[0][:2] = [reduced[0], reduced[1]]
    stacked = jnp.concatenate(
        [jnp.stack([row for rows in norm_grads for row in rows]), reduced[8:40]], axis=0
    )
    if small:
        stacked = sum_four(stacked + flip(stacked, 4), 8)
        below_found, stacked = tie(below_found, stacked)
        stacked = sum_four(stacked, 1)
        total = add_four(below_mine, below_found, True)
        attn_grads[0] = total[:, :D]
        mlp_grads[0] = total[:, D:]
    else:
        stacked = lax.psum(stacked, ALL)
    norm_grad = stacked[: 4 * LAYERS].reshape(LAYERS, 4, D)
    embed_grad = stacked[4 * LAYERS : 4 * LAYERS + VOCAB]

    qkv_grad = jnp.stack([g[:, : 3 * PAIR].reshape(high, 3, PAIR) for g in attn_grads])
    out_grad = jnp.stack([g[:, 3 * PAIR :].T for g in attn_grads])
    up_grad = jnp.stack([g[:, :D] for g in mlp_grads])
    down_grad = jnp.stack([g[:, D:].T for g in mlp_grads])
    qkv_master, qkv_mean, qkv_square = adamw(
        qkv_weight, qkv_first, qkv_second, qkv_grad, 2.0 / math.sqrt(D), decay_matrix
    )
    out_master, out_mean, out_square = adamw(
        out_weight, out_first, out_second, out_grad, 2.0 / math.sqrt(D), decay_matrix
    )
    up_master, up_mean, up_square = adamw(
        up_weight, up_first, up_second, up_grad, 2.0 / math.sqrt(D), decay_matrix
    )
    down_master, down_mean, down_square = adamw(
        down_weight, down_first, down_second, down_grad, 2.0 / math.sqrt(FF), decay_matrix
    )
    norm_master, norm_mean, norm_square = adamw(
        norm_params, norm_first, norm_second, norm_grad, vector_rate, 0.0
    )
    embed_master, embed_mean, embed_square = adamw(
        embed_table, embed_first, embed_second, embed_grad, embed_rate, 0.0
    )
    return (
        activations,
        input_grad,
        qkv_master,
        qkv_mean,
        qkv_square,
        qkv_master.astype(bf16),
        out_master,
        out_mean,
        out_square,
        out_master.astype(bf16),
        up_master,
        up_mean,
        up_square,
        up_master.astype(bf16),
        down_master,
        down_mean,
        down_square,
        down_master.astype(bf16),
        norm_master,
        norm_mean,
        norm_square,
        embed_master,
        embed_mean,
        embed_square,
    )


def solution(mesh):
    rows = P(("dp", "mp"), None)
    qkv = P(None, "dp", None, "mp")
    wide = P(None, "mp", "dp")
    tall = P(None, "dp", "mp")
    same = P()
    return jax.shard_map(
        shards,
        mesh=mesh,
        in_specs=(P(("dp", "mp")), P("dp"), P("dp"), rows, qkv, wide, tall, wide, same, same)
        + (qkv, qkv, wide, wide, tall, tall, wide, wide, same, same, same, same),
        out_specs=(rows, rows)
        + (qkv,) * 4
        + (wide,) * 4
        + (tall,) * 4
        + (wide,) * 4
        + (same,) * 6,
        check_vma=False,
    )
```

```python
import functools
import math

import jax
import jax.numpy as jnp
from jax import lax
from jax.experimental import pallas as pl
from jax.experimental.pallas import tpu as pltpu
from jax.sharding import PartitionSpec as P

HEAD_DIM = 64
FF = 2048
VOCAB = 27
LAYERS = 2
LEN = 1024
STEP = 10
D = 512
PAIR = 2 * HEAD_DIM
CH = 256
SLOT = LEN // CH

bf16 = jnp.bfloat16
f32 = jnp.float32
highest = lax.Precision.HIGHEST
eps_norm = 1e-05
beta_one = 0.5
beta_two = 0.5
adam_eps = 1e-08
decay_matrix = 0.01
vector_rate = 0.6
embed_rate = 1.0
LOG2E = math.log2(math.e)
LN2 = math.log(2.0)
ALL = ("dp", "mp")

NN = (((1,), (0,)), ((), ()))
NT = (((1,), (1,)), ((), ()))


def mm(left, right, dims=NN):
    return lax.dot_general(left, right, dims, preferred_element_type=f32)


def vmem():
    return pl.BlockSpec(memory_space=pltpu.VMEM)


def smem():
    return pl.BlockSpec(memory_space=pltpu.SMEM)


def hbm():
    return pl.BlockSpec(memory_space=pl.ANY)


def after_operands(kernel, prefetched, count):
    def call(*refs):
        return kernel(*refs[:prefetched], *refs[prefetched + count :])

    return call


def kept_out(shape, dtype):
    return pltpu.HBM(shape, dtype)


def from_hbm(*arrays):
    return tuple(pltpu.with_memory_space_constraint(x, pltpu.HBM) for x in arrays)


def params(mib):
    return pltpu.CompilerParams(
        dimension_semantics=("arbitrary",), vmem_limit_bytes=mib * 1024 * 1024
    )


def norm_parts(values):
    row_mean = jnp.mean(values, axis=-1, keepdims=True)
    centered = values - row_mean
    variance = jnp.mean(centered * centered, axis=-1, keepdims=True)
    inverse = lax.rsqrt(variance + eps_norm)
    return centered * inverse, inverse


def layer_norm(values, gain_vec, shift_vec):
    scaled, _ = norm_parts(values)
    return scaled * gain_vec + shift_vec


def norm_backward(grad_out, values, gain_vec):
    scaled, inverse = norm_parts(values)
    weighted = grad_out * gain_vec
    mean_plain = jnp.mean(weighted, axis=-1, keepdims=True)
    mean_scaled = jnp.mean(weighted * scaled, axis=-1, keepdims=True)
    grad_in = (weighted - mean_plain - scaled * mean_scaled) * inverse
    gain_grad = jnp.sum(grad_out * scaled, axis=0, keepdims=True)
    shift_grad = jnp.sum(grad_out, axis=0, keepdims=True)
    return grad_in, gain_grad, shift_grad


def gelu_pair(hidden):
    square = hidden * hidden
    bell = jnp.exp2(square * (-0.5 * LOG2E))
    ratio = 1.0 / (1.0 + (0.3275911 / math.sqrt(2.0)) * jnp.abs(hidden))
    poly = ratio * (
        0.5 * 0.254829592
        + ratio
        * (
            0.5 * -0.284496736
            + ratio * (0.5 * 1.421413741 + ratio * (0.5 * -1.453152027 + ratio * (0.5 * 1.061405429)))
        )
    )
    tail = poly * bell
    phi = jnp.where(hidden < 0.0, tail, 1.0 - tail)
    return hidden * phi, phi + hidden * bell * (1.0 / math.sqrt(2.0 * math.pi))


def time_features(step_values):
    half_width = D // 2
    frequency = jnp.exp(-math.log(10000.0) * jnp.arange(half_width, dtype=f32) / half_width)
    angles = step_values.astype(f32)[:, None] * frequency[None, :]
    return jnp.concatenate([jnp.sin(angles), jnp.cos(angles)], axis=1)


def adamw(weight, mean_old, square_old, gradient, step_rate, decay_weight):
    mean_new = beta_one * mean_old + (1.0 - beta_one) * gradient
    square_new = beta_two * square_old + (1.0 - beta_two) * gradient * gradient
    fix_one = 1.0 - beta_one**STEP
    fix_two = 1.0 - beta_two**STEP
    direction = mean_new / fix_one / (jnp.sqrt(square_new / fix_two) + adam_eps)
    return (weight - step_rate * (direction + decay_weight * weight), mean_new, square_new)


def permute_all(values, target):
    count = lax.axis_size("dp") * lax.axis_size("mp")
    return lax.ppermute(values, ALL, [(i, target(i)) for i in range(count)])


def block_owners(my_dp):
    index = jnp.arange(32, dtype=jnp.int32)
    return my_dp ^ ((((index >> 2) & 3) << 1) | (index >> 4))


def tie(values, after):
    return lax.optimization_barrier((values, after))


def flip(values, bits):
    return permute_all(values, lambda i: i ^ bits)


def gather_z(values):
    return jnp.stack([values] + [flip(values, bits) for bits in (1, 2, 3)])


def scatter_core(own, other):
    return (own.astype(f32) + flip(other, 4).astype(f32)).astype(bf16)


def scatter_four(blocks, unit):
    size = blocks.shape[0] // 4
    found = [flip(blocks[i * size : (i + 1) * size], i * unit) for i in (1, 2, 3)]
    return blocks[:size], found


def add_four(own, found, last):
    one, two, three = [part.astype(f32) for part in found]
    total = (own.astype(f32) + one) + (two + three)
    return total[0] if last else total.astype(bf16)


def gather_dp(held):
    return lax.all_gather(held, "dp", axis=0, tiled=False)


def scatter_dp(blocks, dp):
    places, rows, columns = blocks.shape
    flat = blocks.reshape(places * rows, columns)
    return lax.psum_scatter(flat, "dp", scatter_dimension=0, tiled=True).reshape(
        places // dp, rows, columns
    )


def plain_gather(values):
    dp, mp = lax.axis_size("dp"), lax.axis_size("mp")
    rows, columns = values.shape
    found = lax.all_gather(values, ALL, axis=0, tiled=True).reshape(dp, mp, rows, columns)
    if rows % 16 == 0:
        return found
    return jnp.swapaxes(found, 0, 1).reshape(1, mp, dp * rows, columns)


def plain_scatter(blocks, dp):
    places, rows, columns = blocks.shape
    mp = lax.axis_size("mp")
    if places != dp * mp:
        blocks = jnp.swapaxes(blocks.reshape(mp, dp, D // dp, columns), 0, 1)
    flat = blocks.reshape(dp * mp * (D // dp), columns)
    return lax.psum_scatter(flat, ALL, scatter_dimension=0, tiled=True).astype(f32)


def shift_right(values):
    count = lax.axis_size("mp")
    return lax.ppermute(values, "mp", [(i, i + 1) for i in range(count - 1)])


def shift_left(values):
    count = lax.axis_size("mp")
    return lax.ppermute(values, "mp", [(i + 1, i) for i in range(count - 1)])


def fetch_blocks(table, near, far, targets, sems):
    copies = []
    for place in range(32):
        owner = table[place]
        source = near.at[place] if place < 16 else far.at[place - 16]
        for index, (target, begin, width) in enumerate(targets):
            copies.append(
                pltpu.make_async_copy(
                    source.at[:, pl.ds(begin, width)],
                    target.at[owner, place % 4],
                    sems.at[place, index],
                )
            )
    for copy in copies:
        copy.start()
    return copies


def attn_forward_kernel(gathered, groups, meta, table, *refs):
    if gathered:
        near, far, left, own, right, resid, norm = refs[:7]
        middle, normed, q_o, k_o, v_o, o_o, lse_o, w_o = refs[7:15]
        ext, total, sems = refs[15:]
    else:
        w_in, left, own, right, resid, norm = refs[:6]
        middle, normed, q_o, k_o, v_o, o_o, lse_o = refs[6:13]
        ext, total = refs[13:]
    step = pl.program_id(0)

    @pl.when(step == 0)
    def _():
        if gathered:
            copies = fetch_blocks(table, near, far, [(w_o, 0, D)], sems)
        for index, part in enumerate((left, own, right)):
            ext[pl.ds(3 * index, 3)] = part[...].reshape(3, CH, D)
        total[...] = jnp.zeros_like(total)
        if gathered:
            for copy in copies:
                copy.wait()

    def weight(begin, end):
        found = w_o[:, step, :, begin:end] if gathered else w_in[:, 0, :, begin:end]
        return found.reshape(D, end - begin)

    for j in range(3):
        q_o[0, j] = (mm(ext[3 + j], weight(0, PAIR)) * (LOG2E / math.sqrt(HEAD_DIM))).astype(bf16)

    def project(slot, carry):
        begin = meta[slot]
        kv_w = weight(PAIR, 3 * PAIR)
        for i in range(SLOT):
            both = mm(ext[begin + i], kv_w).astype(bf16)
            k_o[0, slot * SLOT + i] = both[:, :PAIR]
            v_o[0, slot * SLOT + i] = both[:, PAIR:]
        return carry

    lax.fori_loop(0, meta[2], project, 0)
    lane = lax.broadcasted_iota(jnp.int32, (CH, PAIR), 1) // HEAD_DIM
    lane_all = lax.broadcasted_iota(jnp.int32, (LEN, PAIR), 1) // HEAD_DIM

    for j in range(3):
        slot = meta[3 + j]
        query = q_o[0, j]
        keys = k_o[0, pl.ds(slot * SLOT, SLOT)].reshape(LEN, PAIR)
        values = v_o[0, pl.ds(slot * SLOT, SLOT)].reshape(LEN, PAIR)
        zero = jnp.zeros_like(query)
        both = jnp.concatenate([jnp.where(lane == h, query, zero) for h in range(2)], axis=0)
        scores = mm(both, keys, NT)
        top = jnp.max(scores, axis=1, keepdims=True)
        weights = jnp.exp2(scores - top).astype(bf16)
        parts = []
        for h in range(2):
            value_h = jnp.where(lane_all == h, values, jnp.ones_like(values))
            mixed = mm(weights[h * CH : (h + 1) * CH], value_h)
            sums = pltpu.roll(mixed, HEAD_DIM, 1)
            parts.append(mixed / sums)
            spread = top[h * CH : (h + 1) * CH] + jnp.log2(sums)
            lse_o[0, j, h : h + 1] = spread.T[h * HEAD_DIM : h * HEAD_DIM + 1]
        out = jnp.where(lane == 0, parts[0], parts[1]).astype(bf16)
        o_o[0, j] = out
        total[j] += mm(out, weight(3 * PAIR, D), NT)

    @pl.when(step == groups - 1)
    def _():
        for j in range(3):
            rows = pl.ds(j * CH, CH)
            values = resid[rows] + total[j]
            middle[rows] = values
            normed[rows] = layer_norm(values, norm[2:3], norm[3:4]).astype(bf16)


def attn_forward(weights, meta, table, left, own, right, resid, norm, groups, keep):
    rows = own.shape[0]
    gathered = isinstance(weights, tuple)
    const = lambda s, *_: (0, 0)
    pair = lambda s, *_: (s, 0, 0, 0)
    full = pl.BlockSpec((rows, D), const)
    near_out = kept_out if keep else jax.ShapeDtypeStruct
    out_shape = [
        near_out((rows, D), f32),
        near_out((rows, D), bf16),
        kept_out((groups, 3, CH, PAIR), bf16),
        kept_out((groups, 2 * SLOT, CH, PAIR), bf16),
        kept_out((groups, 2 * SLOT, CH, PAIR), bf16),
        kept_out((groups, 3, CH, PAIR), bf16),
        kept_out((groups, 3, 8, CH), f32),
    ]
    out_specs = [
        full,
        full,
        pl.BlockSpec((1, 3, CH, PAIR), pair),
        pl.BlockSpec((1, 2 * SLOT, CH, PAIR), pair),
        pl.BlockSpec((1, 2 * SLOT, CH, PAIR), pair),
        pl.BlockSpec((1, 3, CH, PAIR), pair),
        pl.BlockSpec((1, 3, 8, CH), pair),
    ]
    scratch = [
        pltpu.VMEM((9, CH, D), bf16),
        pltpu.VMEM((3, CH, D), f32),
    ]
    if gathered:
        w_args = list(weights)
        w_specs = [hbm(), hbm()]
        out_shape.append(kept_out((8, 4, 64, D), bf16))
        out_specs.append(pl.BlockSpec((8, 4, 64, D), pair_zero))
        scratch.append(pltpu.SemaphoreType.DMA((32, 1)))
    else:
        w_args = [weights]
        split, _, high, _ = weights.shape
        w_specs = [pl.BlockSpec((split, 1, high, D), lambda s, *_: (0, s, 0, 0))]
    outs = pl.pallas_call(
        functools.partial(attn_forward_kernel, gathered, groups),
        grid_spec=pltpu.PrefetchScalarGridSpec(
            num_scalar_prefetch=2,
            grid=(groups,),
            in_specs=w_specs
            + [full, full, full, full, pl.BlockSpec((4, D), const)],
            out_specs=out_specs,
            scratch_shapes=scratch,
        ),
        out_shape=out_shape,
        compiler_params=params(28),
        cost_estimate=pl.CostEstimate(
            flops=29_000_000_000, bytes_accessed=14_000_000, transcendentals=0
        ),
        name="attn_forward",
    )(meta, table, *from_hbm(*w_args), left, own, right, resid, norm)
    if gathered:
        return outs[:7], outs[7]
    return outs, weights


def pair_zero(s, *_):
    return (0, 0, 0, 0)


def mlp_forward_kernel(gathered, groups, table, *refs):
    if gathered:
        near, far, normed, middle, norm = refs[:5]
        refs = refs[5:]
    else:
        up_in, down_in, normed, middle, norm = refs[:5]
        refs = refs[5:]
    after, act_o, slope_o, next_o = refs[:4]
    refs = refs[4:]
    if gathered:
        up_o, down_o, total, sems = refs
    else:
        (total,) = refs
    step = pl.program_id(0)

    @pl.when(step == 0)
    def _():
        if gathered:
            copies = fetch_blocks(table, near, far, [(up_o, 0, D), (down_o, D, D)], sems)
        total[...] = jnp.zeros_like(total)
        if gathered:
            for copy in copies:
                copy.wait()

    if gathered:
        up_w = up_o[:, step].reshape(D, D)
        down_w = down_o[:, step].reshape(D, D)
    else:
        up_w = up_in[:, 0].reshape(D, D)
        down_w = down_in[:, 0].reshape(D, D)
    for j in range(3):
        rows = pl.ds(j * CH, CH)
        hidden = mm(normed[rows], up_w)
        act, slope = gelu_pair(hidden)
        act = act.astype(bf16)
        act_o[0, rows] = act
        slope_o[0, rows] = slope.astype(bf16)
        total[j] += mm(act, down_w, NT)

    @pl.when(step == groups - 1)
    def _():
        for j in range(3):
            rows = pl.ds(j * CH, CH)
            values = middle[rows] + total[j]
            after[rows] = values
            next_o[rows] = layer_norm(values, norm[0:1], norm[1:2]).astype(bf16)


def mlp_forward(weights, table, normed, middle, norm, groups):
    rows = normed.shape[0]
    gathered = not isinstance(weights[0], tuple)
    const = lambda s, *_: (0, 0)
    full = pl.BlockSpec((rows, D), const)
    part = pl.BlockSpec((1, rows, D), lambda s, *_: (s, 0, 0))
    out_shape = [
        kept_out((rows, D), f32),
        kept_out((groups, rows, D), bf16),
        kept_out((groups, rows, D), bf16),
        jax.ShapeDtypeStruct((rows, D), bf16),
    ]
    out_specs = [full, part, part, full]
    scratch = [pltpu.VMEM((3, CH, D), f32)]
    if gathered:
        w_args = list(weights)
        w_specs = [hbm(), hbm()]
        for _ in range(2):
            out_shape.append(jax.ShapeDtypeStruct((8, 4, 64, D), bf16))
            out_specs.append(pl.BlockSpec((8, 4, 64, D), pair_zero))
        scratch.append(pltpu.SemaphoreType.DMA((32, 2)))
    else:
        (up_w, up_at), (down_w, down_at) = weights
        w_args = [up_w, down_w]
        w_specs = [weight_spec(up_w, up_at), weight_spec(down_w, down_at)]
    outs = pl.pallas_call(
        functools.partial(mlp_forward_kernel, gathered, groups),
        grid_spec=pltpu.PrefetchScalarGridSpec(
            num_scalar_prefetch=1,
            grid=(groups,),
            in_specs=w_specs + [full, full, pl.BlockSpec((4, D), const)],
            out_specs=out_specs,
            scratch_shapes=scratch,
        ),
        out_shape=out_shape,
        compiler_params=params(28),
        cost_estimate=pl.CostEstimate(
            flops=15_000_000_000, bytes_accessed=18_000_000, transcendentals=0
        ),
        name="mlp_forward",
    )(table, *from_hbm(*w_args, normed, middle), norm)
    if gathered:
        return outs[:-2], ((outs[-2], 0), (outs[-1], 0))
    return outs, weights


def weight_spec(weight, at):
    split, _, high, _ = weight.shape
    return pl.BlockSpec((split, 1, high, D), lambda s, *_: (0, s, 0, at))


def put_blocks(out, table, step, groups, split, begin, values):
    high = D // split
    width = values.shape[1]
    for d in range(split):
        place = table[d * groups + step]
        out[place, :, begin : begin + width] = values[d * high : (d + 1) * high]


def mlp_backward_kernel(groups, split, meta, place, *refs):
    grad_in, d_own, d_near, d_left, d_right, source, norm_up = refs[:7]
    refs = refs[7:]
    up_in, down_in, act, slope, normed, middle, norm = refs[:7]
    refs = refs[7:]
    w_grad, grad_out, n_grad = refs[:3]
    refs = refs[3:]
    grad, low, low_t, norm_t, total = refs
    step = pl.program_id(0)

    @pl.when(step == 0)
    def _():
        n_grad[...] = jnp.zeros_like(n_grad)
        for j in range(3):
            rows = pl.ds(j * CH, CH)
            arrived = d_own[rows] + d_near[rows] + d_left[rows].astype(f32)
            arrived += d_right[rows].astype(f32)
            back, gain_grad, shift_grad = norm_backward(arrived, source[rows], norm_up[0:1])
            values = grad_in[rows] + back
            n_grad[0:1] += gain_grad
            n_grad[1:2] += shift_grad
            grad[j] = values
            rounded = values.astype(bf16)
            low[rows] = rounded
            low_t[:, j * CH : (j + 1) * CH] = rounded.T
            norm_t[:, j * CH : (j + 1) * CH] = normed[rows].T
        total[...] = jnp.zeros_like(total)

    up_w = up_in[:, 0].reshape(D, D)
    down_w = down_in[:, 0].reshape(D, D)
    down_grad = mm(low_t[...], act[0]).astype(bf16)
    put_blocks(w_grad, place, step, groups, split, D, down_grad)
    pieces = []
    for j in range(3):
        rows = pl.ds(j * CH, CH)
        piece = (mm(low[rows], down_w) * slope[0, rows].astype(f32)).astype(bf16)
        pieces.append(piece)
        total[j] += mm(piece, up_w, NT)
    up_grad = mm(norm_t[...], jnp.concatenate(pieces, axis=0)).astype(bf16)
    put_blocks(w_grad, place, step, groups, split, 0, up_grad)

    @pl.when(step == groups - 1)
    def _():
        for j in range(3):
            rows = pl.ds(j * CH, CH)
            back, gain_grad, shift_grad = norm_backward(total[j], middle[rows], norm[2:3])
            grad_out[rows] = grad[j] + back
            n_grad[2:3] += gain_grad
            n_grad[3:4] += shift_grad


def mlp_backward(
    weights, meta, place, begin, act, slope, normed, middle, norm, groups, split, after=()
):
    rows = normed.shape[0]
    const = lambda s, *_: (0, 0)
    full = pl.BlockSpec((rows, D), const)
    part = pl.BlockSpec((1, rows, D), lambda s, *_: (s, 0, 0))
    vec = pl.BlockSpec((4, D), const)
    (up_w, up_at), (down_w, down_at) = weights
    begin_specs = [full] * 6 + [vec]
    places = split * groups
    return pl.pallas_call(
        after_operands(
            functools.partial(mlp_backward_kernel, groups, split), 2, len(after)
        ),
        grid_spec=pltpu.PrefetchScalarGridSpec(
            num_scalar_prefetch=2,
            grid=(groups,),
            in_specs=[hbm()] * len(after)
            + begin_specs
            + [weight_spec(up_w, up_at), weight_spec(down_w, down_at)]
            + [part, part, full, full, vec],
            out_specs=[
                pl.BlockSpec((places, D // split, 2 * D), lambda s, *_: (0, 0, 0)),
                full,
                pl.BlockSpec((8, D), const),
            ],
            scratch_shapes=[
                pltpu.VMEM((3, CH, D), f32),
                pltpu.VMEM((rows, D), bf16),
                pltpu.VMEM((D, rows), bf16),
                pltpu.VMEM((D, rows), bf16),
                pltpu.VMEM((3, CH, D), f32),
            ],
        ),
        out_shape=[
            kept_out((places, D // split, 2 * D), bf16),
            kept_out((rows, D), f32),
            jax.ShapeDtypeStruct((8, D), f32),
        ],
        compiler_params=params(28),
        cost_estimate=pl.CostEstimate(
            flops=20_000_000_000, bytes_accessed=20_000_000, transcendentals=0
        ),
        name="mlp_backward",
    )(meta, place, *from_hbm(*after), *begin, *from_hbm(up_w, down_w, act, slope), normed, middle, norm)


def mlp_last_kernel(groups, split, meta, place, *refs):
    scale, cot, up_in, down_in, normed, middle, norm = refs[:7]
    after, w_grad, grad_out, n_grad = refs[7:11]
    low, low_t, norm_t, total, total_grad = refs[11:]
    step = pl.program_id(0)

    def start_grad(j):
        return cot[pl.ds(j * CH, CH)].astype(f32) * scale[meta[6 + j]]

    @pl.when(step == 0)
    def _():
        n_grad[...] = jnp.zeros_like(n_grad)
        for j in range(3):
            rows = pl.ds(j * CH, CH)
            rounded = start_grad(j).astype(bf16)
            low[rows] = rounded
            low_t[:, j * CH : (j + 1) * CH] = rounded.T
            norm_t[:, j * CH : (j + 1) * CH] = normed[rows].T
        total[...] = jnp.zeros_like(total)
        total_grad[...] = jnp.zeros_like(total_grad)

    up_w = up_in[:, 0].reshape(D, D)
    down_w = down_in[:, 0].reshape(D, D)
    acts, pieces = [], []
    for j in range(3):
        rows = pl.ds(j * CH, CH)
        act, slope = gelu_pair(mm(normed[rows], up_w))
        act = act.astype(bf16)
        acts.append(act)
        total[j] += mm(act, down_w, NT)
        piece = (mm(low[rows], down_w) * slope).astype(bf16)
        pieces.append(piece)
        total_grad[j] += mm(piece, up_w, NT)
    down_grad = mm(low_t[...], jnp.concatenate(acts, axis=0)).astype(bf16)
    put_blocks(w_grad, place, step, groups, split, D, down_grad)
    up_grad = mm(norm_t[...], jnp.concatenate(pieces, axis=0)).astype(bf16)
    put_blocks(w_grad, place, step, groups, split, 0, up_grad)

    @pl.when(step == groups - 1)
    def _():
        for j in range(3):
            rows = pl.ds(j * CH, CH)
            values = middle[rows]
            after[rows] = values + total[j]
            back, gain_grad, shift_grad = norm_backward(total_grad[j], values, norm[2:3])
            grad_out[rows] = start_grad(j) + back
            n_grad[2:3] += gain_grad
            n_grad[3:4] += shift_grad


def mlp_last(weights, meta, place, scale, cot, normed, middle, norm, groups, split):
    rows = normed.shape[0]
    const = lambda s, *_: (0, 0)
    full = pl.BlockSpec((rows, D), const)
    (up_w, up_at), (down_w, down_at) = weights
    places = split * groups
    return pl.pallas_call(
        functools.partial(mlp_last_kernel, groups, split),
        grid_spec=pltpu.PrefetchScalarGridSpec(
            num_scalar_prefetch=2,
            grid=(groups,),
            in_specs=[smem(), full]
            + [weight_spec(up_w, up_at), weight_spec(down_w, down_at)]
            + [full, full, pl.BlockSpec((4, D), const)],
            out_specs=[
                full,
                pl.BlockSpec((places, D // split, 2 * D), lambda s, *_: (0, 0, 0)),
                full,
                pl.BlockSpec((8, D), const),
            ],
            scratch_shapes=[
                pltpu.VMEM((rows, D), bf16),
                pltpu.VMEM((D, rows), bf16),
                pltpu.VMEM((D, rows), bf16),
                pltpu.VMEM((3, CH, D), f32),
                pltpu.VMEM((3, CH, D), f32),
            ],
        ),
        out_shape=[
            kept_out((rows, D), f32),
            kept_out((places, D // split, 2 * D), bf16),
            kept_out((rows, D), f32),
            jax.ShapeDtypeStruct((8, D), f32),
        ],
        compiler_params=params(28),
        cost_estimate=pl.CostEstimate(
            flops=30_000_000_000, bytes_accessed=18_000_000, transcendentals=0
        ),
        name="mlp_last",
    )(meta, place, scale, cot, *from_hbm(up_w, down_w), normed, middle, norm)


def head_rows(values, lane):
    zero = jnp.zeros_like(values)
    return [jnp.where(lane == h, values, zero) for h in range(2)]


def group_backward(keys, values, queries, grads, lse, delta):
    scores = mm(keys, queries, NT)
    grad_p = mm(values, grads, NT)
    probability = jnp.exp2(scores - lse)
    grad_s = (probability * (grad_p - delta)).astype(bf16)
    dv = mm(probability.astype(bf16), grads)
    dk = mm(grad_s, queries) * LN2
    both = jnp.concatenate([dk.astype(bf16), dv.astype(bf16)], axis=1)
    return both, mm(keys.T, grad_s)


def pick_heads(dq_t, index):
    begin = 2 * CH * index
    return jnp.concatenate(
        [dq_t[:HEAD_DIM, begin : begin + CH], dq_t[HEAD_DIM:, begin + CH : begin + 2 * CH]], axis=0
    )


def group_inputs(meta, q_i, lse_i, g_t, delta_t):
    lane = lax.broadcasted_iota(jnp.int32, (CH, PAIR), 1) // HEAD_DIM
    queries, grads, lse, delta = [], [], [], []
    for t in range(3):
        j = meta[9 + t]
        queries.append(head_rows(q_i[0, j], lane))
        grads.append(head_rows(g_t[t], lane))
        lse.append([lse_i[0, j, h : h + 1] for h in range(2)])
        delta.append([delta_t[t][h : h + 1] for h in range(2)])
    found = []
    for parts in ((0,), (1, 2)):
        found.append(
            tuple(
                jnp.concatenate([row for t in parts for row in rows[t]], axis=axis)
                for rows, axis in ((queries, 0), (grads, 0), (lse, 1), (delta, 1))
            )
        )
    return found


def key_range(ref, begin, count):
    return ref[0, pl.ds(begin, count)].reshape(count * CH, PAIR)


def attn_backward_far_kernel(groups, meta, *refs):
    w_in, grad_in, small, q_i, k_i, v_i, o_i, lse_i = refs[:8]
    d_left, d_own, d_right, dq_o, dkv_o, g_o, delta_o, small_o = refs[8:16]
    low, d_ext = refs[16:]
    step = pl.program_id(0)

    @pl.when(step == 0)
    def _():
        for t in range(3):
            rows = pl.ds(pl.multiple_of(meta[9 + t] * CH, CH), CH)
            low[t] = grad_in[rows].astype(bf16)
        d_ext[...] = jnp.zeros_like(d_ext)
        small_o[...] = small[...]

    def weight(begin, end):
        return w_in[:, 0, :, begin:end].reshape(D, end - begin)

    grad_low = mm(low[...].reshape(3 * CH, D), weight(3 * PAIR, D)).astype(bf16)
    g_t = [grad_low[t * CH : (t + 1) * CH] for t in range(3)]
    delta_t = []
    for t in range(3):
        g_o[0, t] = g_t[t]
        product = (g_t[t].astype(f32) * o_i[0, meta[9 + t]].astype(f32)).T
        rows = [
            jnp.sum(product[h * HEAD_DIM : (h + 1) * HEAD_DIM], axis=0, keepdims=True)
            for h in range(2)
        ]
        for h in range(2):
            delta_o[0, t, h : h + 1] = rows[h]
        delta_t.append(jnp.concatenate(rows, axis=0))
    one, two = group_inputs(meta, q_i, lse_i, g_t, delta_t)
    kv_w = weight(PAIR, 3 * PAIR)
    both, dq_t = group_backward(
        key_range(k_i, meta[12], 3), key_range(v_i, meta[12], 3), *one
    )
    dkv_o[0, 0:3] = both.reshape(3, CH, 2 * PAIR)
    d_ext[pl.ds(meta[16], 3)] += mm(both, kv_w, NT).reshape(3, CH, D)
    dq_o[0, 0] = pick_heads(dq_t, 0)
    both, dq_t = group_backward(
        key_range(k_i, meta[13], 2), key_range(v_i, meta[13], 2), *two
    )
    dkv_o[0, 3:5] = both.reshape(2, CH, 2 * PAIR)
    d_ext[pl.ds(meta[17], 2)] += mm(both, kv_w, NT).reshape(2, CH, D)
    dq_o[0, 1] = pick_heads(dq_t, 0)
    dq_o[0, 2] = pick_heads(dq_t, 1)

    @pl.when(step == groups - 1)
    def _():
        for j in range(3):
            rows = pl.ds(j * CH, CH)
            d_left[rows] = d_ext[j].astype(bf16)
            d_own[rows] = d_ext[3 + j]
            d_right[rows] = d_ext[6 + j].astype(bf16)


def attn_backward_near_kernel(groups, split, halves, meta, base, *refs):
    w_in, left, own, right, grad_in, q_i, k_i, v_i, o_i, lse_i = refs[:10]
    dq_i, dkv_i, g_i, delta_i, small = refs[10:15]
    w_grads = refs[15 : 15 + halves]
    d_own, small_o, ext_t, low_t, total, dq_all, w_all = refs[15 + halves :]
    step = pl.program_id(0)

    @pl.when(step == 0)
    def _():
        for index, part in enumerate((left, own, right)):
            for j in range(3):
                ext_t[3 * index + j] = part[pl.ds(j * CH, CH)].T
        for j in range(3):
            low_t[:, j * CH : (j + 1) * CH] = grad_in[pl.ds(j * CH, CH)].astype(bf16).T
        total[...] = jnp.zeros_like(total)
        small_o[...] = small[...]

    def weight(begin, end):
        return w_in[:, 0, :, begin:end].reshape(D, end - begin)

    def columns(begin, count):
        return jnp.concatenate([ext_t[begin + i] for i in range(count)], axis=1)

    g_t = [g_i[0, t] for t in range(3)]
    delta_t = [delta_i[0, t] for t in range(3)]
    one, two = group_inputs(meta, q_i, lse_i, g_t, delta_t)
    kv_w = weight(PAIR, 3 * PAIR)
    first, dq_one = group_backward(
        key_range(k_i, meta[14], 1), key_range(v_i, meta[14], 1), *one
    )
    second, dq_two = group_backward(
        key_range(k_i, meta[15], 2), key_range(v_i, meta[15], 2), *two
    )
    total[meta[18] - 3] += mm(first, kv_w, NT)
    total[pl.ds(meta[19] - 3, 2)] += mm(second, kv_w, NT).reshape(2, CH, D)
    for t, part in enumerate((pick_heads(dq_one, 0), pick_heads(dq_two, 0), pick_heads(dq_two, 1))):
        whole = ((dq_i[0, t] + part).T * (1.0 / math.sqrt(HEAD_DIM))).astype(bf16)
        j = meta[9 + t]
        dq_all[pl.ds(pl.multiple_of(j * CH, CH), CH)] = whole
        total[j] += mm(whole, weight(0, PAIR), NT)
    out_grad = mm(low_t[...], o_i[0].reshape(3 * CH, PAIR)).astype(bf16)
    w_all[:, 3 * PAIR :] = out_grad
    q_grad = mm(columns(3, 3), dq_all[...]).astype(bf16)
    w_all[:, :PAIR] = q_grad
    kv_grad = (
        mm(columns(meta[16], 3), dkv_i[0, 0:3].reshape(3 * CH, 2 * PAIR))
        + mm(columns(meta[17], 2), dkv_i[0, 3:5].reshape(2 * CH, 2 * PAIR))
        + mm(columns(meta[18], 1), first)
        + mm(columns(meta[19], 2), second)
    )
    w_all[:, PAIR : 3 * PAIR] = kv_grad.astype(bf16)
    high = D // split
    for apart in range(split):
        rows = pl.ds(pl.multiple_of((base[0] ^ apart) * high, high), high)
        w_grads[apart % halves][(apart // halves) * groups + step] = w_all[rows]

    @pl.when(step == groups - 1)
    def _():
        d_own[...] = total[...].reshape(3 * CH, D)


def attn_backward_far(weight, meta, grad_in, kept, groups, small, after=()):
    rows = grad_in.shape[0]
    const = lambda s, *_: (0, 0)
    pair = lambda s, *_: (s, 0, 0, 0)
    full = pl.BlockSpec((rows, D), const)
    three = pl.BlockSpec((1, 3, CH, PAIR), pair)
    eight = pl.BlockSpec((1, 2 * SLOT, CH, PAIR), pair)
    lines = pl.BlockSpec((1, 3, 8, CH), pair)
    tiny = pl.BlockSpec((8, D), const)
    return pl.pallas_call(
        after_operands(functools.partial(attn_backward_far_kernel, groups), 1, len(after)),
        grid_spec=pltpu.PrefetchScalarGridSpec(
            num_scalar_prefetch=1,
            grid=(groups,),
            in_specs=[hbm()] * len(after)
            + [weight_spec(*weight), full, tiny, three, eight, eight, three, lines],
            out_specs=[
                full,
                full,
                full,
                pl.BlockSpec((1, 3, PAIR, CH), pair),
                pl.BlockSpec((1, 5, CH, 2 * PAIR), pair),
                three,
                lines,
                tiny,
            ],
            scratch_shapes=[
                pltpu.VMEM((3, CH, D), bf16),
                pltpu.VMEM((9, CH, D), f32),
            ],
        ),
        out_shape=[
            jax.ShapeDtypeStruct((rows, D), bf16),
            jax.ShapeDtypeStruct((rows, D), f32),
            jax.ShapeDtypeStruct((rows, D), bf16),
            jax.ShapeDtypeStruct((groups, 3, PAIR, CH), f32),
            jax.ShapeDtypeStruct((groups, 5, CH, 2 * PAIR), bf16),
            jax.ShapeDtypeStruct((groups, 3, CH, PAIR), bf16),
            jax.ShapeDtypeStruct((groups, 3, 8, CH), f32),
            jax.ShapeDtypeStruct((8, D), f32),
        ],
        compiler_params=params(28),
        cost_estimate=pl.CostEstimate(
            flops=24_000_000_000, bytes_accessed=16_000_000, transcendentals=0
        ),
        name="attn_backward_far",
    )(meta, *from_hbm(*after, weight[0]), grad_in, small, *from_hbm(*kept))


def attn_backward_near(weight, meta, base, ext, grad_in, kept, far, groups, split, small, halves):
    rows = grad_in.shape[0]
    const = lambda s, *_: (0, 0)
    pair = lambda s, *_: (s, 0, 0, 0)
    full = pl.BlockSpec((rows, D), const)
    three = pl.BlockSpec((1, 3, CH, PAIR), pair)
    eight = pl.BlockSpec((1, 2 * SLOT, CH, PAIR), pair)
    lines = pl.BlockSpec((1, 3, 8, CH), pair)
    tiny = pl.BlockSpec((8, D), const)
    places = split * groups
    return pl.pallas_call(
        functools.partial(attn_backward_near_kernel, groups, split, halves),
        grid_spec=pltpu.PrefetchScalarGridSpec(
            num_scalar_prefetch=2,
            grid=(groups,),
            in_specs=[weight_spec(*weight), full, full, full, full, three, eight, eight, three, lines]
            + [
                pl.BlockSpec((1, 3, PAIR, CH), pair),
                pl.BlockSpec((1, 5, CH, 2 * PAIR), pair),
                three,
                lines,
                tiny,
            ],
            out_specs=[pl.BlockSpec((places // halves, D // split, D), lambda s, *_: (0, 0, 0))]
            * halves
            + [full, tiny],
            scratch_shapes=[
                pltpu.VMEM((9, D, CH), bf16),
                pltpu.VMEM((D, rows), bf16),
                pltpu.VMEM((3, CH, D), f32),
                pltpu.VMEM((rows, PAIR), bf16),
                pltpu.VMEM((D, D), bf16),
            ],
        ),
        out_shape=[jax.ShapeDtypeStruct((places // halves, D // split, D), bf16)] * halves
        + [jax.ShapeDtypeStruct((rows, D), f32), jax.ShapeDtypeStruct((8, D), f32)],
        compiler_params=params(28),
        cost_estimate=pl.CostEstimate(
            flops=20_000_000_000, bytes_accessed=22_000_000, transcendentals=0
        ),
        name="attn_backward_near",
    )(meta, base, *from_hbm(weight[0]), *ext, grad_in, *from_hbm(*kept), *far, small)


def entry_backward_kernel(
    grad_in, d_own, d_near, d_left, d_right, source, norm, ids, grad_out, small
):
    small[...] = jnp.zeros_like(small)
    for j in range(3):
        rows = pl.ds(j * CH, CH)
        arrived = d_own[rows] + d_near[rows] + d_left[rows].astype(f32) + d_right[rows].astype(f32)
        back, gain_grad, shift_grad = norm_backward(arrived, source[rows], norm[0:1])
        values = grad_in[rows] + back
        grad_out[rows] = values
        small[0:1] += gain_grad
        small[1:2] += shift_grad
        letter = lax.broadcasted_iota(jnp.int32, (32, CH), 0)
        chosen = (letter == ids[:, j * CH : (j + 1) * CH]).astype(bf16)
        high = values.astype(bf16)
        rest = values - high.astype(f32)
        middle = rest.astype(bf16)
        low = (rest - middle.astype(f32)).astype(bf16)
        small[8:40] += mm(chosen, high) + mm(chosen, middle) + mm(chosen, low)


def entry_backward(grad_in, d_own, d_near, d_left, d_right, source, norm, ids, after=()):
    rows = grad_in.shape[0]
    return pl.pallas_call(
        after_operands(entry_backward_kernel, 0, len(after)),
        in_specs=[hbm()] * len(after) + [vmem()] * 8,
        out_specs=[vmem()] * 2,
        out_shape=[
            kept_out((rows, D), f32),
            jax.ShapeDtypeStruct((40, D), f32),
        ],
        compiler_params=pltpu.CompilerParams(vmem_limit_bytes=40 * 1024 * 1024),
        cost_estimate=pl.CostEstimate(
            flops=100_000_000, bytes_accessed=9_000_000, transcendentals=0
        ),
        name="entry_backward",
    )(*after, grad_in, d_own, d_near, d_left, d_right, source, norm, ids)


def backward_plan(my_mp, row_start, first_seq, chunk_seq):
    lead = jnp.where(my_mp < 2, 0, 2)
    late_one = my_mp % 2 == 0
    late_two = my_mp < 2
    found = [lead, 1, 2 - lead]
    lead_seq = jnp.where(my_mp < 2, chunk_seq[0], chunk_seq[2])
    shifts = [
        (lead_seq, jnp.where(late_one, 1, 0)),
        (chunk_seq[1], jnp.where(late_two, 2, 0)),
        (lead_seq, jnp.where(late_one, 0, 3)),
        (chunk_seq[1], jnp.where(late_two, 0, 2)),
    ]
    found += [(seq - first_seq) * SLOT + shift for seq, shift in shifts]
    found += [3 + (seq * LEN - row_start) // CH + shift for seq, shift in shifts]
    return [jnp.asarray(entry) for entry in found]


def shards(
    token_ids,
    timesteps,
    importance,
    cotangent,
    qkv_weight,
    out_weight,
    up_weight,
    down_weight,
    norm_params,
    embed_table,
    qkv_first,
    qkv_second,
    out_first,
    out_second,
    up_first,
    up_second,
    down_first,
    down_second,
    norm_first,
    norm_second,
    embed_first,
    embed_second,
):
    dp, mp = lax.axis_size("dp"), lax.axis_size("mp")
    small = dp == 8 and mp == 4
    groups = mp
    split = dp if small else 1
    row_count = token_ids.shape[0]
    seq_here = timesteps.shape[0]
    high = D // dp
    my_mp = lax.axis_index("mp")
    my_dp = lax.axis_index("dp")
    row_start = my_mp * row_count

    first_seq = row_start // LEN
    last_seq = (row_start + row_count - 1) // LEN
    chunk_seq = [(row_start + CH * j) // LEN for j in range(3)]
    meta = jnp.stack(
        [
            3 + (first_seq * LEN - row_start) // CH,
            3 + (last_seq * LEN - row_start) // CH,
            last_seq - first_seq + 1,
        ]
        + [seq - first_seq for seq in chunk_seq]
        + chunk_seq
        + backward_plan(my_mp, row_start, first_seq, chunk_seq)
    ).astype(jnp.int32)
    in_order = jnp.arange(split * groups, dtype=jnp.int32)
    owner = block_owners(my_dp) if small else in_order
    base = jnp.where(small, my_dp, 0).astype(jnp.int32)[None]
    halves = 2 if small else 1

    attn_mine = []
    mlp_mine = []
    for layer in range(LAYERS):
        attn_mine.append(
            jnp.concatenate(
                [qkv_weight[layer].reshape(high, -1), out_weight[layer].T], axis=1
            ).astype(bf16)
        )
        mlp_mine.append(
            jnp.concatenate([up_weight[layer], down_weight[layer].T], axis=1).astype(bf16)
        )
    both_mine = jnp.concatenate([attn_mine[1], mlp_mine[1]], axis=1)
    if small:
        lines = row_count // D + (row_count % D > 0)
        ids_low = jnp.pad(token_ids.astype(bf16), (0, lines * D - row_count)).reshape(lines, D)
        first_mine = jnp.concatenate([attn_mine[0], ids_low], axis=0)
        first_z = gather_z(first_mine)
        attn_z = first_z[:, :high]
        ids_z = first_z[:, high:].reshape(4, lines * D)[:, :row_count].astype(jnp.int32)
        ids_left = ids_z[my_mp ^ jnp.maximum(my_mp - 1, 0)]
        ids_right = ids_z[my_mp ^ jnp.minimum(my_mp + 1, mp - 1)]
    else:
        ids_left, ids_right = shift_right(token_ids), shift_left(token_ids)
    ids_ext = jnp.concatenate([ids_left, token_ids, ids_right])
    seq_ext = (row_start - row_count + jnp.arange(3 * row_count, dtype=jnp.int32)) // LEN
    letters = (ids_ext[:, None] == jnp.arange(VOCAB, dtype=jnp.int32)[None, :]).astype(f32)
    member = (seq_ext[:, None] == jnp.arange(seq_here, dtype=jnp.int32)[None, :]).astype(f32)
    entry_ext = jnp.dot(letters, embed_table, precision=highest) + jnp.dot(
        member, time_features(timesteps), precision=highest
    )
    normed_ext = layer_norm(entry_ext, norm_params[0, 0], norm_params[0, 1]).astype(bf16)
    resid = entry_ext[row_count : 2 * row_count]
    ext = (
        normed_ext[:row_count],
        normed_ext[row_count : 2 * row_count],
        normed_ext[2 * row_count :],
    )

    if small:
        mlp_first, attn_z = tie(mlp_mine[0], attn_z)
        attn_sent = [flip(attn_z, bits) for bits in (8, 16, 24)]
        attn_sent, (ext, resid) = tie(attn_sent, (ext, resid))
        attn_xy = jnp.concatenate([attn_z] + list(attn_sent), axis=0)
        mlp_z = gather_z(mlp_first)
        mlp_z, attn_xy = tie(mlp_z, attn_xy)
        attn_w = [(attn_xy, flip(attn_xy, 4))]
        mlp_found = gather_dp(mlp_z)
        both_mine, mlp_z = tie(both_mine, mlp_z)
        both_sent = [flip(both_mine, bits) for bits in (1, 2, 3)]
    else:
        attn_w = [plain_gather(attn_mine[0])]
        mlp_found = plain_gather(mlp_mine[0])
        attn_w.append(plain_gather(both_mine))
        mlp_w = [((mlp_found, 0), (mlp_found, 1)), ((attn_w[1], 1), (attn_w[1], 2))]

    kept = []
    for layer in range(LAYERS):
        last = layer == LAYERS - 1
        outs, w_attn = attn_forward(
            attn_w[layer], meta, owner, *ext, resid, norm_params[layer], groups, layer + 1 < LAYERS
        )
        middle, normed = outs[:2]
        if small and layer == 0:
            both_sent, normed = tie(both_sent, normed)
            both_found = gather_dp(jnp.stack([both_mine] + list(both_sent)))
            attn_w.append(both_found)
            mlp_w = [((mlp_found, 0), (mlp_found, 1)), ((both_found, 1), (both_found, 2))]
        w_mlp = mlp_w[layer]
        if layer + 1 < LAYERS:
            mlp_outs, w_mlp = mlp_forward(
                w_mlp, owner, normed, middle, norm_params[layer + 1], groups
            )
        kept.append((ext, resid, middle, normed, outs[2:], mlp_outs[1:3], (w_attn, 0), w_mlp))
        if layer + 1 < LAYERS:
            resid, following = mlp_outs[0], mlp_outs[3]
            ext = (shift_right(following), following, shift_left(following))

    norm_grads = [[None] * 4 for _ in range(LAYERS)]
    attn_grads = [None] * LAYERS
    mlp_grads = [None] * LAYERS
    after = ()
    for layer in reversed(range(LAYERS)):
        ext, source, middle, normed, attn_kept, (act, slope), w_attn, w_mlp = kept[layer]
        norm = norm_params[layer]
        if layer + 1 == LAYERS:
            activations, mlp_grad, grad_mid, n_grad = mlp_last(
                w_mlp, meta, in_order, importance, cotangent, normed, middle, norm, groups, split
            )
        else:
            mlp_grad, grad_mid, n_grad = mlp_backward(
                w_mlp,
                meta,
                in_order,
                begin,
                act,
                slope,
                normed,
                middle,
                norm,
                groups,
                split,
                after,
            )
        after = ()
        if small:
            if layer + 1 < LAYERS:
                attn_found, (mlp_grad, grad_mid) = tie(attn_found, (mlp_grad, grad_mid))
            mlp_rows = scatter_dp(mlp_grad, dp)
            if layer + 1 < LAYERS:
                attn_rows = add_four(attn_mine_rows, attn_found, False)
                above = jnp.concatenate([attn_rows, above], axis=2)
                above_mine, above_found = scatter_four(above, 1)
                after = (above,)
        d_left, d_own, d_right, *far, n_grad = attn_backward_far(
            w_attn, meta, grad_mid, attn_kept, groups, n_grad, after
        )
        if small and layer + 1 < LAYERS:
            above_found, (d_left, d_right) = tie(above_found, (d_left, d_right))
        from_right = shift_left(d_left)
        from_left = shift_right(d_right)
        *attn_grad, d_near, n_grad = attn_backward_near(
            w_attn, meta, base, ext, grad_mid, attn_kept, far, groups, split, n_grad, halves
        )
        (from_left, from_right), (attn_grad, d_near) = tie(
            (from_left, from_right), (attn_grad, d_near)
        )
        after = ()
        if not small:
            mlp_grads[layer] = plain_scatter(mlp_grad, dp)
            attn_grads[layer] = plain_scatter(attn_grad[0], dp)
        elif layer + 1 == LAYERS:
            attn_held = scatter_core(*attn_grad)
            attn_mine_rows, attn_found = scatter_four(attn_held, 8)
            above = mlp_rows
            after = (attn_held,)
        else:
            above_total = add_four(above_mine, above_found, True)
            attn_grads[1] = above_total[:, :D]
            mlp_grads[1] = above_total[:, D:]
        norm_grads[layer][2:] = [n_grad[2], n_grad[3]]
        if layer + 1 < LAYERS:
            norm_grads[layer + 1][:2] = [n_grad[0], n_grad[1]]
        begin = (grad_mid, d_own, d_near, from_left, from_right, source, norm_params[layer])
    input_grad, reduced = entry_backward(*begin, token_ids[None, :])
    norm_grads[0][:2] = [reduced[0], reduced[1]]
    stacked = jnp.concatenate(
        [jnp.stack([row for rows in norm_grads for row in rows]), reduced[8:40]], axis=0
    )
    if small:
        rows = D // dp
        rest = stacked.astype(bf16)
        rest = (rest.astype(f32) + flip(rest, 4).astype(f32)).astype(bf16)
        held = scatter_core(*attn_grad).reshape(16 * rows, D)
        sent = [
            flip(jnp.concatenate([held[4 * rows * i : 4 * rows * (i + 1)], rest], axis=0), 8 * i)
            for i in (1, 2, 3)
        ]
        mlp_own, mlp_sent = scatter_four(mlp_rows, 1)
        mlp_sent, sent = tie(mlp_sent, sent)
        mine = add_four(jnp.concatenate([held[: 4 * rows], rest], axis=0)[None], [p[None] for p in sent], True)
        held, rest = mine[: 4 * rows].astype(bf16), mine[4 * rows :].astype(bf16)
        sent = [
            flip(jnp.concatenate([held[rows * i : rows * (i + 1)], rest], axis=0), i)
            for i in (1, 2, 3)
        ]
        total = add_four(
            jnp.concatenate([held[:rows], rest], axis=0)[None], [p[None] for p in sent], True
        )
        attn_grads[0] = total[:rows]
        stacked = total[rows:]
        mlp_grads[0] = add_four(mlp_own, mlp_sent, True)
    else:
        stacked = lax.psum(stacked, ALL)
    norm_grad = stacked[: 4 * LAYERS].reshape(LAYERS, 4, D)
    embed_grad = stacked[4 * LAYERS : 4 * LAYERS + VOCAB]

    qkv_grad = jnp.stack([g[:, : 3 * PAIR].reshape(high, 3, PAIR) for g in attn_grads])
    out_grad = jnp.stack([g[:, 3 * PAIR :].T for g in attn_grads])
    up_grad = jnp.stack([g[:, :D] for g in mlp_grads])
    down_grad = jnp.stack([g[:, D:].T for g in mlp_grads])
    qkv_master, qkv_mean, qkv_square = adamw(
        qkv_weight, qkv_first, qkv_second, qkv_grad, 2.0 / math.sqrt(D), decay_matrix
    )
    out_master, out_mean, out_square = adamw(
        out_weight, out_first, out_second, out_grad, 2.0 / math.sqrt(D), decay_matrix
    )
    up_master, up_mean, up_square = adamw(
        up_weight, up_first, up_second, up_grad, 2.0 / math.sqrt(D), decay_matrix
    )
    down_master, down_mean, down_square = adamw(
        down_weight, down_first, down_second, down_grad, 2.0 / math.sqrt(FF), decay_matrix
    )
    norm_master, norm_mean, norm_square = adamw(
        norm_params, norm_first, norm_second, norm_grad, vector_rate, 0.0
    )
    embed_master, embed_mean, embed_square = adamw(
        embed_table, embed_first, embed_second, embed_grad, embed_rate, 0.0
    )
    return (
        activations,
        input_grad,
        qkv_master,
        qkv_mean,
        qkv_square,
        qkv_master.astype(bf16),
        out_master,
        out_mean,
        out_square,
        out_master.astype(bf16),
        up_master,
        up_mean,
        up_square,
        up_master.astype(bf16),
        down_master,
        down_mean,
        down_square,
        down_master.astype(bf16),
        norm_master,
        norm_mean,
        norm_square,
        embed_master,
        embed_mean,
        embed_square,
    )


def solution(mesh):
    rows = P(("dp", "mp"), None)
    qkv = P(None, "dp", None, "mp")
    wide = P(None, "mp", "dp")
    tall = P(None, "dp", "mp")
    same = P()
    return jax.shard_map(
        shards,
        mesh=mesh,
        in_specs=(P(("dp", "mp")), P("dp"), P("dp"), rows, qkv, wide, tall, wide, same, same)
        + (qkv, qkv, wide, wide, tall, tall, wide, wide, same, same, same, same),
        out_specs=(rows, rows)
        + (qkv,) * 4
        + (wide,) * 4
        + (tall,) * 4
        + (wide,) * 4
        + (same,) * 6,
        check_vma=False,
    )
```

```python
import functools
import math

import jax
import jax.numpy as jnp
from jax import lax
from jax.experimental import pallas as pl
from jax.experimental.pallas import tpu as pltpu
from jax.sharding import PartitionSpec as P

HEAD_DIM = 64
FF = 2048
VOCAB = 27
LAYERS = 2
LEN = 1024
STEP = 10
D = 512
PAIR = 2 * HEAD_DIM
CH = 256
SLOT = LEN // CH

bf16 = jnp.bfloat16
f32 = jnp.float32
highest = lax.Precision.HIGHEST
eps_norm = 1e-05
beta_one = 0.5
beta_two = 0.5
adam_eps = 1e-08
decay_matrix = 0.01
vector_rate = 0.6
embed_rate = 1.0
LOG2E = math.log2(math.e)
LN2 = math.log(2.0)
ALL = ("dp", "mp")

NN = (((1,), (0,)), ((), ()))
NT = (((1,), (1,)), ((), ()))


def mm(left, right, dims=NN):
    return lax.dot_general(left, right, dims, preferred_element_type=f32)


def vmem():
    return pl.BlockSpec(memory_space=pltpu.VMEM)


def smem():
    return pl.BlockSpec(memory_space=pltpu.SMEM)


def hbm():
    return pl.BlockSpec(memory_space=pl.ANY)


def after_operands(kernel, prefetched, count):
    def call(*refs):
        return kernel(*refs[:prefetched], *refs[prefetched + count :])

    return call


def kept_out(shape, dtype):
    return pltpu.HBM(shape, dtype)


def from_hbm(*arrays):
    return tuple(pltpu.with_memory_space_constraint(x, pltpu.HBM) for x in arrays)


def params(mib):
    return pltpu.CompilerParams(
        dimension_semantics=("arbitrary",), vmem_limit_bytes=mib * 1024 * 1024
    )


def norm_parts(values):
    row_mean = jnp.mean(values, axis=-1, keepdims=True)
    centered = values - row_mean
    variance = jnp.mean(centered * centered, axis=-1, keepdims=True)
    inverse = lax.rsqrt(variance + eps_norm)
    return centered * inverse, inverse


def layer_norm(values, gain_vec, shift_vec):
    scaled, _ = norm_parts(values)
    return scaled * gain_vec + shift_vec


def norm_backward(grad_out, values, gain_vec):
    scaled, inverse = norm_parts(values)
    weighted = grad_out * gain_vec
    mean_plain = jnp.mean(weighted, axis=-1, keepdims=True)
    mean_scaled = jnp.mean(weighted * scaled, axis=-1, keepdims=True)
    grad_in = (weighted - mean_plain - scaled * mean_scaled) * inverse
    gain_grad = jnp.sum(grad_out * scaled, axis=0, keepdims=True)
    shift_grad = jnp.sum(grad_out, axis=0, keepdims=True)
    return grad_in, gain_grad, shift_grad


def gelu_pair(hidden):
    square = hidden * hidden
    bell = jnp.exp2(square * (-0.5 * LOG2E))
    ratio = 1.0 / (1.0 + (0.3275911 / math.sqrt(2.0)) * jnp.abs(hidden))
    poly = ratio * (
        0.5 * 0.254829592
        + ratio
        * (
            0.5 * -0.284496736
            + ratio * (0.5 * 1.421413741 + ratio * (0.5 * -1.453152027 + ratio * (0.5 * 1.061405429)))
        )
    )
    tail = poly * bell
    phi = jnp.where(hidden < 0.0, tail, 1.0 - tail)
    return hidden * phi, phi + hidden * bell * (1.0 / math.sqrt(2.0 * math.pi))


def time_features(step_values):
    half_width = D // 2
    frequency = jnp.exp(-math.log(10000.0) * jnp.arange(half_width, dtype=f32) / half_width)
    angles = step_values.astype(f32)[:, None] * frequency[None, :]
    return jnp.concatenate([jnp.sin(angles), jnp.cos(angles)], axis=1)


def adamw(weight, mean_old, square_old, gradient, step_rate, decay_weight):
    mean_new = beta_one * mean_old + (1.0 - beta_one) * gradient
    square_new = beta_two * square_old + (1.0 - beta_two) * gradient * gradient
    fix_one = 1.0 - beta_one**STEP
    fix_two = 1.0 - beta_two**STEP
    direction = mean_new / fix_one / (jnp.sqrt(square_new / fix_two) + adam_eps)
    return (weight - step_rate * (direction + decay_weight * weight), mean_new, square_new)


def permute_all(values, target):
    count = lax.axis_size("dp") * lax.axis_size("mp")
    return lax.ppermute(values, ALL, [(i, target(i)) for i in range(count)])


def block_owners(my_dp):
    index = jnp.arange(32, dtype=jnp.int32)
    return my_dp ^ ((((index >> 2) & 3) << 1) | (index >> 4))


def tie(values, after):
    return lax.optimization_barrier((values, after))


def flip(values, bits):
    return permute_all(values, lambda i: i ^ bits)


def gather_z(values):
    return jnp.stack([values] + [flip(values, bits) for bits in (1, 2, 3)])


def scatter_core(own, other):
    return (own.astype(f32) + flip(other, 4).astype(f32)).astype(bf16)


def scatter_four(blocks, unit):
    size = blocks.shape[0] // 4
    found = [flip(blocks[i * size : (i + 1) * size], i * unit) for i in (1, 2, 3)]
    return blocks[:size], found


def add_four(own, found, last):
    one, two, three = [part.astype(f32) for part in found]
    total = (own.astype(f32) + one) + (two + three)
    return total[0] if last else total.astype(bf16)


def gather_dp(held):
    return lax.all_gather(held, "dp", axis=0, tiled=False)


def scatter_dp(blocks, dp):
    places, rows, columns = blocks.shape
    flat = blocks.reshape(places * rows, columns)
    return lax.psum_scatter(flat, "dp", scatter_dimension=0, tiled=True).reshape(
        places // dp, rows, columns
    )


def plain_gather(values):
    dp, mp = lax.axis_size("dp"), lax.axis_size("mp")
    rows, columns = values.shape
    found = lax.all_gather(values, ALL, axis=0, tiled=True).reshape(dp, mp, rows, columns)
    if rows % 16 == 0:
        return found
    return jnp.swapaxes(found, 0, 1).reshape(1, mp, dp * rows, columns)


def plain_scatter(blocks, dp):
    places, rows, columns = blocks.shape
    mp = lax.axis_size("mp")
    if places != dp * mp:
        blocks = jnp.swapaxes(blocks.reshape(mp, dp, D // dp, columns), 0, 1)
    flat = blocks.reshape(dp * mp * (D // dp), columns)
    return lax.psum_scatter(flat, ALL, scatter_dimension=0, tiled=True).astype(f32)


def shift_right(values):
    count = lax.axis_size("mp")
    return lax.ppermute(values, "mp", [(i, i + 1) for i in range(count - 1)])


def shift_left(values):
    count = lax.axis_size("mp")
    return lax.ppermute(values, "mp", [(i + 1, i) for i in range(count - 1)])


def fetch_blocks(table, near, far, targets, sems):
    copies = []
    for place in range(32):
        owner = table[place]
        source = near.at[place] if place < 16 else far.at[place - 16]
        for index, (target, begin, width) in enumerate(targets):
            copies.append(
                pltpu.make_async_copy(
                    source.at[:, pl.ds(begin, width)],
                    target.at[owner, place % 4],
                    sems.at[place, index],
                )
            )
    for copy in copies:
        copy.start()
    return copies


def attn_forward_kernel(gathered, groups, meta, table, *refs):
    if gathered:
        near, far, left, own, right, resid, norm = refs[:7]
        middle, normed, q_o, k_o, v_o, o_o, lse_o, w_o = refs[7:15]
        ext, total, sems = refs[15:]
    else:
        w_in, left, own, right, resid, norm = refs[:6]
        middle, normed, q_o, k_o, v_o, o_o, lse_o = refs[6:13]
        ext, total = refs[13:]
    step = pl.program_id(0)

    @pl.when(step == 0)
    def _():
        if gathered:
            copies = fetch_blocks(table, near, far, [(w_o, 0, D)], sems)
        for index, part in enumerate((left, own, right)):
            ext[pl.ds(3 * index, 3)] = part[...].reshape(3, CH, D)
        total[...] = jnp.zeros_like(total)
        if gathered:
            for copy in copies:
                copy.wait()

    def weight(begin, end):
        found = w_o[:, step, :, begin:end] if gathered else w_in[:, 0, :, begin:end]
        return found.reshape(D, end - begin)

    for j in range(3):
        q_o[0, j] = (mm(ext[3 + j], weight(0, PAIR)) * (LOG2E / math.sqrt(HEAD_DIM))).astype(bf16)

    def project(slot, carry):
        begin = meta[slot]
        kv_w = weight(PAIR, 3 * PAIR)
        for i in range(SLOT):
            both = mm(ext[begin + i], kv_w).astype(bf16)
            k_o[0, slot * SLOT + i] = both[:, :PAIR]
            v_o[0, slot * SLOT + i] = both[:, PAIR:]
        return carry

    lax.fori_loop(0, meta[2], project, 0)
    lane = lax.broadcasted_iota(jnp.int32, (CH, PAIR), 1) // HEAD_DIM
    lane_all = lax.broadcasted_iota(jnp.int32, (LEN, PAIR), 1) // HEAD_DIM

    for j in range(3):
        slot = meta[3 + j]
        query = q_o[0, j]
        keys = k_o[0, pl.ds(slot * SLOT, SLOT)].reshape(LEN, PAIR)
        values = v_o[0, pl.ds(slot * SLOT, SLOT)].reshape(LEN, PAIR)
        zero = jnp.zeros_like(query)
        both = jnp.concatenate([jnp.where(lane == h, query, zero) for h in range(2)], axis=0)
        scores = mm(both, keys, NT)
        top = jnp.max(scores, axis=1, keepdims=True)
        weights = jnp.exp2(scores - top).astype(bf16)
        parts = []
        for h in range(2):
            value_h = jnp.where(lane_all == h, values, jnp.ones_like(values))
            mixed = mm(weights[h * CH : (h + 1) * CH], value_h)
            sums = pltpu.roll(mixed, HEAD_DIM, 1)
            parts.append(mixed / sums)
            spread = top[h * CH : (h + 1) * CH] + jnp.log2(sums)
            lse_o[0, j, h : h + 1] = spread.T[h * HEAD_DIM : h * HEAD_DIM + 1]
        out = jnp.where(lane == 0, parts[0], parts[1]).astype(bf16)
        o_o[0, j] = out
        total[j] += mm(out, weight(3 * PAIR, D), NT)

    @pl.when(step == groups - 1)
    def _():
        for j in range(3):
            rows = pl.ds(j * CH, CH)
            values = resid[rows] + total[j]
            middle[rows] = values
            normed[rows] = layer_norm(values, norm[2:3], norm[3:4]).astype(bf16)


def attn_forward(weights, meta, table, left, own, right, resid, norm, groups):
    rows = own.shape[0]
    gathered = isinstance(weights, tuple)
    const = lambda s, *_: (0, 0)
    pair = lambda s, *_: (s, 0, 0, 0)
    full = pl.BlockSpec((rows, D), const)
    out_shape = [
        kept_out((rows, D), f32),
        kept_out((rows, D), bf16),
        kept_out((groups, 3, CH, PAIR), bf16),
        kept_out((groups, 2 * SLOT, CH, PAIR), bf16),
        kept_out((groups, 2 * SLOT, CH, PAIR), bf16),
        kept_out((groups, 3, CH, PAIR), bf16),
        kept_out((groups, 3, 8, CH), f32),
    ]
    out_specs = [
        full,
        full,
        pl.BlockSpec((1, 3, CH, PAIR), pair),
        pl.BlockSpec((1, 2 * SLOT, CH, PAIR), pair),
        pl.BlockSpec((1, 2 * SLOT, CH, PAIR), pair),
        pl.BlockSpec((1, 3, CH, PAIR), pair),
        pl.BlockSpec((1, 3, 8, CH), pair),
    ]
    scratch = [
        pltpu.VMEM((9, CH, D), bf16),
        pltpu.VMEM((3, CH, D), f32),
    ]
    if gathered:
        w_args = list(weights)
        w_specs = [hbm(), hbm()]
        out_shape.append(kept_out((8, 4, 64, D), bf16))
        out_specs.append(pl.BlockSpec((8, 4, 64, D), pair_zero))
        scratch.append(pltpu.SemaphoreType.DMA((32, 1)))
    else:
        w_args = [weights]
        split, _, high, _ = weights.shape
        w_specs = [pl.BlockSpec((split, 1, high, D), lambda s, *_: (0, s, 0, 0))]
    outs = pl.pallas_call(
        functools.partial(attn_forward_kernel, gathered, groups),
        grid_spec=pltpu.PrefetchScalarGridSpec(
            num_scalar_prefetch=2,
            grid=(groups,),
            in_specs=w_specs
            + [full, full, full, full, pl.BlockSpec((4, D), const)],
            out_specs=out_specs,
            scratch_shapes=scratch,
        ),
        out_shape=out_shape,
        compiler_params=params(28),
        cost_estimate=pl.CostEstimate(
            flops=29_000_000_000, bytes_accessed=14_000_000, transcendentals=0
        ),
        name="attn_forward",
    )(meta, table, *from_hbm(*w_args, left, own, right, resid), norm)
    if gathered:
        return outs[:7], outs[7]
    return outs, weights


def pair_zero(s, *_):
    return (0, 0, 0, 0)


def mlp_forward_kernel(gathered, groups, table, *refs):
    if gathered:
        near, far, normed, middle, norm = refs[:5]
        refs = refs[5:]
    else:
        up_in, down_in, normed, middle, norm = refs[:5]
        refs = refs[5:]
    after, act_o, slope_o, next_o = refs[:4]
    refs = refs[4:]
    if gathered:
        up_o, down_o, total, sems = refs
    else:
        (total,) = refs
    step = pl.program_id(0)

    @pl.when(step == 0)
    def _():
        if gathered:
            copies = fetch_blocks(table, near, far, [(up_o, 0, D), (down_o, D, D)], sems)
        total[...] = jnp.zeros_like(total)
        if gathered:
            for copy in copies:
                copy.wait()

    if gathered:
        up_w = up_o[:, step].reshape(D, D)
        down_w = down_o[:, step].reshape(D, D)
    else:
        up_w = up_in[:, 0].reshape(D, D)
        down_w = down_in[:, 0].reshape(D, D)
    for j in range(3):
        rows = pl.ds(j * CH, CH)
        hidden = mm(normed[rows], up_w)
        act, slope = gelu_pair(hidden)
        act = act.astype(bf16)
        act_o[0, rows] = act
        slope_o[0, rows] = slope.astype(bf16)
        total[j] += mm(act, down_w, NT)

    @pl.when(step == groups - 1)
    def _():
        for j in range(3):
            rows = pl.ds(j * CH, CH)
            values = middle[rows] + total[j]
            after[rows] = values
            next_o[rows] = layer_norm(values, norm[0:1], norm[1:2]).astype(bf16)


def mlp_forward(weights, table, normed, middle, norm, groups):
    rows = normed.shape[0]
    gathered = not isinstance(weights[0], tuple)
    const = lambda s, *_: (0, 0)
    full = pl.BlockSpec((rows, D), const)
    part = pl.BlockSpec((1, rows, D), lambda s, *_: (s, 0, 0))
    out_shape = [
        kept_out((rows, D), f32),
        kept_out((groups, rows, D), bf16),
        kept_out((groups, rows, D), bf16),
        jax.ShapeDtypeStruct((rows, D), bf16),
    ]
    out_specs = [full, part, part, full]
    scratch = [pltpu.VMEM((3, CH, D), f32)]
    if gathered:
        w_args = list(weights)
        w_specs = [hbm(), hbm()]
        for _ in range(2):
            out_shape.append(jax.ShapeDtypeStruct((8, 4, 64, D), bf16))
            out_specs.append(pl.BlockSpec((8, 4, 64, D), pair_zero))
        scratch.append(pltpu.SemaphoreType.DMA((32, 2)))
    else:
        (up_w, up_at), (down_w, down_at) = weights
        w_args = [up_w, down_w]
        w_specs = [weight_spec(up_w, up_at), weight_spec(down_w, down_at)]
    outs = pl.pallas_call(
        functools.partial(mlp_forward_kernel, gathered, groups),
        grid_spec=pltpu.PrefetchScalarGridSpec(
            num_scalar_prefetch=1,
            grid=(groups,),
            in_specs=w_specs + [full, full, pl.BlockSpec((4, D), const)],
            out_specs=out_specs,
            scratch_shapes=scratch,
        ),
        out_shape=out_shape,
        compiler_params=params(28),
        cost_estimate=pl.CostEstimate(
            flops=15_000_000_000, bytes_accessed=18_000_000, transcendentals=0
        ),
        name="mlp_forward",
    )(table, *from_hbm(*w_args, normed, middle), norm)
    if gathered:
        return outs[:-2], ((outs[-2], 0), (outs[-1], 0))
    return outs, weights


def weight_spec(weight, at):
    split, _, high, _ = weight.shape
    return pl.BlockSpec((split, 1, high, D), lambda s, *_: (0, s, 0, at))


def put_blocks(out, table, step, groups, split, begin, values):
    high = D // split
    width = values.shape[1]
    for d in range(split):
        place = table[d * groups + step]
        out[place, :, begin : begin + width] = values[d * high : (d + 1) * high]


def mlp_backward_kernel(groups, split, meta, place, *refs):
    grad_in, d_own, d_near, d_left, d_right, source, norm_up = refs[:7]
    refs = refs[7:]
    up_in, down_in, act, slope, normed, middle, norm = refs[:7]
    refs = refs[7:]
    w_grad, grad_out, n_grad = refs[:3]
    refs = refs[3:]
    grad, low, low_t, norm_t, total = refs
    step = pl.program_id(0)

    @pl.when(step == 0)
    def _():
        n_grad[...] = jnp.zeros_like(n_grad)
        for j in range(3):
            rows = pl.ds(j * CH, CH)
            arrived = d_own[rows] + d_near[rows] + d_left[rows].astype(f32)
            arrived += d_right[rows].astype(f32)
            back, gain_grad, shift_grad = norm_backward(arrived, source[rows], norm_up[0:1])
            values = grad_in[rows] + back
            n_grad[0:1] += gain_grad
            n_grad[1:2] += shift_grad
            grad[j] = values
            rounded = values.astype(bf16)
            low[rows] = rounded
            low_t[:, j * CH : (j + 1) * CH] = rounded.T
            norm_t[:, j * CH : (j + 1) * CH] = normed[rows].T
        total[...] = jnp.zeros_like(total)

    up_w = up_in[:, 0].reshape(D, D)
    down_w = down_in[:, 0].reshape(D, D)
    down_grad = mm(low_t[...], act[0]).astype(bf16)
    put_blocks(w_grad, place, step, groups, split, D, down_grad)
    pieces = []
    for j in range(3):
        rows = pl.ds(j * CH, CH)
        piece = (mm(low[rows], down_w) * slope[0, rows].astype(f32)).astype(bf16)
        pieces.append(piece)
        total[j] += mm(piece, up_w, NT)
    up_grad = mm(norm_t[...], jnp.concatenate(pieces, axis=0)).astype(bf16)
    put_blocks(w_grad, place, step, groups, split, 0, up_grad)

    @pl.when(step == groups - 1)
    def _():
        for j in range(3):
            rows = pl.ds(j * CH, CH)
            back, gain_grad, shift_grad = norm_backward(total[j], middle[rows], norm[2:3])
            grad_out[rows] = grad[j] + back
            n_grad[2:3] += gain_grad
            n_grad[3:4] += shift_grad


def mlp_backward(
    weights, meta, place, begin, act, slope, normed, middle, norm, groups, split, after=()
):
    rows = normed.shape[0]
    const = lambda s, *_: (0, 0)
    full = pl.BlockSpec((rows, D), const)
    part = pl.BlockSpec((1, rows, D), lambda s, *_: (s, 0, 0))
    vec = pl.BlockSpec((4, D), const)
    (up_w, up_at), (down_w, down_at) = weights
    begin_specs = [full] * 6 + [vec]
    places = split * groups
    return pl.pallas_call(
        after_operands(
            functools.partial(mlp_backward_kernel, groups, split), 2, len(after)
        ),
        grid_spec=pltpu.PrefetchScalarGridSpec(
            num_scalar_prefetch=2,
            grid=(groups,),
            in_specs=[hbm()] * len(after)
            + begin_specs
            + [weight_spec(up_w, up_at), weight_spec(down_w, down_at)]
            + [part, part, full, full, vec],
            out_specs=[
                pl.BlockSpec((places, D // split, 2 * D), lambda s, *_: (0, 0, 0)),
                full,
                pl.BlockSpec((8, D), const),
            ],
            scratch_shapes=[
                pltpu.VMEM((3, CH, D), f32),
                pltpu.VMEM((rows, D), bf16),
                pltpu.VMEM((D, rows), bf16),
                pltpu.VMEM((D, rows), bf16),
                pltpu.VMEM((3, CH, D), f32),
            ],
        ),
        out_shape=[
            kept_out((places, D // split, 2 * D), bf16),
            kept_out((rows, D), f32),
            jax.ShapeDtypeStruct((8, D), f32),
        ],
        compiler_params=params(28),
        cost_estimate=pl.CostEstimate(
            flops=20_000_000_000, bytes_accessed=20_000_000, transcendentals=0
        ),
        name="mlp_backward",
    )(meta, place, *from_hbm(*after), *begin, *from_hbm(up_w, down_w, act, slope), normed, middle, norm)


def mlp_last_kernel(groups, split, meta, place, *refs):
    scale, cot, up_in, down_in, normed, middle, norm = refs[:7]
    after, w_grad, grad_out, n_grad = refs[7:11]
    low, low_t, norm_t, total, total_grad = refs[11:]
    step = pl.program_id(0)

    def start_grad(j):
        return cot[pl.ds(j * CH, CH)].astype(f32) * scale[meta[6 + j]]

    @pl.when(step == 0)
    def _():
        n_grad[...] = jnp.zeros_like(n_grad)
        for j in range(3):
            rows = pl.ds(j * CH, CH)
            rounded = start_grad(j).astype(bf16)
            low[rows] = rounded
            low_t[:, j * CH : (j + 1) * CH] = rounded.T
            norm_t[:, j * CH : (j + 1) * CH] = normed[rows].T
        total[...] = jnp.zeros_like(total)
        total_grad[...] = jnp.zeros_like(total_grad)

    up_w = up_in[:, 0].reshape(D, D)
    down_w = down_in[:, 0].reshape(D, D)
    acts, pieces = [], []
    for j in range(3):
        rows = pl.ds(j * CH, CH)
        act, slope = gelu_pair(mm(normed[rows], up_w))
        act = act.astype(bf16)
        acts.append(act)
        total[j] += mm(act, down_w, NT)
        piece = (mm(low[rows], down_w) * slope).astype(bf16)
        pieces.append(piece)
        total_grad[j] += mm(piece, up_w, NT)
    down_grad = mm(low_t[...], jnp.concatenate(acts, axis=0)).astype(bf16)
    put_blocks(w_grad, place, step, groups, split, D, down_grad)
    up_grad = mm(norm_t[...], jnp.concatenate(pieces, axis=0)).astype(bf16)
    put_blocks(w_grad, place, step, groups, split, 0, up_grad)

    @pl.when(step == groups - 1)
    def _():
        for j in range(3):
            rows = pl.ds(j * CH, CH)
            values = middle[rows]
            after[rows] = values + total[j]
            back, gain_grad, shift_grad = norm_backward(total_grad[j], values, norm[2:3])
            grad_out[rows] = start_grad(j) + back
            n_grad[2:3] += gain_grad
            n_grad[3:4] += shift_grad


def mlp_last(weights, meta, place, scale, cot, normed, middle, norm, groups, split):
    rows = normed.shape[0]
    const = lambda s, *_: (0, 0)
    full = pl.BlockSpec((rows, D), const)
    (up_w, up_at), (down_w, down_at) = weights
    places = split * groups
    return pl.pallas_call(
        functools.partial(mlp_last_kernel, groups, split),
        grid_spec=pltpu.PrefetchScalarGridSpec(
            num_scalar_prefetch=2,
            grid=(groups,),
            in_specs=[smem(), full]
            + [weight_spec(up_w, up_at), weight_spec(down_w, down_at)]
            + [full, full, pl.BlockSpec((4, D), const)],
            out_specs=[
                full,
                pl.BlockSpec((places, D // split, 2 * D), lambda s, *_: (0, 0, 0)),
                full,
                pl.BlockSpec((8, D), const),
            ],
            scratch_shapes=[
                pltpu.VMEM((rows, D), bf16),
                pltpu.VMEM((D, rows), bf16),
                pltpu.VMEM((D, rows), bf16),
                pltpu.VMEM((3, CH, D), f32),
                pltpu.VMEM((3, CH, D), f32),
            ],
        ),
        out_shape=[
            kept_out((rows, D), f32),
            kept_out((places, D // split, 2 * D), bf16),
            kept_out((rows, D), f32),
            jax.ShapeDtypeStruct((8, D), f32),
        ],
        compiler_params=params(28),
        cost_estimate=pl.CostEstimate(
            flops=30_000_000_000, bytes_accessed=18_000_000, transcendentals=0
        ),
        name="mlp_last",
    )(meta, place, scale, cot, *from_hbm(up_w, down_w, normed, middle), norm)


def head_rows(values, lane):
    zero = jnp.zeros_like(values)
    return [jnp.where(lane == h, values, zero) for h in range(2)]


def group_backward(keys, values, queries, grads, lse, delta):
    scores = mm(keys, queries, NT)
    grad_p = mm(values, grads, NT)
    probability = jnp.exp2(scores - lse)
    grad_s = (probability * (grad_p - delta)).astype(bf16)
    dv = mm(probability.astype(bf16), grads)
    dk = mm(grad_s, queries) * LN2
    both = jnp.concatenate([dk.astype(bf16), dv.astype(bf16)], axis=1)
    return both, mm(keys.T, grad_s)


def pick_heads(dq_t, index):
    begin = 2 * CH * index
    return jnp.concatenate(
        [dq_t[:HEAD_DIM, begin : begin + CH], dq_t[HEAD_DIM:, begin + CH : begin + 2 * CH]], axis=0
    )


def group_inputs(meta, q_i, lse_i, g_t, delta_t):
    lane = lax.broadcasted_iota(jnp.int32, (CH, PAIR), 1) // HEAD_DIM
    queries, grads, lse, delta = [], [], [], []
    for t in range(3):
        j = meta[9 + t]
        queries.append(head_rows(q_i[0, j], lane))
        grads.append(head_rows(g_t[t], lane))
        lse.append([lse_i[0, j, h : h + 1] for h in range(2)])
        delta.append([delta_t[t][h : h + 1] for h in range(2)])
    found = []
    for parts in ((0,), (1, 2)):
        found.append(
            tuple(
                jnp.concatenate([row for t in parts for row in rows[t]], axis=axis)
                for rows, axis in ((queries, 0), (grads, 0), (lse, 1), (delta, 1))
            )
        )
    return found


def key_range(ref, begin, count):
    return ref[0, pl.ds(begin, count)].reshape(count * CH, PAIR)


def attn_backward_far_kernel(groups, meta, *refs):
    w_in, grad_in, small, q_i, k_i, v_i, o_i, lse_i = refs[:8]
    d_left, d_own, d_right, dq_o, dkv_o, g_o, delta_o, small_o = refs[8:16]
    low, d_ext = refs[16:]
    step = pl.program_id(0)

    @pl.when(step == 0)
    def _():
        for t in range(3):
            rows = pl.ds(pl.multiple_of(meta[9 + t] * CH, CH), CH)
            low[t] = grad_in[rows].astype(bf16)
        d_ext[...] = jnp.zeros_like(d_ext)
        small_o[...] = small[...]

    def weight(begin, end):
        return w_in[:, 0, :, begin:end].reshape(D, end - begin)

    grad_low = mm(low[...].reshape(3 * CH, D), weight(3 * PAIR, D)).astype(bf16)
    g_t = [grad_low[t * CH : (t + 1) * CH] for t in range(3)]
    delta_t = []
    for t in range(3):
        g_o[0, t] = g_t[t]
        product = (g_t[t].astype(f32) * o_i[0, meta[9 + t]].astype(f32)).T
        rows = [
            jnp.sum(product[h * HEAD_DIM : (h + 1) * HEAD_DIM], axis=0, keepdims=True)
            for h in range(2)
        ]
        for h in range(2):
            delta_o[0, t, h : h + 1] = rows[h]
        delta_t.append(jnp.concatenate(rows, axis=0))
    one, two = group_inputs(meta, q_i, lse_i, g_t, delta_t)
    kv_w = weight(PAIR, 3 * PAIR)
    both, dq_t = group_backward(
        key_range(k_i, meta[12], 3), key_range(v_i, meta[12], 3), *one
    )
    dkv_o[0, 0:3] = both.reshape(3, CH, 2 * PAIR)
    d_ext[pl.ds(meta[16], 3)] += mm(both, kv_w, NT).reshape(3, CH, D)
    dq_o[0, 0] = pick_heads(dq_t, 0)
    both, dq_t = group_backward(
        key_range(k_i, meta[13], 2), key_range(v_i, meta[13], 2), *two
    )
    dkv_o[0, 3:5] = both.reshape(2, CH, 2 * PAIR)
    d_ext[pl.ds(meta[17], 2)] += mm(both, kv_w, NT).reshape(2, CH, D)
    dq_o[0, 1] = pick_heads(dq_t, 0)
    dq_o[0, 2] = pick_heads(dq_t, 1)

    @pl.when(step == groups - 1)
    def _():
        for j in range(3):
            rows = pl.ds(j * CH, CH)
            d_left[rows] = d_ext[j].astype(bf16)
            d_own[rows] = d_ext[3 + j]
            d_right[rows] = d_ext[6 + j].astype(bf16)


def attn_backward_near_kernel(groups, split, halves, meta, base, *refs):
    w_in, left, own, right, grad_in, q_i, k_i, v_i, o_i, lse_i = refs[:10]
    dq_i, dkv_i, g_i, delta_i, small = refs[10:15]
    w_grads = refs[15 : 15 + halves]
    d_own, small_o, ext_t, low_t, total, dq_all, w_all = refs[15 + halves :]
    step = pl.program_id(0)

    @pl.when(step == 0)
    def _():
        for index, part in enumerate((left, own, right)):
            for j in range(3):
                ext_t[3 * index + j] = part[pl.ds(j * CH, CH)].T
        for j in range(3):
            low_t[:, j * CH : (j + 1) * CH] = grad_in[pl.ds(j * CH, CH)].astype(bf16).T
        total[...] = jnp.zeros_like(total)
        small_o[...] = small[...]

    def weight(begin, end):
        return w_in[:, 0, :, begin:end].reshape(D, end - begin)

    def columns(begin, count):
        return jnp.concatenate([ext_t[begin + i] for i in range(count)], axis=1)

    g_t = [g_i[0, t] for t in range(3)]
    delta_t = [delta_i[0, t] for t in range(3)]
    one, two = group_inputs(meta, q_i, lse_i, g_t, delta_t)
    kv_w = weight(PAIR, 3 * PAIR)
    first, dq_one = group_backward(
        key_range(k_i, meta[14], 1), key_range(v_i, meta[14], 1), *one
    )
    second, dq_two = group_backward(
        key_range(k_i, meta[15], 2), key_range(v_i, meta[15], 2), *two
    )
    total[meta[18] - 3] += mm(first, kv_w, NT)
    total[pl.ds(meta[19] - 3, 2)] += mm(second, kv_w, NT).reshape(2, CH, D)
    for t, part in enumerate((pick_heads(dq_one, 0), pick_heads(dq_two, 0), pick_heads(dq_two, 1))):
        whole = ((dq_i[0, t] + part).T * (1.0 / math.sqrt(HEAD_DIM))).astype(bf16)
        j = meta[9 + t]
        dq_all[pl.ds(pl.multiple_of(j * CH, CH), CH)] = whole
        total[j] += mm(whole, weight(0, PAIR), NT)
    out_grad = mm(low_t[...], o_i[0].reshape(3 * CH, PAIR)).astype(bf16)
    w_all[:, 3 * PAIR :] = out_grad
    q_grad = mm(columns(3, 3), dq_all[...]).astype(bf16)
    w_all[:, :PAIR] = q_grad
    kv_grad = (
        mm(columns(meta[16], 3), dkv_i[0, 0:3].reshape(3 * CH, 2 * PAIR))
        + mm(columns(meta[17], 2), dkv_i[0, 3:5].reshape(2 * CH, 2 * PAIR))
        + mm(columns(meta[18], 1), first)
        + mm(columns(meta[19], 2), second)
    )
    w_all[:, PAIR : 3 * PAIR] = kv_grad.astype(bf16)
    high = D // split
    for apart in range(split):
        rows = pl.ds(pl.multiple_of((base[0] ^ apart) * high, high), high)
        w_grads[apart % halves][(apart // halves) * groups + step] = w_all[rows]

    @pl.when(step == groups - 1)
    def _():
        d_own[...] = total[...].reshape(3 * CH, D)


def attn_backward_far(weight, meta, grad_in, kept, groups, small, after=()):
    rows = grad_in.shape[0]
    const = lambda s, *_: (0, 0)
    pair = lambda s, *_: (s, 0, 0, 0)
    full = pl.BlockSpec((rows, D), const)
    three = pl.BlockSpec((1, 3, CH, PAIR), pair)
    eight = pl.BlockSpec((1, 2 * SLOT, CH, PAIR), pair)
    lines = pl.BlockSpec((1, 3, 8, CH), pair)
    tiny = pl.BlockSpec((8, D), const)
    return pl.pallas_call(
        after_operands(functools.partial(attn_backward_far_kernel, groups), 1, len(after)),
        grid_spec=pltpu.PrefetchScalarGridSpec(
            num_scalar_prefetch=1,
            grid=(groups,),
            in_specs=[hbm()] * len(after)
            + [weight_spec(*weight), full, tiny, three, eight, eight, three, lines],
            out_specs=[
                full,
                full,
                full,
                pl.BlockSpec((1, 3, PAIR, CH), pair),
                pl.BlockSpec((1, 5, CH, 2 * PAIR), pair),
                three,
                lines,
                tiny,
            ],
            scratch_shapes=[
                pltpu.VMEM((3, CH, D), bf16),
                pltpu.VMEM((9, CH, D), f32),
            ],
        ),
        out_shape=[
            jax.ShapeDtypeStruct((rows, D), bf16),
            jax.ShapeDtypeStruct((rows, D), f32),
            jax.ShapeDtypeStruct((rows, D), bf16),
            jax.ShapeDtypeStruct((groups, 3, PAIR, CH), f32),
            jax.ShapeDtypeStruct((groups, 5, CH, 2 * PAIR), bf16),
            jax.ShapeDtypeStruct((groups, 3, CH, PAIR), bf16),
            jax.ShapeDtypeStruct((groups, 3, 8, CH), f32),
            jax.ShapeDtypeStruct((8, D), f32),
        ],
        compiler_params=params(28),
        cost_estimate=pl.CostEstimate(
            flops=24_000_000_000, bytes_accessed=16_000_000, transcendentals=0
        ),
        name="attn_backward_far",
    )(meta, *from_hbm(*after, weight[0], grad_in), small, *from_hbm(*kept))


def attn_backward_near(weight, meta, base, ext, grad_in, kept, far, groups, split, small, halves):
    rows = grad_in.shape[0]
    const = lambda s, *_: (0, 0)
    pair = lambda s, *_: (s, 0, 0, 0)
    full = pl.BlockSpec((rows, D), const)
    three = pl.BlockSpec((1, 3, CH, PAIR), pair)
    eight = pl.BlockSpec((1, 2 * SLOT, CH, PAIR), pair)
    lines = pl.BlockSpec((1, 3, 8, CH), pair)
    tiny = pl.BlockSpec((8, D), const)
    places = split * groups
    return pl.pallas_call(
        functools.partial(attn_backward_near_kernel, groups, split, halves),
        grid_spec=pltpu.PrefetchScalarGridSpec(
            num_scalar_prefetch=2,
            grid=(groups,),
            in_specs=[weight_spec(*weight), full, full, full, full, three, eight, eight, three, lines]
            + [
                pl.BlockSpec((1, 3, PAIR, CH), pair),
                pl.BlockSpec((1, 5, CH, 2 * PAIR), pair),
                three,
                lines,
                tiny,
            ],
            out_specs=[pl.BlockSpec((places // halves, D // split, D), lambda s, *_: (0, 0, 0))]
            * halves
            + [full, tiny],
            scratch_shapes=[
                pltpu.VMEM((9, D, CH), bf16),
                pltpu.VMEM((D, rows), bf16),
                pltpu.VMEM((3, CH, D), f32),
                pltpu.VMEM((rows, PAIR), bf16),
                pltpu.VMEM((D, D), bf16),
            ],
        ),
        out_shape=[jax.ShapeDtypeStruct((places // halves, D // split, D), bf16)] * halves
        + [jax.ShapeDtypeStruct((rows, D), f32), jax.ShapeDtypeStruct((8, D), f32)],
        compiler_params=params(28),
        cost_estimate=pl.CostEstimate(
            flops=20_000_000_000, bytes_accessed=22_000_000, transcendentals=0
        ),
        name="attn_backward_near",
    )(meta, base, *from_hbm(weight[0], *ext), grad_in, *from_hbm(*kept), *far, small)


def entry_backward_kernel(
    grad_in, d_own, d_near, d_left, d_right, source, norm, ids, grad_out, small
):
    small[...] = jnp.zeros_like(small)
    for j in range(3):
        rows = pl.ds(j * CH, CH)
        arrived = d_own[rows] + d_near[rows] + d_left[rows].astype(f32) + d_right[rows].astype(f32)
        back, gain_grad, shift_grad = norm_backward(arrived, source[rows], norm[0:1])
        values = grad_in[rows] + back
        grad_out[rows] = values
        small[0:1] += gain_grad
        small[1:2] += shift_grad
        letter = lax.broadcasted_iota(jnp.int32, (32, CH), 0)
        chosen = (letter == ids[:, j * CH : (j + 1) * CH]).astype(bf16)
        high = values.astype(bf16)
        rest = values - high.astype(f32)
        middle = rest.astype(bf16)
        low = (rest - middle.astype(f32)).astype(bf16)
        small[8:40] += mm(chosen, high) + mm(chosen, middle) + mm(chosen, low)


def entry_backward(grad_in, d_own, d_near, d_left, d_right, source, norm, ids, after=()):
    rows = grad_in.shape[0]
    return pl.pallas_call(
        after_operands(entry_backward_kernel, 0, len(after)),
        in_specs=[hbm()] * len(after) + [vmem()] * 8,
        out_specs=[vmem()] * 2,
        out_shape=[
            kept_out((rows, D), f32),
            jax.ShapeDtypeStruct((40, D), f32),
        ],
        compiler_params=pltpu.CompilerParams(vmem_limit_bytes=40 * 1024 * 1024),
        cost_estimate=pl.CostEstimate(
            flops=100_000_000, bytes_accessed=9_000_000, transcendentals=0
        ),
        name="entry_backward",
    )(*after, grad_in, d_own, d_near, d_left, d_right, source, norm, ids)


def backward_plan(my_mp, row_start, first_seq, chunk_seq):
    lead = jnp.where(my_mp < 2, 0, 2)
    late_one = my_mp % 2 == 0
    late_two = my_mp < 2
    found = [lead, 1, 2 - lead]
    lead_seq = jnp.where(my_mp < 2, chunk_seq[0], chunk_seq[2])
    shifts = [
        (lead_seq, jnp.where(late_one, 1, 0)),
        (chunk_seq[1], jnp.where(late_two, 2, 0)),
        (lead_seq, jnp.where(late_one, 0, 3)),
        (chunk_seq[1], jnp.where(late_two, 0, 2)),
    ]
    found += [(seq - first_seq) * SLOT + shift for seq, shift in shifts]
    found += [3 + (seq * LEN - row_start) // CH + shift for seq, shift in shifts]
    return [jnp.asarray(entry) for entry in found]


def shards(
    token_ids,
    timesteps,
    importance,
    cotangent,
    qkv_weight,
    out_weight,
    up_weight,
    down_weight,
    norm_params,
    embed_table,
    qkv_first,
    qkv_second,
    out_first,
    out_second,
    up_first,
    up_second,
    down_first,
    down_second,
    norm_first,
    norm_second,
    embed_first,
    embed_second,
):
    dp, mp = lax.axis_size("dp"), lax.axis_size("mp")
    small = dp == 8 and mp == 4
    groups = mp
    split = dp if small else 1
    row_count = token_ids.shape[0]
    seq_here = timesteps.shape[0]
    high = D // dp
    my_mp = lax.axis_index("mp")
    my_dp = lax.axis_index("dp")
    row_start = my_mp * row_count

    first_seq = row_start // LEN
    last_seq = (row_start + row_count - 1) // LEN
    chunk_seq = [(row_start + CH * j) // LEN for j in range(3)]
    meta = jnp.stack(
        [
            3 + (first_seq * LEN - row_start) // CH,
            3 + (last_seq * LEN - row_start) // CH,
            last_seq - first_seq + 1,
        ]
        + [seq - first_seq for seq in chunk_seq]
        + chunk_seq
        + backward_plan(my_mp, row_start, first_seq, chunk_seq)
    ).astype(jnp.int32)
    in_order = jnp.arange(split * groups, dtype=jnp.int32)
    owner = block_owners(my_dp) if small else in_order
    base = jnp.where(small, my_dp, 0).astype(jnp.int32)[None]
    halves = 2 if small else 1

    attn_mine = []
    mlp_mine = []
    for layer in range(LAYERS):
        attn_mine.append(
            jnp.concatenate(
                [qkv_weight[layer].reshape(high, -1), out_weight[layer].T], axis=1
            ).astype(bf16)
        )
        mlp_mine.append(
            jnp.concatenate([up_weight[layer], down_weight[layer].T], axis=1).astype(bf16)
        )
    both_mine = jnp.concatenate([attn_mine[1], mlp_mine[1]], axis=1)
    if small:
        lines = row_count // D + (row_count % D > 0)
        ids_low = jnp.pad(token_ids.astype(bf16), (0, lines * D - row_count)).reshape(lines, D)
        first_mine = jnp.concatenate([attn_mine[0], ids_low], axis=0)
        first_z = gather_z(first_mine)
        attn_z = first_z[:, :high]
        ids_z = first_z[:, high:].reshape(4, lines * D)[:, :row_count].astype(jnp.int32)
        ids_left = ids_z[my_mp ^ jnp.maximum(my_mp - 1, 0)]
        ids_right = ids_z[my_mp ^ jnp.minimum(my_mp + 1, mp - 1)]
    else:
        ids_left, ids_right = shift_right(token_ids), shift_left(token_ids)
    ids_ext = jnp.concatenate([ids_left, token_ids, ids_right])
    seq_ext = (row_start - row_count + jnp.arange(3 * row_count, dtype=jnp.int32)) // LEN
    letters = (ids_ext[:, None] == jnp.arange(VOCAB, dtype=jnp.int32)[None, :]).astype(f32)
    member = (seq_ext[:, None] == jnp.arange(seq_here, dtype=jnp.int32)[None, :]).astype(f32)
    entry_ext = jnp.dot(letters, embed_table, precision=highest) + jnp.dot(
        member, time_features(timesteps), precision=highest
    )
    normed_ext = layer_norm(entry_ext, norm_params[0, 0], norm_params[0, 1]).astype(bf16)
    resid = entry_ext[row_count : 2 * row_count]
    ext = (
        normed_ext[:row_count],
        normed_ext[row_count : 2 * row_count],
        normed_ext[2 * row_count :],
    )

    if small:
        mlp_first, attn_z = tie(mlp_mine[0], attn_z)
        attn_sent = [flip(attn_z, bits) for bits in (8, 16, 24)]
        attn_sent, (ext, resid) = tie(attn_sent, (ext, resid))
        attn_xy = jnp.concatenate([attn_z] + list(attn_sent), axis=0)
        mlp_z = gather_z(mlp_first)
        mlp_z, attn_xy = tie(mlp_z, attn_xy)
        attn_w = [(attn_xy, flip(attn_xy, 4))]
        mlp_found = gather_dp(mlp_z)
        both_mine, mlp_z = tie(both_mine, mlp_z)
        both_sent = [flip(both_mine, bits) for bits in (1, 2, 3)]
    else:
        attn_w = [plain_gather(attn_mine[0])]
        mlp_found = plain_gather(mlp_mine[0])
        attn_w.append(plain_gather(both_mine))
        mlp_w = [((mlp_found, 0), (mlp_found, 1)), ((attn_w[1], 1), (attn_w[1], 2))]

    kept = []
    for layer in range(LAYERS):
        last = layer == LAYERS - 1
        outs, w_attn = attn_forward(
            attn_w[layer], meta, owner, *ext, resid, norm_params[layer], groups
        )
        middle, normed = outs[:2]
        if small and layer == 0:
            both_sent, normed = tie(both_sent, normed)
            both_z = jnp.stack([both_mine] + list(both_sent))
            last_found = gather_dp(both_z[:, :, D:])
            mlp_w = [((mlp_found, 0), (mlp_found, 1)), ((last_found, 0), (last_found, 1))]
            attn_z = both_z[:, :, :D]
            attn_sent = [flip(attn_z, bits) for bits in (8, 16, 24)]
            attn_z, normed = tie(attn_z, normed)
        w_mlp = mlp_w[layer]
        if layer + 1 < LAYERS:
            mlp_outs, w_mlp = mlp_forward(
                w_mlp, owner, normed, middle, norm_params[layer + 1], groups
            )
        kept.append((ext, resid, middle, normed, outs[2:], mlp_outs[1:3], (w_attn, 0), w_mlp))
        if layer + 1 < LAYERS:
            resid, following = mlp_outs[0], mlp_outs[3]
            if small:
                attn_sent, following = tie(attn_sent, following)
                attn_xy = jnp.concatenate([attn_z] + list(attn_sent), axis=0)
                attn_w.append((attn_xy, flip(attn_xy, 4)))
            ext = (shift_right(following), following, shift_left(following))

    norm_grads = [[None] * 4 for _ in range(LAYERS)]
    attn_grads = [None] * LAYERS
    mlp_grads = [None] * LAYERS
    after = ()
    for layer in reversed(range(LAYERS)):
        ext, source, middle, normed, attn_kept, (act, slope), w_attn, w_mlp = kept[layer]
        norm = norm_params[layer]
        if layer + 1 == LAYERS:
            activations, mlp_grad, grad_mid, n_grad = mlp_last(
                w_mlp, meta, in_order, importance, cotangent, normed, middle, norm, groups, split
            )
        else:
            mlp_grad, grad_mid, n_grad = mlp_backward(
                w_mlp,
                meta,
                in_order,
                begin,
                act,
                slope,
                normed,
                middle,
                norm,
                groups,
                split,
                after,
            )
        after = ()
        if small:
            if layer + 1 < LAYERS:
                attn_found, (mlp_grad, grad_mid) = tie(attn_found, (mlp_grad, grad_mid))
            mlp_rows = scatter_dp(mlp_grad, dp)
            if layer + 1 < LAYERS:
                attn_rows = add_four(attn_mine_rows, attn_found, False)
                above = jnp.concatenate([attn_rows, above], axis=2)
                above_mine, above_found = scatter_four(above, 1)
                after = (above,)
        d_left, d_own, d_right, *far, n_grad = attn_backward_far(
            w_attn, meta, grad_mid, attn_kept, groups, n_grad, after
        )
        if small and layer + 1 < LAYERS:
            above_found, (d_left, d_right) = tie(above_found, (d_left, d_right))
        from_right = shift_left(d_left)
        from_left = shift_right(d_right)
        *attn_grad, d_near, n_grad = attn_backward_near(
            w_attn, meta, base, ext, grad_mid, attn_kept, far, groups, split, n_grad, halves
        )
        (from_left, from_right), (attn_grad, d_near) = tie(
            (from_left, from_right), (attn_grad, d_near)
        )
        after = ()
        if not small:
            mlp_grads[layer] = plain_scatter(mlp_grad, dp)
            attn_grads[layer] = plain_scatter(attn_grad[0], dp)
        elif layer + 1 == LAYERS:
            attn_held = scatter_core(*attn_grad)
            attn_mine_rows, attn_found = scatter_four(attn_held, 8)
            above = mlp_rows
            after = (attn_held,)
        else:
            above_total = add_four(above_mine, above_found, True)
            attn_grads[1] = above_total[:, :D]
            mlp_grads[1] = above_total[:, D:]
        norm_grads[layer][2:] = [n_grad[2], n_grad[3]]
        if layer + 1 < LAYERS:
            norm_grads[layer + 1][:2] = [n_grad[0], n_grad[1]]
        begin = (grad_mid, d_own, d_near, from_left, from_right, source, norm_params[layer])
    input_grad, reduced = entry_backward(*begin, token_ids[None, :])
    norm_grads[0][:2] = [reduced[0], reduced[1]]
    stacked = jnp.concatenate(
        [jnp.stack([row for rows in norm_grads for row in rows]), reduced[8:40]], axis=0
    )
    if small:
        rows = D // dp
        rest = stacked.astype(bf16)
        rest = (rest.astype(f32) + flip(rest, 4).astype(f32)).astype(bf16)
        held = scatter_core(*attn_grad).reshape(16 * rows, D)
        sent = [
            flip(jnp.concatenate([held[4 * rows * i : 4 * rows * (i + 1)], rest], axis=0), 8 * i)
            for i in (1, 2, 3)
        ]
        mlp_own, mlp_sent = scatter_four(mlp_rows, 1)
        mlp_sent, sent = tie(mlp_sent, sent)
        mine = add_four(jnp.concatenate([held[: 4 * rows], rest], axis=0)[None], [p[None] for p in sent], True)
        held, rest = mine[: 4 * rows].astype(bf16), mine[4 * rows :].astype(bf16)
        sent = [
            flip(jnp.concatenate([held[rows * i : rows * (i + 1)], rest], axis=0), i)
            for i in (1, 2, 3)
        ]
        total = add_four(
            jnp.concatenate([held[:rows], rest], axis=0)[None], [p[None] for p in sent], True
        )
        attn_grads[0] = total[:rows]
        stacked = total[rows:]
        mlp_grads[0] = add_four(mlp_own, mlp_sent, True)
    else:
        stacked = lax.psum(stacked, ALL)
    norm_grad = stacked[: 4 * LAYERS].reshape(LAYERS, 4, D)
    embed_grad = stacked[4 * LAYERS : 4 * LAYERS + VOCAB]

    qkv_grad = jnp.stack([g[:, : 3 * PAIR].reshape(high, 3, PAIR) for g in attn_grads])
    out_grad = jnp.stack([g[:, 3 * PAIR :].T for g in attn_grads])
    up_grad = jnp.stack([g[:, :D] for g in mlp_grads])
    down_grad = jnp.stack([g[:, D:].T for g in mlp_grads])
    qkv_master, qkv_mean, qkv_square = adamw(
        qkv_weight, qkv_first, qkv_second, qkv_grad, 2.0 / math.sqrt(D), decay_matrix
    )
    out_master, out_mean, out_square = adamw(
        out_weight, out_first, out_second, out_grad, 2.0 / math.sqrt(D), decay_matrix
    )
    up_master, up_mean, up_square = adamw(
        up_weight, up_first, up_second, up_grad, 2.0 / math.sqrt(D), decay_matrix
    )
    down_master, down_mean, down_square = adamw(
        down_weight, down_first, down_second, down_grad, 2.0 / math.sqrt(FF), decay_matrix
    )
    norm_master, norm_mean, norm_square = adamw(
        norm_params, norm_first, norm_second, norm_grad, vector_rate, 0.0
    )
    embed_master, embed_mean, embed_square = adamw(
        embed_table, embed_first, embed_second, embed_grad, embed_rate, 0.0
    )
    return (
        activations,
        input_grad,
        qkv_master,
        qkv_mean,
        qkv_square,
        qkv_master.astype(bf16),
        out_master,
        out_mean,
        out_square,
        out_master.astype(bf16),
        up_master,
        up_mean,
        up_square,
        up_master.astype(bf16),
        down_master,
        down_mean,
        down_square,
        down_master.astype(bf16),
        norm_master,
        norm_mean,
        norm_square,
        embed_master,
        embed_mean,
        embed_square,
    )


def solution(mesh):
    rows = P(("dp", "mp"), None)
    qkv = P(None, "dp", None, "mp")
    wide = P(None, "mp", "dp")
    tall = P(None, "dp", "mp")
    same = P()
    return jax.shard_map(
        shards,
        mesh=mesh,
        in_specs=(P(("dp", "mp")), P("dp"), P("dp"), rows, qkv, wide, tall, wide, same, same)
        + (qkv, qkv, wide, wide, tall, tall, wide, wide, same, same, same, same),
        out_specs=(rows, rows)
        + (qkv,) * 4
        + (wide,) * 4
        + (tall,) * 4
        + (wide,) * 4
        + (same,) * 6,
        check_vma=False,
    )
```

```python
import functools
import math

import jax
import jax.numpy as jnp
from jax import lax
from jax.experimental import pallas as pl
from jax.experimental.pallas import tpu as pltpu
from jax.sharding import PartitionSpec as P

HEAD_DIM = 64
FF = 2048
VOCAB = 27
LAYERS = 2
LEN = 1024
STEP = 10
D = 512
PAIR = 2 * HEAD_DIM
CH = 256
SLOT = LEN // CH

bf16 = jnp.bfloat16
f32 = jnp.float32
highest = lax.Precision.HIGHEST
eps_norm = 1e-05
beta_one = 0.5
beta_two = 0.5
adam_eps = 1e-08
decay_matrix = 0.01
vector_rate = 0.6
embed_rate = 1.0
LOG2E = math.log2(math.e)
LN2 = math.log(2.0)
ALL = ("dp", "mp")

NN = (((1,), (0,)), ((), ()))
NT = (((1,), (1,)), ((), ()))


def mm(left, right, dims=NN):
    return lax.dot_general(left, right, dims, preferred_element_type=f32)


def vmem():
    return pl.BlockSpec(memory_space=pltpu.VMEM)


def smem():
    return pl.BlockSpec(memory_space=pltpu.SMEM)


def hbm():
    return pl.BlockSpec(memory_space=pl.ANY)


def after_operands(kernel, prefetched, count):
    def call(*refs):
        return kernel(*refs[:prefetched], *refs[prefetched + count :])

    return call


def kept_out(shape, dtype):
    return pltpu.HBM(shape, dtype)


def from_hbm(*arrays):
    return tuple(pltpu.with_memory_space_constraint(x, pltpu.HBM) for x in arrays)


def params(mib):
    return pltpu.CompilerParams(
        dimension_semantics=("arbitrary",), vmem_limit_bytes=mib * 1024 * 1024
    )


def norm_parts(values):
    row_mean = jnp.mean(values, axis=-1, keepdims=True)
    centered = values - row_mean
    variance = jnp.mean(centered * centered, axis=-1, keepdims=True)
    inverse = lax.rsqrt(variance + eps_norm)
    return centered * inverse, inverse


def layer_norm(values, gain_vec, shift_vec):
    scaled, _ = norm_parts(values)
    return scaled * gain_vec + shift_vec


def norm_backward(grad_out, values, gain_vec):
    scaled, inverse = norm_parts(values)
    weighted = grad_out * gain_vec
    mean_plain = jnp.mean(weighted, axis=-1, keepdims=True)
    mean_scaled = jnp.mean(weighted * scaled, axis=-1, keepdims=True)
    grad_in = (weighted - mean_plain - scaled * mean_scaled) * inverse
    gain_grad = jnp.sum(grad_out * scaled, axis=0, keepdims=True)
    shift_grad = jnp.sum(grad_out, axis=0, keepdims=True)
    return grad_in, gain_grad, shift_grad


def gelu_pair(hidden):
    square = hidden * hidden
    bell = jnp.exp2(square * (-0.5 * LOG2E))
    phi = 0.5 + 0.5 * lax.erf(hidden * (1.0 / math.sqrt(2.0)))
    return hidden * phi, phi + hidden * bell * (1.0 / math.sqrt(2.0 * math.pi))


def time_features(step_values):
    half_width = D // 2
    frequency = jnp.exp(-math.log(10000.0) * jnp.arange(half_width, dtype=f32) / half_width)
    angles = step_values.astype(f32)[:, None] * frequency[None, :]
    return jnp.concatenate([jnp.sin(angles), jnp.cos(angles)], axis=1)


def adamw(weight, mean_old, square_old, gradient, step_rate, decay_weight):
    mean_new = beta_one * mean_old + (1.0 - beta_one) * gradient
    square_new = beta_two * square_old + (1.0 - beta_two) * gradient * gradient
    fix_one = 1.0 - beta_one**STEP
    fix_two = 1.0 - beta_two**STEP
    direction = mean_new / fix_one / (jnp.sqrt(square_new / fix_two) + adam_eps)
    return (weight - step_rate * (direction + decay_weight * weight), mean_new, square_new)


def permute_all(values, target):
    count = lax.axis_size("dp") * lax.axis_size("mp")
    return lax.ppermute(values, ALL, [(i, target(i)) for i in range(count)])


def block_owners(my_dp):
    index = jnp.arange(32, dtype=jnp.int32)
    return my_dp ^ ((((index >> 2) & 3) << 1) | (index >> 4))


def tie(values, after):
    return lax.optimization_barrier((values, after))


def flip(values, bits):
    return permute_all(values, lambda i: i ^ bits)


def gather_z(values):
    return jnp.stack([values] + [flip(values, bits) for bits in (1, 2, 3)])


def scatter_core(own, other):
    return (own.astype(f32) + flip(other, 4).astype(f32)).astype(bf16)


def scatter_four(blocks, unit):
    size = blocks.shape[0] // 4
    found = [flip(blocks[i * size : (i + 1) * size], i * unit) for i in (1, 2, 3)]
    return blocks[:size], found


def add_four(own, found, last):
    one, two, three = [part.astype(f32) for part in found]
    total = (own.astype(f32) + one) + (two + three)
    return total[0] if last else total.astype(bf16)


def gather_dp(held):
    return lax.all_gather(held, "dp", axis=0, tiled=False)


def scatter_dp(blocks, dp):
    places, rows, columns = blocks.shape
    flat = blocks.reshape(places * rows, columns)
    return lax.psum_scatter(flat, "dp", scatter_dimension=0, tiled=True).reshape(
        places // dp, rows, columns
    )


def plain_gather(values):
    dp, mp = lax.axis_size("dp"), lax.axis_size("mp")
    rows, columns = values.shape
    found = lax.all_gather(values, ALL, axis=0, tiled=True).reshape(dp, mp, rows, columns)
    if rows % 16 == 0:
        return found
    return jnp.swapaxes(found, 0, 1).reshape(1, mp, dp * rows, columns)


def plain_scatter(blocks, dp):
    places, rows, columns = blocks.shape
    mp = lax.axis_size("mp")
    if places != dp * mp:
        blocks = jnp.swapaxes(blocks.reshape(mp, dp, D // dp, columns), 0, 1)
    flat = blocks.reshape(dp * mp * (D // dp), columns)
    return lax.psum_scatter(flat, ALL, scatter_dimension=0, tiled=True).astype(f32)


def shift_right(values):
    count = lax.axis_size("mp")
    return lax.ppermute(values, "mp", [(i, i + 1) for i in range(count - 1)])


def shift_left(values):
    count = lax.axis_size("mp")
    return lax.ppermute(values, "mp", [(i + 1, i) for i in range(count - 1)])


def fetch_blocks(table, near, far, targets, sems):
    copies = []
    for place in range(32):
        owner = table[place]
        source = near.at[place] if place < 16 else far.at[place - 16]
        for index, (target, begin, width) in enumerate(targets):
            copies.append(
                pltpu.make_async_copy(
                    source.at[:, pl.ds(begin, width)],
                    target.at[owner, place % 4],
                    sems.at[place, index],
                )
            )
    for copy in copies:
        copy.start()
    return copies


def attn_forward_kernel(gathered, groups, meta, table, *refs):
    if gathered:
        near, far, left, own, right, resid, norm = refs[:7]
        middle, normed, q_o, k_o, v_o, o_o, lse_o, w_o = refs[7:15]
        ext, total, sems = refs[15:]
    else:
        w_in, left, own, right, resid, norm = refs[:6]
        middle, normed, q_o, k_o, v_o, o_o, lse_o = refs[6:13]
        ext, total = refs[13:]
    step = pl.program_id(0)

    @pl.when(step == 0)
    def _():
        if gathered:
            copies = fetch_blocks(table, near, far, [(w_o, 0, D)], sems)
        for index, part in enumerate((left, own, right)):
            ext[pl.ds(3 * index, 3)] = part[...].reshape(3, CH, D)
        total[...] = jnp.zeros_like(total)
        if gathered:
            for copy in copies:
                copy.wait()

    def weight(begin, end):
        found = w_o[:, step, :, begin:end] if gathered else w_in[:, 0, :, begin:end]
        return found.reshape(D, end - begin)

    for j in range(3):
        q_o[0, j] = (mm(ext[3 + j], weight(0, PAIR)) * (LOG2E / math.sqrt(HEAD_DIM))).astype(bf16)

    def project(slot, carry):
        begin = meta[slot]
        kv_w = weight(PAIR, 3 * PAIR)
        for i in range(SLOT):
            both = mm(ext[begin + i], kv_w).astype(bf16)
            k_o[0, slot * SLOT + i] = both[:, :PAIR]
            v_o[0, slot * SLOT + i] = both[:, PAIR:]
        return carry

    lax.fori_loop(0, meta[2], project, 0)
    lane = lax.broadcasted_iota(jnp.int32, (CH, PAIR), 1) // HEAD_DIM
    lane_all = lax.broadcasted_iota(jnp.int32, (LEN, PAIR), 1) // HEAD_DIM

    for j in range(3):
        slot = meta[3 + j]
        query = q_o[0, j]
        keys = k_o[0, pl.ds(slot * SLOT, SLOT)].reshape(LEN, PAIR)
        values = v_o[0, pl.ds(slot * SLOT, SLOT)].reshape(LEN, PAIR)
        zero = jnp.zeros_like(query)
        both = jnp.concatenate([jnp.where(lane == h, query, zero) for h in range(2)], axis=0)
        scores = mm(both, keys, NT)
        top = jnp.max(scores, axis=1, keepdims=True)
        weights = jnp.exp2(scores - top).astype(bf16)
        parts = []
        for h in range(2):
            value_h = jnp.where(lane_all == h, values, jnp.ones_like(values))
            mixed = mm(weights[h * CH : (h + 1) * CH], value_h)
            sums = pltpu.roll(mixed, HEAD_DIM, 1)
            parts.append(mixed / sums)
            spread = top[h * CH : (h + 1) * CH] + jnp.log2(sums)
            lse_o[0, j, h : h + 1] = spread.T[h * HEAD_DIM : h * HEAD_DIM + 1]
        out = jnp.where(lane == 0, parts[0], parts[1]).astype(bf16)
        o_o[0, j] = out
        total[j] += mm(out, weight(3 * PAIR, D), NT)

    @pl.when(step == groups - 1)
    def _():
        for j in range(3):
            rows = pl.ds(j * CH, CH)
            values = resid[rows] + total[j]
            middle[rows] = values
            normed[rows] = layer_norm(values, norm[2:3], norm[3:4]).astype(bf16)


def attn_forward(weights, meta, table, left, own, right, resid, norm, groups):
    rows = own.shape[0]
    gathered = isinstance(weights, tuple)
    const = lambda s, *_: (0, 0)
    pair = lambda s, *_: (s, 0, 0, 0)
    full = pl.BlockSpec((rows, D), const)
    out_shape = [
        kept_out((rows, D), f32),
        kept_out((rows, D), bf16),
        kept_out((groups, 3, CH, PAIR), bf16),
        kept_out((groups, 2 * SLOT, CH, PAIR), bf16),
        kept_out((groups, 2 * SLOT, CH, PAIR), bf16),
        kept_out((groups, 3, CH, PAIR), bf16),
        kept_out((groups, 3, 8, CH), f32),
    ]
    out_specs = [
        full,
        full,
        pl.BlockSpec((1, 3, CH, PAIR), pair),
        pl.BlockSpec((1, 2 * SLOT, CH, PAIR), pair),
        pl.BlockSpec((1, 2 * SLOT, CH, PAIR), pair),
        pl.BlockSpec((1, 3, CH, PAIR), pair),
        pl.BlockSpec((1, 3, 8, CH), pair),
    ]
    scratch = [
        pltpu.VMEM((9, CH, D), bf16),
        pltpu.VMEM((3, CH, D), f32),
    ]
    if gathered:
        w_args = list(weights)
        w_specs = [hbm(), hbm()]
        out_shape.append(kept_out((8, 4, 64, D), bf16))
        out_specs.append(pl.BlockSpec((8, 4, 64, D), pair_zero))
        scratch.append(pltpu.SemaphoreType.DMA((32, 1)))
    else:
        w_args = [weights]
        split, _, high, _ = weights.shape
        w_specs = [pl.BlockSpec((split, 1, high, D), lambda s, *_: (0, s, 0, 0))]
    outs = pl.pallas_call(
        functools.partial(attn_forward_kernel, gathered, groups),
        grid_spec=pltpu.PrefetchScalarGridSpec(
            num_scalar_prefetch=2,
            grid=(groups,),
            in_specs=w_specs
            + [full, full, full, full, pl.BlockSpec((4, D), const)],
            out_specs=out_specs,
            scratch_shapes=scratch,
        ),
        out_shape=out_shape,
        compiler_params=params(28),
        cost_estimate=pl.CostEstimate(
            flops=29_000_000_000, bytes_accessed=14_000_000, transcendentals=0
        ),
        name="attn_forward",
    )(meta, table, *from_hbm(*w_args, left, own, right, resid), norm)
    if gathered:
        return outs[:7], outs[7]
    return outs, weights


def pair_zero(s, *_):
    return (0, 0, 0, 0)


def mlp_forward_kernel(gathered, groups, table, *refs):
    if gathered:
        near, far, normed, middle, norm = refs[:5]
        refs = refs[5:]
    else:
        up_in, down_in, normed, middle, norm = refs[:5]
        refs = refs[5:]
    after, act_o, slope_o, next_o = refs[:4]
    refs = refs[4:]
    if gathered:
        up_o, down_o, total, sems = refs
    else:
        (total,) = refs
    step = pl.program_id(0)

    @pl.when(step == 0)
    def _():
        if gathered:
            copies = fetch_blocks(table, near, far, [(up_o, 0, D), (down_o, D, D)], sems)
        total[...] = jnp.zeros_like(total)
        if gathered:
            for copy in copies:
                copy.wait()

    if gathered:
        up_w = up_o[:, step].reshape(D, D)
        down_w = down_o[:, step].reshape(D, D)
    else:
        up_w = up_in[:, 0].reshape(D, D)
        down_w = down_in[:, 0].reshape(D, D)
    for j in range(3):
        rows = pl.ds(j * CH, CH)
        hidden = mm(normed[rows], up_w)
        act, slope = gelu_pair(hidden)
        act = act.astype(bf16)
        act_o[0, rows] = act
        slope_o[0, rows] = slope.astype(bf16)
        total[j] += mm(act, down_w, NT)

    @pl.when(step == groups - 1)
    def _():
        for j in range(3):
            rows = pl.ds(j * CH, CH)
            values = middle[rows] + total[j]
            after[rows] = values
            next_o[rows] = layer_norm(values, norm[0:1], norm[1:2]).astype(bf16)


def mlp_forward(weights, table, normed, middle, norm, groups):
    rows = normed.shape[0]
    gathered = not isinstance(weights[0], tuple)
    const = lambda s, *_: (0, 0)
    full = pl.BlockSpec((rows, D), const)
    part = pl.BlockSpec((1, rows, D), lambda s, *_: (s, 0, 0))
    out_shape = [
        kept_out((rows, D), f32),
        kept_out((groups, rows, D), bf16),
        kept_out((groups, rows, D), bf16),
        jax.ShapeDtypeStruct((rows, D), bf16),
    ]
    out_specs = [full, part, part, full]
    scratch = [pltpu.VMEM((3, CH, D), f32)]
    if gathered:
        w_args = list(weights)
        w_specs = [hbm(), hbm()]
        for _ in range(2):
            out_shape.append(jax.ShapeDtypeStruct((8, 4, 64, D), bf16))
            out_specs.append(pl.BlockSpec((8, 4, 64, D), pair_zero))
        scratch.append(pltpu.SemaphoreType.DMA((32, 2)))
    else:
        (up_w, up_at), (down_w, down_at) = weights
        w_args = [up_w, down_w]
        w_specs = [weight_spec(up_w, up_at), weight_spec(down_w, down_at)]
    outs = pl.pallas_call(
        functools.partial(mlp_forward_kernel, gathered, groups),
        grid_spec=pltpu.PrefetchScalarGridSpec(
            num_scalar_prefetch=1,
            grid=(groups,),
            in_specs=w_specs + [full, full, pl.BlockSpec((4, D), const)],
            out_specs=out_specs,
            scratch_shapes=scratch,
        ),
        out_shape=out_shape,
        compiler_params=params(28),
        cost_estimate=pl.CostEstimate(
            flops=15_000_000_000, bytes_accessed=18_000_000, transcendentals=0
        ),
        name="mlp_forward",
    )(table, *from_hbm(*w_args, normed, middle), norm)
    if gathered:
        return outs[:-2], ((outs[-2], 0), (outs[-1], 0))
    return outs, weights


def weight_spec(weight, at):
    split, _, high, _ = weight.shape
    return pl.BlockSpec((split, 1, high, D), lambda s, *_: (0, s, 0, at))


def put_blocks(out, table, step, groups, split, begin, values):
    high = D // split
    width = values.shape[1]
    for d in range(split):
        place = table[d * groups + step]
        out[place, :, begin : begin + width] = values[d * high : (d + 1) * high]


def mlp_backward_kernel(groups, split, meta, place, *refs):
    grad_in, d_own, d_near, d_left, d_right, source, norm_up = refs[:7]
    refs = refs[7:]
    up_in, down_in, act, slope, normed, middle, norm = refs[:7]
    refs = refs[7:]
    w_grad, grad_out, n_grad = refs[:3]
    refs = refs[3:]
    grad, low, low_t, norm_t, total = refs
    step = pl.program_id(0)

    @pl.when(step == 0)
    def _():
        n_grad[...] = jnp.zeros_like(n_grad)
        for j in range(3):
            rows = pl.ds(j * CH, CH)
            arrived = d_own[rows] + d_near[rows] + d_left[rows].astype(f32)
            arrived += d_right[rows].astype(f32)
            back, gain_grad, shift_grad = norm_backward(arrived, source[rows], norm_up[0:1])
            values = grad_in[rows] + back
            n_grad[0:1] += gain_grad
            n_grad[1:2] += shift_grad
            grad[j] = values
            rounded = values.astype(bf16)
            low[rows] = rounded
            low_t[:, j * CH : (j + 1) * CH] = rounded.T
            norm_t[:, j * CH : (j + 1) * CH] = normed[rows].T
        total[...] = jnp.zeros_like(total)

    up_w = up_in[:, 0].reshape(D, D)
    down_w = down_in[:, 0].reshape(D, D)
    down_grad = mm(low_t[...], act[0]).astype(bf16)
    put_blocks(w_grad, place, step, groups, split, D, down_grad)
    pieces = []
    for j in range(3):
        rows = pl.ds(j * CH, CH)
        piece = (mm(low[rows], down_w) * slope[0, rows].astype(f32)).astype(bf16)
        pieces.append(piece)
        total[j] += mm(piece, up_w, NT)
    up_grad = mm(norm_t[...], jnp.concatenate(pieces, axis=0)).astype(bf16)
    put_blocks(w_grad, place, step, groups, split, 0, up_grad)

    @pl.when(step == groups - 1)
    def _():
        for j in range(3):
            rows = pl.ds(j * CH, CH)
            back, gain_grad, shift_grad = norm_backward(total[j], middle[rows], norm[2:3])
            grad_out[rows] = grad[j] + back
            n_grad[2:3] += gain_grad
            n_grad[3:4] += shift_grad


def mlp_backward(
    weights, meta, place, begin, act, slope, normed, middle, norm, groups, split, after=()
):
    rows = normed.shape[0]
    const = lambda s, *_: (0, 0)
    full = pl.BlockSpec((rows, D), const)
    part = pl.BlockSpec((1, rows, D), lambda s, *_: (s, 0, 0))
    vec = pl.BlockSpec((4, D), const)
    (up_w, up_at), (down_w, down_at) = weights
    begin_specs = [full] * 6 + [vec]
    places = split * groups
    return pl.pallas_call(
        after_operands(
            functools.partial(mlp_backward_kernel, groups, split), 2, len(after)
        ),
        grid_spec=pltpu.PrefetchScalarGridSpec(
            num_scalar_prefetch=2,
            grid=(groups,),
            in_specs=[hbm()] * len(after)
            + begin_specs
            + [weight_spec(up_w, up_at), weight_spec(down_w, down_at)]
            + [part, part, full, full, vec],
            out_specs=[
                pl.BlockSpec((places, D // split, 2 * D), lambda s, *_: (0, 0, 0)),
                full,
                pl.BlockSpec((8, D), const),
            ],
            scratch_shapes=[
                pltpu.VMEM((3, CH, D), f32),
                pltpu.VMEM((rows, D), bf16),
                pltpu.VMEM((D, rows), bf16),
                pltpu.VMEM((D, rows), bf16),
                pltpu.VMEM((3, CH, D), f32),
            ],
        ),
        out_shape=[
            kept_out((places, D // split, 2 * D), bf16),
            kept_out((rows, D), f32),
            jax.ShapeDtypeStruct((8, D), f32),
        ],
        compiler_params=params(28),
        cost_estimate=pl.CostEstimate(
            flops=20_000_000_000, bytes_accessed=20_000_000, transcendentals=0
        ),
        name="mlp_backward",
    )(meta, place, *from_hbm(*after), *begin, *from_hbm(up_w, down_w, act, slope), normed, middle, norm)


def mlp_last_kernel(groups, split, meta, place, *refs):
    scale, cot, up_in, down_in, normed, middle, norm = refs[:7]
    after, w_grad, grad_out, n_grad = refs[7:11]
    low, low_t, norm_t, total, total_grad = refs[11:]
    step = pl.program_id(0)

    def start_grad(j):
        return cot[pl.ds(j * CH, CH)].astype(f32) * scale[meta[6 + j]]

    @pl.when(step == 0)
    def _():
        n_grad[...] = jnp.zeros_like(n_grad)
        for j in range(3):
            rows = pl.ds(j * CH, CH)
            rounded = start_grad(j).astype(bf16)
            low[rows] = rounded
            low_t[:, j * CH : (j + 1) * CH] = rounded.T
            norm_t[:, j * CH : (j + 1) * CH] = normed[rows].T
        total[...] = jnp.zeros_like(total)
        total_grad[...] = jnp.zeros_like(total_grad)

    up_w = up_in[:, 0].reshape(D, D)
    down_w = down_in[:, 0].reshape(D, D)
    acts, pieces = [], []
    for j in range(3):
        rows = pl.ds(j * CH, CH)
        act, slope = gelu_pair(mm(normed[rows], up_w))
        act = act.astype(bf16)
        acts.append(act)
        total[j] += mm(act, down_w, NT)
        piece = (mm(low[rows], down_w) * slope).astype(bf16)
        pieces.append(piece)
        total_grad[j] += mm(piece, up_w, NT)
    down_grad = mm(low_t[...], jnp.concatenate(acts, axis=0)).astype(bf16)
    put_blocks(w_grad, place, step, groups, split, D, down_grad)
    up_grad = mm(norm_t[...], jnp.concatenate(pieces, axis=0)).astype(bf16)
    put_blocks(w_grad, place, step, groups, split, 0, up_grad)

    @pl.when(step == groups - 1)
    def _():
        for j in range(3):
            rows = pl.ds(j * CH, CH)
            values = middle[rows]
            after[rows] = values + total[j]
            back, gain_grad, shift_grad = norm_backward(total_grad[j], values, norm[2:3])
            grad_out[rows] = start_grad(j) + back
            n_grad[2:3] += gain_grad
            n_grad[3:4] += shift_grad


def mlp_last(weights, meta, place, scale, cot, normed, middle, norm, groups, split):
    rows = normed.shape[0]
    const = lambda s, *_: (0, 0)
    full = pl.BlockSpec((rows, D), const)
    (up_w, up_at), (down_w, down_at) = weights
    places = split * groups
    return pl.pallas_call(
        functools.partial(mlp_last_kernel, groups, split),
        grid_spec=pltpu.PrefetchScalarGridSpec(
            num_scalar_prefetch=2,
            grid=(groups,),
            in_specs=[smem(), full]
            + [weight_spec(up_w, up_at), weight_spec(down_w, down_at)]
            + [full, full, pl.BlockSpec((4, D), const)],
            out_specs=[
                full,
                pl.BlockSpec((places, D // split, 2 * D), lambda s, *_: (0, 0, 0)),
                full,
                pl.BlockSpec((8, D), const),
            ],
            scratch_shapes=[
                pltpu.VMEM((rows, D), bf16),
                pltpu.VMEM((D, rows), bf16),
                pltpu.VMEM((D, rows), bf16),
                pltpu.VMEM((3, CH, D), f32),
                pltpu.VMEM((3, CH, D), f32),
            ],
        ),
        out_shape=[
            kept_out((rows, D), f32),
            kept_out((places, D // split, 2 * D), bf16),
            kept_out((rows, D), f32),
            jax.ShapeDtypeStruct((8, D), f32),
        ],
        compiler_params=params(28),
        cost_estimate=pl.CostEstimate(
            flops=30_000_000_000, bytes_accessed=18_000_000, transcendentals=0
        ),
        name="mlp_last",
    )(meta, place, scale, cot, *from_hbm(up_w, down_w, normed, middle), norm)


def head_rows(values, lane):
    zero = jnp.zeros_like(values)
    return [jnp.where(lane == h, values, zero) for h in range(2)]


def group_backward(keys, values, queries, grads, lse, delta):
    scores = mm(keys, queries, NT)
    grad_p = mm(values, grads, NT)
    probability = jnp.exp2(scores - lse)
    grad_s = (probability * (grad_p - delta)).astype(bf16)
    dv = mm(probability.astype(bf16), grads)
    dk = mm(grad_s, queries) * LN2
    both = jnp.concatenate([dk.astype(bf16), dv.astype(bf16)], axis=1)
    return both, mm(keys.T, grad_s)


def pick_heads(dq_t, index):
    begin = 2 * CH * index
    return jnp.concatenate(
        [dq_t[:HEAD_DIM, begin : begin + CH], dq_t[HEAD_DIM:, begin + CH : begin + 2 * CH]], axis=0
    )


def group_inputs(meta, q_i, lse_i, g_t, delta_t):
    lane = lax.broadcasted_iota(jnp.int32, (CH, PAIR), 1) // HEAD_DIM
    queries, grads, lse, delta = [], [], [], []
    for t in range(3):
        j = meta[9 + t]
        queries.append(head_rows(q_i[0, j], lane))
        grads.append(head_rows(g_t[t], lane))
        lse.append([lse_i[0, j, h : h + 1] for h in range(2)])
        delta.append([delta_t[t][h : h + 1] for h in range(2)])
    found = []
    for parts in ((0,), (1, 2)):
        found.append(
            tuple(
                jnp.concatenate([row for t in parts for row in rows[t]], axis=axis)
                for rows, axis in ((queries, 0), (grads, 0), (lse, 1), (delta, 1))
            )
        )
    return found


def key_range(ref, begin, count):
    return ref[0, pl.ds(begin, count)].reshape(count * CH, PAIR)


def attn_backward_far_kernel(groups, meta, *refs):
    w_in, grad_in, small, q_i, k_i, v_i, o_i, lse_i = refs[:8]
    d_left, d_own, d_right, dq_o, dkv_o, g_o, delta_o, small_o = refs[8:16]
    low, d_ext = refs[16:]
    step = pl.program_id(0)

    @pl.when(step == 0)
    def _():
        for t in range(3):
            rows = pl.ds(pl.multiple_of(meta[9 + t] * CH, CH), CH)
            low[t] = grad_in[rows].astype(bf16)
        d_ext[...] = jnp.zeros_like(d_ext)
        small_o[...] = small[...]

    def weight(begin, end):
        return w_in[:, 0, :, begin:end].reshape(D, end - begin)

    grad_low = mm(low[...].reshape(3 * CH, D), weight(3 * PAIR, D)).astype(bf16)
    g_t = [grad_low[t * CH : (t + 1) * CH] for t in range(3)]
    delta_t = []
    for t in range(3):
        g_o[0, t] = g_t[t]
        product = (g_t[t].astype(f32) * o_i[0, meta[9 + t]].astype(f32)).T
        rows = [
            jnp.sum(product[h * HEAD_DIM : (h + 1) * HEAD_DIM], axis=0, keepdims=True)
            for h in range(2)
        ]
        for h in range(2):
            delta_o[0, t, h : h + 1] = rows[h]
        delta_t.append(jnp.concatenate(rows, axis=0))
    one, two = group_inputs(meta, q_i, lse_i, g_t, delta_t)
    kv_w = weight(PAIR, 3 * PAIR)
    both, dq_t = group_backward(
        key_range(k_i, meta[12], 3), key_range(v_i, meta[12], 3), *one
    )
    dkv_o[0, 0:3] = both.reshape(3, CH, 2 * PAIR)
    d_ext[pl.ds(meta[16], 3)] += mm(both, kv_w, NT).reshape(3, CH, D)
    dq_o[0, 0] = pick_heads(dq_t, 0)
    both, dq_t = group_backward(
        key_range(k_i, meta[13], 2), key_range(v_i, meta[13], 2), *two
    )
    dkv_o[0, 3:5] = both.reshape(2, CH, 2 * PAIR)
    d_ext[pl.ds(meta[17], 2)] += mm(both, kv_w, NT).reshape(2, CH, D)
    dq_o[0, 1] = pick_heads(dq_t, 0)
    dq_o[0, 2] = pick_heads(dq_t, 1)

    @pl.when(step == groups - 1)
    def _():
        for j in range(3):
            rows = pl.ds(j * CH, CH)
            d_left[rows] = d_ext[j].astype(bf16)
            d_own[rows] = d_ext[3 + j]
            d_right[rows] = d_ext[6 + j].astype(bf16)


def attn_backward_near_kernel(groups, split, halves, meta, base, *refs):
    w_in, left, own, right, grad_in, q_i, k_i, v_i, o_i, lse_i = refs[:10]
    dq_i, dkv_i, g_i, delta_i, small = refs[10:15]
    w_grads = refs[15 : 15 + halves]
    d_own, small_o, ext_t, low_t, total, dq_all, w_all = refs[15 + halves :]
    step = pl.program_id(0)

    @pl.when(step == 0)
    def _():
        for index, part in enumerate((left, own, right)):
            for j in range(3):
                ext_t[3 * index + j] = part[pl.ds(j * CH, CH)].T
        for j in range(3):
            low_t[:, j * CH : (j + 1) * CH] = grad_in[pl.ds(j * CH, CH)].astype(bf16).T
        total[...] = jnp.zeros_like(total)
        small_o[...] = small[...]

    def weight(begin, end):
        return w_in[:, 0, :, begin:end].reshape(D, end - begin)

    def columns(begin, count):
        return jnp.concatenate([ext_t[begin + i] for i in range(count)], axis=1)

    g_t = [g_i[0, t] for t in range(3)]
    delta_t = [delta_i[0, t] for t in range(3)]
    one, two = group_inputs(meta, q_i, lse_i, g_t, delta_t)
    kv_w = weight(PAIR, 3 * PAIR)
    first, dq_one = group_backward(
        key_range(k_i, meta[14], 1), key_range(v_i, meta[14], 1), *one
    )
    second, dq_two = group_backward(
        key_range(k_i, meta[15], 2), key_range(v_i, meta[15], 2), *two
    )
    total[meta[18] - 3] += mm(first, kv_w, NT)
    total[pl.ds(meta[19] - 3, 2)] += mm(second, kv_w, NT).reshape(2, CH, D)
    for t, part in enumerate((pick_heads(dq_one, 0), pick_heads(dq_two, 0), pick_heads(dq_two, 1))):
        whole = ((dq_i[0, t] + part).T * (1.0 / math.sqrt(HEAD_DIM))).astype(bf16)
        j = meta[9 + t]
        dq_all[pl.ds(pl.multiple_of(j * CH, CH), CH)] = whole
        total[j] += mm(whole, weight(0, PAIR), NT)
    out_grad = mm(low_t[...], o_i[0].reshape(3 * CH, PAIR)).astype(bf16)
    w_all[:, 3 * PAIR :] = out_grad
    q_grad = mm(columns(3, 3), dq_all[...]).astype(bf16)
    w_all[:, :PAIR] = q_grad
    kv_grad = (
        mm(columns(meta[16], 3), dkv_i[0, 0:3].reshape(3 * CH, 2 * PAIR))
        + mm(columns(meta[17], 2), dkv_i[0, 3:5].reshape(2 * CH, 2 * PAIR))
        + mm(columns(meta[18], 1), first)
        + mm(columns(meta[19], 2), second)
    )
    w_all[:, PAIR : 3 * PAIR] = kv_grad.astype(bf16)
    high = D // split
    for apart in range(split):
        rows = pl.ds(pl.multiple_of((base[0] ^ apart) * high, high), high)
        w_grads[apart % halves][(apart // halves) * groups + step] = w_all[rows]

    @pl.when(step == groups - 1)
    def _():
        d_own[...] = total[...].reshape(3 * CH, D)


def attn_backward_far(weight, meta, grad_in, kept, groups, small, after=()):
    rows = grad_in.shape[0]
    const = lambda s, *_: (0, 0)
    pair = lambda s, *_: (s, 0, 0, 0)
    full = pl.BlockSpec((rows, D), const)
    three = pl.BlockSpec((1, 3, CH, PAIR), pair)
    eight = pl.BlockSpec((1, 2 * SLOT, CH, PAIR), pair)
    lines = pl.BlockSpec((1, 3, 8, CH), pair)
    tiny = pl.BlockSpec((8, D), const)
    return pl.pallas_call(
        after_operands(functools.partial(attn_backward_far_kernel, groups), 1, len(after)),
        grid_spec=pltpu.PrefetchScalarGridSpec(
            num_scalar_prefetch=1,
            grid=(groups,),
            in_specs=[hbm()] * len(after)
            + [weight_spec(*weight), full, tiny, three, eight, eight, three, lines],
            out_specs=[
                full,
                full,
                full,
                pl.BlockSpec((1, 3, PAIR, CH), pair),
                pl.BlockSpec((1, 5, CH, 2 * PAIR), pair),
                three,
                lines,
                tiny,
            ],
            scratch_shapes=[
                pltpu.VMEM((3, CH, D), bf16),
                pltpu.VMEM((9, CH, D), f32),
            ],
        ),
        out_shape=[
            jax.ShapeDtypeStruct((rows, D), bf16),
            jax.ShapeDtypeStruct((rows, D), f32),
            jax.ShapeDtypeStruct((rows, D), bf16),
            jax.ShapeDtypeStruct((groups, 3, PAIR, CH), f32),
            jax.ShapeDtypeStruct((groups, 5, CH, 2 * PAIR), bf16),
            jax.ShapeDtypeStruct((groups, 3, CH, PAIR), bf16),
            jax.ShapeDtypeStruct((groups, 3, 8, CH), f32),
            jax.ShapeDtypeStruct((8, D), f32),
        ],
        compiler_params=params(28),
        cost_estimate=pl.CostEstimate(
            flops=24_000_000_000, bytes_accessed=16_000_000, transcendentals=0
        ),
        name="attn_backward_far",
    )(meta, *from_hbm(*after, weight[0], grad_in), small, *from_hbm(*kept))


def attn_backward_near(weight, meta, base, ext, grad_in, kept, far, groups, split, small, halves):
    rows = grad_in.shape[0]
    const = lambda s, *_: (0, 0)
    pair = lambda s, *_: (s, 0, 0, 0)
    full = pl.BlockSpec((rows, D), const)
    three = pl.BlockSpec((1, 3, CH, PAIR), pair)
    eight = pl.BlockSpec((1, 2 * SLOT, CH, PAIR), pair)
    lines = pl.BlockSpec((1, 3, 8, CH), pair)
    tiny = pl.BlockSpec((8, D), const)
    places = split * groups
    return pl.pallas_call(
        functools.partial(attn_backward_near_kernel, groups, split, halves),
        grid_spec=pltpu.PrefetchScalarGridSpec(
            num_scalar_prefetch=2,
            grid=(groups,),
            in_specs=[weight_spec(*weight), full, full, full, full, three, eight, eight, three, lines]
            + [
                pl.BlockSpec((1, 3, PAIR, CH), pair),
                pl.BlockSpec((1, 5, CH, 2 * PAIR), pair),
                three,
                lines,
                tiny,
            ],
            out_specs=[pl.BlockSpec((places // halves, D // split, D), lambda s, *_: (0, 0, 0))]
            * halves
            + [full, tiny],
            scratch_shapes=[
                pltpu.VMEM((9, D, CH), bf16),
                pltpu.VMEM((D, rows), bf16),
                pltpu.VMEM((3, CH, D), f32),
                pltpu.VMEM((rows, PAIR), bf16),
                pltpu.VMEM((D, D), bf16),
            ],
        ),
        out_shape=[jax.ShapeDtypeStruct((places // halves, D // split, D), bf16)] * halves
        + [jax.ShapeDtypeStruct((rows, D), f32), jax.ShapeDtypeStruct((8, D), f32)],
        compiler_params=params(28),
        cost_estimate=pl.CostEstimate(
            flops=20_000_000_000, bytes_accessed=22_000_000, transcendentals=0
        ),
        name="attn_backward_near",
    )(meta, base, *from_hbm(weight[0], *ext), grad_in, *from_hbm(*kept), *far, small)


def entry_backward_kernel(
    grad_in, d_own, d_near, d_left, d_right, source, norm, ids, grad_out, small
):
    small[...] = jnp.zeros_like(small)
    for j in range(3):
        rows = pl.ds(j * CH, CH)
        arrived = d_own[rows] + d_near[rows] + d_left[rows].astype(f32) + d_right[rows].astype(f32)
        back, gain_grad, shift_grad = norm_backward(arrived, source[rows], norm[0:1])
        values = grad_in[rows] + back
        grad_out[rows] = values
        small[0:1] += gain_grad
        small[1:2] += shift_grad
        letter = lax.broadcasted_iota(jnp.int32, (32, CH), 0)
        chosen = (letter == ids[:, j * CH : (j + 1) * CH]).astype(bf16)
        high = values.astype(bf16)
        rest = values - high.astype(f32)
        middle = rest.astype(bf16)
        low = (rest - middle.astype(f32)).astype(bf16)
        small[8:40] += mm(chosen, high) + mm(chosen, middle) + mm(chosen, low)


def entry_backward(grad_in, d_own, d_near, d_left, d_right, source, norm, ids, after=()):
    rows = grad_in.shape[0]
    return pl.pallas_call(
        after_operands(entry_backward_kernel, 0, len(after)),
        in_specs=[hbm()] * len(after) + [vmem()] * 8,
        out_specs=[vmem()] * 2,
        out_shape=[
            kept_out((rows, D), f32),
            jax.ShapeDtypeStruct((40, D), f32),
        ],
        compiler_params=pltpu.CompilerParams(vmem_limit_bytes=40 * 1024 * 1024),
        cost_estimate=pl.CostEstimate(
            flops=100_000_000, bytes_accessed=9_000_000, transcendentals=0
        ),
        name="entry_backward",
    )(*after, grad_in, d_own, d_near, d_left, d_right, source, norm, ids)


def backward_plan(my_mp, row_start, first_seq, chunk_seq):
    lead = jnp.where(my_mp < 2, 0, 2)
    late_one = my_mp % 2 == 0
    late_two = my_mp < 2
    found = [lead, 1, 2 - lead]
    lead_seq = jnp.where(my_mp < 2, chunk_seq[0], chunk_seq[2])
    shifts = [
        (lead_seq, jnp.where(late_one, 1, 0)),
        (chunk_seq[1], jnp.where(late_two, 2, 0)),
        (lead_seq, jnp.where(late_one, 0, 3)),
        (chunk_seq[1], jnp.where(late_two, 0, 2)),
    ]
    found += [(seq - first_seq) * SLOT + shift for seq, shift in shifts]
    found += [3 + (seq * LEN - row_start) // CH + shift for seq, shift in shifts]
    return [jnp.asarray(entry) for entry in found]


def shards(
    token_ids,
    timesteps,
    importance,
    cotangent,
    qkv_weight,
    out_weight,
    up_weight,
    down_weight,
    norm_params,
    embed_table,
    qkv_first,
    qkv_second,
    out_first,
    out_second,
    up_first,
    up_second,
    down_first,
    down_second,
    norm_first,
    norm_second,
    embed_first,
    embed_second,
):
    dp, mp = lax.axis_size("dp"), lax.axis_size("mp")
    small = dp == 8 and mp == 4
    groups = mp
    split = dp if small else 1
    row_count = token_ids.shape[0]
    seq_here = timesteps.shape[0]
    high = D // dp
    my_mp = lax.axis_index("mp")
    my_dp = lax.axis_index("dp")
    row_start = my_mp * row_count

    first_seq = row_start // LEN
    last_seq = (row_start + row_count - 1) // LEN
    chunk_seq = [(row_start + CH * j) // LEN for j in range(3)]
    meta = jnp.stack(
        [
            3 + (first_seq * LEN - row_start) // CH,
            3 + (last_seq * LEN - row_start) // CH,
            last_seq - first_seq + 1,
        ]
        + [seq - first_seq for seq in chunk_seq]
        + chunk_seq
        + backward_plan(my_mp, row_start, first_seq, chunk_seq)
    ).astype(jnp.int32)
    in_order = jnp.arange(split * groups, dtype=jnp.int32)
    owner = block_owners(my_dp) if small else in_order
    base = jnp.where(small, my_dp, 0).astype(jnp.int32)[None]
    halves = 2 if small else 1

    attn_mine = []
    mlp_mine = []
    for layer in range(LAYERS):
        attn_mine.append(
            jnp.concatenate(
                [qkv_weight[layer].reshape(high, -1), out_weight[layer].T], axis=1
            ).astype(bf16)
        )
        mlp_mine.append(
            jnp.concatenate([up_weight[layer], down_weight[layer].T], axis=1).astype(bf16)
        )
    both_mine = jnp.concatenate([attn_mine[1], mlp_mine[1]], axis=1)
    if small:
        lines = row_count // D + (row_count % D > 0)
        ids_low = jnp.pad(token_ids.astype(bf16), (0, lines * D - row_count)).reshape(lines, D)
        first_mine = jnp.concatenate([attn_mine[0], ids_low], axis=0)
        first_z = gather_z(first_mine)
        attn_z = first_z[:, :high]
        ids_z = first_z[:, high:].reshape(4, lines * D)[:, :row_count].astype(jnp.int32)
        ids_left = ids_z[my_mp ^ jnp.maximum(my_mp - 1, 0)]
        ids_right = ids_z[my_mp ^ jnp.minimum(my_mp + 1, mp - 1)]
    else:
        ids_left, ids_right = shift_right(token_ids), shift_left(token_ids)
    ids_ext = jnp.concatenate([ids_left, token_ids, ids_right])
    seq_ext = (row_start - row_count + jnp.arange(3 * row_count, dtype=jnp.int32)) // LEN
    letters = (ids_ext[:, None] == jnp.arange(VOCAB, dtype=jnp.int32)[None, :]).astype(f32)
    member = (seq_ext[:, None] == jnp.arange(seq_here, dtype=jnp.int32)[None, :]).astype(f32)
    entry_ext = jnp.dot(letters, embed_table, precision=highest) + jnp.dot(
        member, time_features(timesteps), precision=highest
    )
    normed_ext = layer_norm(entry_ext, norm_params[0, 0], norm_params[0, 1]).astype(bf16)
    resid = entry_ext[row_count : 2 * row_count]
    ext = (
        normed_ext[:row_count],
        normed_ext[row_count : 2 * row_count],
        normed_ext[2 * row_count :],
    )

    if small:
        mlp_first, attn_z = tie(mlp_mine[0], attn_z)
        attn_sent = [flip(attn_z, bits) for bits in (8, 16, 24)]
        attn_sent, (ext, resid) = tie(attn_sent, (ext, resid))
        attn_xy = jnp.concatenate([attn_z] + list(attn_sent), axis=0)
        mlp_z = gather_z(mlp_first)
        mlp_z, attn_xy = tie(mlp_z, attn_xy)
        attn_w = [(attn_xy, flip(attn_xy, 4))]
        mlp_found = gather_dp(mlp_z)
        both_mine, mlp_z = tie(both_mine, mlp_z)
        both_sent = [flip(both_mine, bits) for bits in (1, 2, 3)]
    else:
        attn_w = [plain_gather(attn_mine[0])]
        mlp_found = plain_gather(mlp_mine[0])
        attn_w.append(plain_gather(both_mine))
        mlp_w = [((mlp_found, 0), (mlp_found, 1)), ((attn_w[1], 1), (attn_w[1], 2))]

    kept = []
    for layer in range(LAYERS):
        last = layer == LAYERS - 1
        outs, w_attn = attn_forward(
            attn_w[layer], meta, owner, *ext, resid, norm_params[layer], groups
        )
        middle, normed = outs[:2]
        if small and layer == 0:
            both_sent, normed = tie(both_sent, normed)
            both_z = jnp.stack([both_mine] + list(both_sent))
            last_found = gather_dp(both_z[:, :, D:])
            mlp_w = [((mlp_found, 0), (mlp_found, 1)), ((last_found, 0), (last_found, 1))]
            attn_z = both_z[:, :, :D]
            attn_sent = [flip(attn_z, bits) for bits in (8, 16, 24)]
            attn_z, normed = tie(attn_z, normed)
        w_mlp = mlp_w[layer]
        if layer + 1 < LAYERS:
            mlp_outs, w_mlp = mlp_forward(
                w_mlp, owner, normed, middle, norm_params[layer + 1], groups
            )
        kept.append((ext, resid, middle, normed, outs[2:], mlp_outs[1:3], (w_attn, 0), w_mlp))
        if layer + 1 < LAYERS:
            resid, following = mlp_outs[0], mlp_outs[3]
            if small:
                attn_sent, following = tie(attn_sent, following)
                attn_xy = jnp.concatenate([attn_z] + list(attn_sent), axis=0)
                attn_w.append((attn_xy, flip(attn_xy, 4)))
            ext = (shift_right(following), following, shift_left(following))

    norm_grads = [[None] * 4 for _ in range(LAYERS)]
    attn_grads = [None] * LAYERS
    mlp_grads = [None] * LAYERS
    after = ()
    for layer in reversed(range(LAYERS)):
        ext, source, middle, normed, attn_kept, (act, slope), w_attn, w_mlp = kept[layer]
        norm = norm_params[layer]
        if layer + 1 == LAYERS:
            activations, mlp_grad, grad_mid, n_grad = mlp_last(
                w_mlp, meta, in_order, importance, cotangent, normed, middle, norm, groups, split
            )
        else:
            mlp_grad, grad_mid, n_grad = mlp_backward(
                w_mlp,
                meta,
                in_order,
                begin,
                act,
                slope,
                normed,
                middle,
                norm,
                groups,
                split,
                after,
            )
        after = ()
        if small:
            if layer + 1 < LAYERS:
                attn_found, (mlp_grad, grad_mid) = tie(attn_found, (mlp_grad, grad_mid))
            mlp_rows = scatter_dp(mlp_grad, dp)
            if layer + 1 < LAYERS:
                attn_rows = add_four(attn_mine_rows, attn_found, False)
                above = jnp.concatenate([attn_rows, above], axis=2)
                above_mine, above_found = scatter_four(above, 1)
                after = (attn_rows,)
        d_left, d_own, d_right, *far, n_grad = attn_backward_far(
            w_attn, meta, grad_mid, attn_kept, groups, n_grad, after
        )
        if small and layer + 1 < LAYERS:
            above_found, (d_left, d_right) = tie(above_found, (d_left, d_right))
        from_right = shift_left(d_left)
        from_left = shift_right(d_right)
        *attn_grad, d_near, n_grad = attn_backward_near(
            w_attn, meta, base, ext, grad_mid, attn_kept, far, groups, split, n_grad, halves
        )
        (from_left, from_right), (attn_grad, d_near) = tie(
            (from_left, from_right), (attn_grad, d_near)
        )
        after = ()
        if not small:
            mlp_grads[layer] = plain_scatter(mlp_grad, dp)
            attn_grads[layer] = plain_scatter(attn_grad[0], dp)
        elif layer + 1 == LAYERS:
            attn_held = scatter_core(*attn_grad)
            attn_mine_rows, attn_found = scatter_four(attn_held, 8)
            above = mlp_rows
            after = (attn_held,)
        else:
            above_total = add_four(above_mine, above_found, True)
            attn_grads[1] = above_total[:, :D]
            mlp_grads[1] = above_total[:, D:]
        norm_grads[layer][2:] = [n_grad[2], n_grad[3]]
        if layer + 1 < LAYERS:
            norm_grads[layer + 1][:2] = [n_grad[0], n_grad[1]]
        begin = (grad_mid, d_own, d_near, from_left, from_right, source, norm_params[layer])
    input_grad, reduced = entry_backward(*begin, token_ids[None, :])
    norm_grads[0][:2] = [reduced[0], reduced[1]]
    stacked = jnp.concatenate(
        [jnp.stack([row for rows in norm_grads for row in rows]), reduced[8:40]], axis=0
    )
    if small:
        rows = D // dp
        rest = stacked.astype(bf16)
        rest = (rest.astype(f32) + flip(rest, 4).astype(f32)).astype(bf16)
        held = scatter_core(*attn_grad).reshape(16 * rows, D)
        sent = [
            flip(jnp.concatenate([held[4 * rows * i : 4 * rows * (i + 1)], rest], axis=0), 8 * i)
            for i in (1, 2, 3)
        ]
        mlp_own, mlp_sent = scatter_four(mlp_rows, 1)
        mlp_sent, sent = tie(mlp_sent, sent)
        mine = add_four(jnp.concatenate([held[: 4 * rows], rest], axis=0)[None], [p[None] for p in sent], True)
        held, rest = mine[: 4 * rows].astype(bf16), mine[4 * rows :].astype(bf16)
        sent = [
            flip(jnp.concatenate([held[rows * i : rows * (i + 1)], rest], axis=0), i)
            for i in (1, 2, 3)
        ]
        total = add_four(
            jnp.concatenate([held[:rows], rest], axis=0)[None], [p[None] for p in sent], True
        )
        attn_grads[0] = total[:rows]
        stacked = total[rows:]
        mlp_grads[0] = add_four(mlp_own, mlp_sent, True)
    else:
        stacked = lax.psum(stacked, ALL)
    norm_grad = stacked[: 4 * LAYERS].reshape(LAYERS, 4, D)
    embed_grad = stacked[4 * LAYERS : 4 * LAYERS + VOCAB]

    qkv_grad = jnp.stack([g[:, : 3 * PAIR].reshape(high, 3, PAIR) for g in attn_grads])
    out_grad = jnp.stack([g[:, 3 * PAIR :].T for g in attn_grads])
    up_grad = jnp.stack([g[:, :D] for g in mlp_grads])
    down_grad = jnp.stack([g[:, D:].T for g in mlp_grads])
    qkv_master, qkv_mean, qkv_square = adamw(
        qkv_weight, qkv_first, qkv_second, qkv_grad, 2.0 / math.sqrt(D), decay_matrix
    )
    out_master, out_mean, out_square = adamw(
        out_weight, out_first, out_second, out_grad, 2.0 / math.sqrt(D), decay_matrix
    )
    up_master, up_mean, up_square = adamw(
        up_weight, up_first, up_second, up_grad, 2.0 / math.sqrt(D), decay_matrix
    )
    down_master, down_mean, down_square = adamw(
        down_weight, down_first, down_second, down_grad, 2.0 / math.sqrt(FF), decay_matrix
    )
    norm_master, norm_mean, norm_square = adamw(
        norm_params, norm_first, norm_second, norm_grad, vector_rate, 0.0
    )
    embed_master, embed_mean, embed_square = adamw(
        embed_table, embed_first, embed_second, embed_grad, embed_rate, 0.0
    )
    return (
        activations,
        input_grad,
        qkv_master,
        qkv_mean,
        qkv_square,
        qkv_master.astype(bf16),
        out_master,
        out_mean,
        out_square,
        out_master.astype(bf16),
        up_master,
        up_mean,
        up_square,
        up_master.astype(bf16),
        down_master,
        down_mean,
        down_square,
        down_master.astype(bf16),
        norm_master,
        norm_mean,
        norm_square,
        embed_master,
        embed_mean,
        embed_square,
    )


def solution(mesh):
    rows = P(("dp", "mp"), None)
    qkv = P(None, "dp", None, "mp")
    wide = P(None, "mp", "dp")
    tall = P(None, "dp", "mp")
    same = P()
    return jax.shard_map(
        shards,
        mesh=mesh,
        in_specs=(P(("dp", "mp")), P("dp"), P("dp"), rows, qkv, wide, tall, wide, same, same)
        + (qkv, qkv, wide, wide, tall, tall, wide, wide, same, same, same, same),
        out_specs=(rows, rows)
        + (qkv,) * 4
        + (wide,) * 4
        + (tall,) * 4
        + (wide,) * 4
        + (same,) * 6,
        check_vma=False,
    )
```

```python
import functools
import math

import jax
import jax.numpy as jnp
from jax import lax
from jax.experimental import pallas as pl
from jax.experimental.pallas import tpu as pltpu
from jax.sharding import PartitionSpec as P

HEAD_DIM = 64
FF = 2048
VOCAB = 27
LAYERS = 2
LEN = 1024
STEP = 10
D = 512
PAIR = 2 * HEAD_DIM
CH = 256
SLOT = LEN // CH

bf16 = jnp.bfloat16
f32 = jnp.float32
highest = lax.Precision.HIGHEST
eps_norm = 1e-05
beta_one = 0.5
beta_two = 0.5
adam_eps = 1e-08
decay_matrix = 0.01
vector_rate = 0.6
embed_rate = 1.0
LOG2E = math.log2(math.e)
LN2 = math.log(2.0)
ALL = ("dp", "mp")

NN = (((1,), (0,)), ((), ()))
NT = (((1,), (1,)), ((), ()))


def mm(left, right, dims=NN):
    return lax.dot_general(left, right, dims, preferred_element_type=f32)


def vmem():
    return pl.BlockSpec(memory_space=pltpu.VMEM)


def smem():
    return pl.BlockSpec(memory_space=pltpu.SMEM)


def hbm():
    return pl.BlockSpec(memory_space=pl.ANY)


def after_operands(kernel, prefetched, count):
    def call(*refs):
        return kernel(*refs[:prefetched], *refs[prefetched + count :])

    return call


def kept_out(shape, dtype):
    return pltpu.HBM(shape, dtype)


def from_hbm(*arrays):
    return tuple(pltpu.with_memory_space_constraint(x, pltpu.HBM) for x in arrays)


def params(mib):
    return pltpu.CompilerParams(
        dimension_semantics=("arbitrary",), vmem_limit_bytes=mib * 1024 * 1024
    )


def norm_parts(values):
    row_mean = jnp.mean(values, axis=-1, keepdims=True)
    centered = values - row_mean
    variance = jnp.mean(centered * centered, axis=-1, keepdims=True)
    inverse = lax.rsqrt(variance + eps_norm)
    return centered * inverse, inverse


def layer_norm(values, gain_vec, shift_vec):
    scaled, _ = norm_parts(values)
    return scaled * gain_vec + shift_vec


def norm_backward(grad_out, values, gain_vec):
    scaled, inverse = norm_parts(values)
    weighted = grad_out * gain_vec
    mean_plain = jnp.mean(weighted, axis=-1, keepdims=True)
    mean_scaled = jnp.mean(weighted * scaled, axis=-1, keepdims=True)
    grad_in = (weighted - mean_plain - scaled * mean_scaled) * inverse
    gain_grad = jnp.sum(grad_out * scaled, axis=0, keepdims=True)
    shift_grad = jnp.sum(grad_out, axis=0, keepdims=True)
    return grad_in, gain_grad, shift_grad


def gelu_pair(hidden):
    square = hidden * hidden
    bell = jnp.exp2(square * (-0.5 * LOG2E))
    phi = 0.5 + 0.5 * lax.erf(hidden * (1.0 / math.sqrt(2.0)))
    return hidden * phi, phi + hidden * bell * (1.0 / math.sqrt(2.0 * math.pi))


def time_features(step_values):
    half_width = D // 2
    frequency = jnp.exp(-math.log(10000.0) * jnp.arange(half_width, dtype=f32) / half_width)
    angles = step_values.astype(f32)[:, None] * frequency[None, :]
    return jnp.concatenate([jnp.sin(angles), jnp.cos(angles)], axis=1)


def adamw(weight, mean_old, square_old, gradient, step_rate, decay_weight):
    mean_new = beta_one * mean_old + (1.0 - beta_one) * gradient
    square_new = beta_two * square_old + (1.0 - beta_two) * gradient * gradient
    fix_one = 1.0 - beta_one**STEP
    fix_two = 1.0 - beta_two**STEP
    direction = mean_new / fix_one / (jnp.sqrt(square_new / fix_two) + adam_eps)
    return (weight - step_rate * (direction + decay_weight * weight), mean_new, square_new)


def permute_all(values, target):
    count = lax.axis_size("dp") * lax.axis_size("mp")
    return lax.ppermute(values, ALL, [(i, target(i)) for i in range(count)])


def block_owners(my_dp):
    index = jnp.arange(32, dtype=jnp.int32)
    return my_dp ^ ((((index >> 2) & 3) << 1) | (index >> 4))


def tie(values, after):
    return lax.optimization_barrier((values, after))


def flip(values, bits):
    return permute_all(values, lambda i: i ^ bits)


def gather_z(values):
    return jnp.stack([values] + [flip(values, bits) for bits in (1, 2, 3)])


def scatter_core(own, other):
    return (own.astype(f32) + flip(other, 4).astype(f32)).astype(bf16)


def scatter_four(blocks, unit):
    size = blocks.shape[0] // 4
    found = [flip(blocks[i * size : (i + 1) * size], i * unit) for i in (1, 2, 3)]
    return blocks[:size], found


def add_four(own, found, last):
    one, two, three = [part.astype(f32) for part in found]
    total = (own.astype(f32) + one) + (two + three)
    return total[0] if last else total.astype(bf16)


def gather_dp(held):
    return lax.all_gather(held, "dp", axis=0, tiled=False)


def scatter_dp(blocks, dp):
    places, rows, columns = blocks.shape
    flat = blocks.reshape(places * rows, columns)
    return lax.psum_scatter(flat, "dp", scatter_dimension=0, tiled=True).reshape(
        places // dp, rows, columns
    )


def plain_gather(values):
    dp, mp = lax.axis_size("dp"), lax.axis_size("mp")
    rows, columns = values.shape
    found = lax.all_gather(values, ALL, axis=0, tiled=True).reshape(dp, mp, rows, columns)
    if rows % 16 == 0:
        return found
    return jnp.swapaxes(found, 0, 1).reshape(1, mp, dp * rows, columns)


def plain_scatter(blocks, dp):
    places, rows, columns = blocks.shape
    mp = lax.axis_size("mp")
    if places != dp * mp:
        blocks = jnp.swapaxes(blocks.reshape(mp, dp, D // dp, columns), 0, 1)
    flat = blocks.reshape(dp * mp * (D // dp), columns)
    return lax.psum_scatter(flat, ALL, scatter_dimension=0, tiled=True).astype(f32)


def shift_right(values):
    count = lax.axis_size("mp")
    return lax.ppermute(values, "mp", [(i, i + 1) for i in range(count - 1)])


def shift_left(values):
    count = lax.axis_size("mp")
    return lax.ppermute(values, "mp", [(i + 1, i) for i in range(count - 1)])


def fetch_blocks(table, near, far, targets, sems):
    copies = []
    for place in range(32):
        owner = table[place]
        source = near.at[place] if place < 16 else far.at[place - 16]
        for index, (target, begin, width) in enumerate(targets):
            copies.append(
                pltpu.make_async_copy(
                    source.at[:, pl.ds(begin, width)],
                    target.at[owner, place % 4],
                    sems.at[place, index],
                )
            )
    for copy in copies:
        copy.start()
    return copies


def attn_forward_kernel(gathered, groups, meta, table, *refs):
    if gathered:
        near, far, left, own, right, resid, norm = refs[:7]
        middle, normed, q_o, k_o, v_o, o_o, lse_o, w_o = refs[7:15]
        ext, total, sems = refs[15:]
    else:
        w_in, left, own, right, resid, norm = refs[:6]
        middle, normed, q_o, k_o, v_o, o_o, lse_o = refs[6:13]
        ext, total = refs[13:]
    step = pl.program_id(0)

    @pl.when(step == 0)
    def _():
        if gathered:
            copies = fetch_blocks(table, near, far, [(w_o, 0, D)], sems)
        for index, part in enumerate((left, own, right)):
            ext[pl.ds(3 * index, 3)] = part[...].reshape(3, CH, D)
        total[...] = jnp.zeros_like(total)
        if gathered:
            for copy in copies:
                copy.wait()

    def weight(begin, end):
        found = w_o[:, step, :, begin:end] if gathered else w_in[:, 0, :, begin:end]
        return found.reshape(D, end - begin)

    for j in range(3):
        q_o[0, j] = (mm(ext[3 + j], weight(0, PAIR)) * (LOG2E / math.sqrt(HEAD_DIM))).astype(bf16)

    def project(slot, carry):
        begin = meta[slot]
        kv_w = weight(PAIR, 3 * PAIR)
        both = mm(ext[pl.ds(begin, SLOT)].reshape(LEN, D), kv_w).astype(bf16)
        k_o[0, pl.ds(slot * SLOT, SLOT)] = both[:, :PAIR].reshape(SLOT, CH, PAIR)
        v_o[0, pl.ds(slot * SLOT, SLOT)] = both[:, PAIR:].reshape(SLOT, CH, PAIR)
        return carry

    lax.fori_loop(0, meta[2], project, 0)
    lane = lax.broadcasted_iota(jnp.int32, (CH, PAIR), 1) // HEAD_DIM
    lane_all = lax.broadcasted_iota(jnp.int32, (LEN, PAIR), 1) // HEAD_DIM

    for j in range(3):
        slot = meta[3 + j]
        query = q_o[0, j]
        keys = k_o[0, pl.ds(slot * SLOT, SLOT)].reshape(LEN, PAIR)
        values = v_o[0, pl.ds(slot * SLOT, SLOT)].reshape(LEN, PAIR)
        zero = jnp.zeros_like(query)
        both = jnp.concatenate([jnp.where(lane == h, query, zero) for h in range(2)], axis=0)
        scores = mm(both, keys, NT)
        top = jnp.max(scores, axis=1, keepdims=True)
        weights = jnp.exp2(scores - top).astype(bf16)
        mixed = []
        for h in range(2):
            value_h = jnp.where(lane_all == h, values, jnp.ones_like(values))
            mixed.append(mm(weights[h * CH : (h + 1) * CH], value_h))
        sums = pltpu.roll(jnp.where(lane == 1, mixed[0], mixed[1]), HEAD_DIM, 1)
        lines = (jnp.where(lane == 0, top[:CH], top[CH:]) + jnp.log2(sums)).T
        for h in range(2):
            lse_o[0, j, h : h + 1] = lines[h * HEAD_DIM : h * HEAD_DIM + 1]
        out = (jnp.where(lane == 0, mixed[0], mixed[1]) / sums).astype(bf16)
        o_o[0, j] = out
        total[j] += mm(out, weight(3 * PAIR, D), NT)

    @pl.when(step == groups - 1)
    def _():
        for j in range(3):
            rows = pl.ds(j * CH, CH)
            values = resid[rows] + total[j]
            middle[rows] = values
            normed[rows] = layer_norm(values, norm[2:3], norm[3:4]).astype(bf16)


def attn_forward(weights, meta, table, left, own, right, resid, norm, groups):
    rows = own.shape[0]
    gathered = isinstance(weights, tuple)
    const = lambda s, *_: (0, 0)
    pair = lambda s, *_: (s, 0, 0, 0)
    full = pl.BlockSpec((rows, D), const)
    out_shape = [
        kept_out((rows, D), f32),
        kept_out((rows, D), bf16),
        kept_out((groups, 3, CH, PAIR), bf16),
        kept_out((groups, 2 * SLOT, CH, PAIR), bf16),
        kept_out((groups, 2 * SLOT, CH, PAIR), bf16),
        kept_out((groups, 3, CH, PAIR), bf16),
        kept_out((groups, 3, 8, CH), f32),
    ]
    out_specs = [
        full,
        full,
        pl.BlockSpec((1, 3, CH, PAIR), pair),
        pl.BlockSpec((1, 2 * SLOT, CH, PAIR), pair),
        pl.BlockSpec((1, 2 * SLOT, CH, PAIR), pair),
        pl.BlockSpec((1, 3, CH, PAIR), pair),
        pl.BlockSpec((1, 3, 8, CH), pair),
    ]
    scratch = [
        pltpu.VMEM((9, CH, D), bf16),
        pltpu.VMEM((3, CH, D), f32),
    ]
    if gathered:
        w_args = list(weights)
        w_specs = [hbm(), hbm()]
        out_shape.append(kept_out((8, 4, 64, D), bf16))
        out_specs.append(pl.BlockSpec((8, 4, 64, D), pair_zero))
        scratch.append(pltpu.SemaphoreType.DMA((32, 1)))
    else:
        w_args = [weights]
        split, _, high, _ = weights.shape
        w_specs = [pl.BlockSpec((split, 1, high, D), lambda s, *_: (0, s, 0, 0))]
    outs = pl.pallas_call(
        functools.partial(attn_forward_kernel, gathered, groups),
        grid_spec=pltpu.PrefetchScalarGridSpec(
            num_scalar_prefetch=2,
            grid=(groups,),
            in_specs=w_specs
            + [full, full, full, full, pl.BlockSpec((4, D), const)],
            out_specs=out_specs,
            scratch_shapes=scratch,
        ),
        out_shape=out_shape,
        compiler_params=params(28),
        cost_estimate=pl.CostEstimate(
            flops=29_000_000_000, bytes_accessed=14_000_000, transcendentals=0
        ),
        name="attn_forward",
    )(meta, table, *from_hbm(*w_args, left, own, right, resid), norm)
    if gathered:
        return outs[:7], outs[7]
    return outs, weights


def pair_zero(s, *_):
    return (0, 0, 0, 0)


def mlp_forward_kernel(gathered, groups, table, *refs):
    if gathered:
        near, far, normed, middle, norm = refs[:5]
        refs = refs[5:]
    else:
        up_in, down_in, normed, middle, norm = refs[:5]
        refs = refs[5:]
    after, act_o, slope_o, next_o = refs[:4]
    refs = refs[4:]
    if gathered:
        up_o, down_o, total, sems = refs
    else:
        (total,) = refs
    step = pl.program_id(0)

    @pl.when(step == 0)
    def _():
        if gathered:
            copies = fetch_blocks(table, near, far, [(up_o, 0, D), (down_o, D, D)], sems)
        total[...] = jnp.zeros_like(total)
        if gathered:
            for copy in copies:
                copy.wait()

    if gathered:
        up_w = up_o[:, step].reshape(D, D)
        down_w = down_o[:, step].reshape(D, D)
    else:
        up_w = up_in[:, 0].reshape(D, D)
        down_w = down_in[:, 0].reshape(D, D)
    for j in range(3):
        rows = pl.ds(j * CH, CH)
        hidden = mm(normed[rows], up_w)
        act, slope = gelu_pair(hidden)
        act = act.astype(bf16)
        act_o[0, rows] = act
        slope_o[0, rows] = slope.astype(bf16)
        total[j] += mm(act, down_w, NT)

    @pl.when(step == groups - 1)
    def _():
        for j in range(3):
            rows = pl.ds(j * CH, CH)
            values = middle[rows] + total[j]
            after[rows] = values
            next_o[rows] = layer_norm(values, norm[0:1], norm[1:2]).astype(bf16)


def mlp_forward(weights, table, normed, middle, norm, groups):
    rows = normed.shape[0]
    gathered = not isinstance(weights[0], tuple)
    const = lambda s, *_: (0, 0)
    full = pl.BlockSpec((rows, D), const)
    part = pl.BlockSpec((1, rows, D), lambda s, *_: (s, 0, 0))
    out_shape = [
        kept_out((rows, D), f32),
        kept_out((groups, rows, D), bf16),
        kept_out((groups, rows, D), bf16),
        jax.ShapeDtypeStruct((rows, D), bf16),
    ]
    out_specs = [full, part, part, full]
    scratch = [pltpu.VMEM((3, CH, D), f32)]
    if gathered:
        w_args = list(weights)
        w_specs = [hbm(), hbm()]
        for _ in range(2):
            out_shape.append(jax.ShapeDtypeStruct((8, 4, 64, D), bf16))
            out_specs.append(pl.BlockSpec((8, 4, 64, D), pair_zero))
        scratch.append(pltpu.SemaphoreType.DMA((32, 2)))
    else:
        (up_w, up_at), (down_w, down_at) = weights
        w_args = [up_w, down_w]
        w_specs = [weight_spec(up_w, up_at), weight_spec(down_w, down_at)]
    outs = pl.pallas_call(
        functools.partial(mlp_forward_kernel, gathered, groups),
        grid_spec=pltpu.PrefetchScalarGridSpec(
            num_scalar_prefetch=1,
            grid=(groups,),
            in_specs=w_specs + [full, full, pl.BlockSpec((4, D), const)],
            out_specs=out_specs,
            scratch_shapes=scratch,
        ),
        out_shape=out_shape,
        compiler_params=params(28),
        cost_estimate=pl.CostEstimate(
            flops=15_000_000_000, bytes_accessed=18_000_000, transcendentals=0
        ),
        name="mlp_forward",
    )(table, *from_hbm(*w_args, normed, middle), norm)
    if gathered:
        return outs[:-2], ((outs[-2], 0), (outs[-1], 0))
    return outs, weights


def weight_spec(weight, at):
    split, _, high, _ = weight.shape
    return pl.BlockSpec((split, 1, high, D), lambda s, *_: (0, s, 0, at))


def put_blocks(out, table, step, groups, split, begin, values):
    high = D // split
    width = values.shape[1]
    for d in range(split):
        place = table[d * groups + step]
        out[place, :, begin : begin + width] = values[d * high : (d + 1) * high]


def mlp_backward_kernel(groups, split, meta, place, *refs):
    grad_in, d_own, d_near, d_left, d_right, source, norm_up = refs[:7]
    refs = refs[7:]
    up_in, down_in, act, slope, normed, middle, norm = refs[:7]
    refs = refs[7:]
    w_grad, grad_out, n_grad = refs[:3]
    refs = refs[3:]
    grad, low, low_t, norm_t, total = refs
    step = pl.program_id(0)

    @pl.when(step == 0)
    def _():
        n_grad[...] = jnp.zeros_like(n_grad)
        for j in range(3):
            rows = pl.ds(j * CH, CH)
            arrived = d_own[rows] + d_near[rows] + d_left[rows].astype(f32)
            arrived += d_right[rows].astype(f32)
            back, gain_grad, shift_grad = norm_backward(arrived, source[rows], norm_up[0:1])
            values = grad_in[rows] + back
            n_grad[0:1] += gain_grad
            n_grad[1:2] += shift_grad
            grad[j] = values
            rounded = values.astype(bf16)
            low[rows] = rounded
            low_t[:, j * CH : (j + 1) * CH] = rounded.T
            norm_t[:, j * CH : (j + 1) * CH] = normed[rows].T
        total[...] = jnp.zeros_like(total)

    up_w = up_in[:, 0].reshape(D, D)
    down_w = down_in[:, 0].reshape(D, D)
    down_grad = mm(low_t[...], act[0]).astype(bf16)
    put_blocks(w_grad, place, step, groups, split, D, down_grad)
    pieces = []
    for j in range(3):
        rows = pl.ds(j * CH, CH)
        piece = (mm(low[rows], down_w) * slope[0, rows].astype(f32)).astype(bf16)
        pieces.append(piece)
        total[j] += mm(piece, up_w, NT)
    up_grad = mm(norm_t[...], jnp.concatenate(pieces, axis=0)).astype(bf16)
    put_blocks(w_grad, place, step, groups, split, 0, up_grad)

    @pl.when(step == groups - 1)
    def _():
        for j in range(3):
            rows = pl.ds(j * CH, CH)
            back, gain_grad, shift_grad = norm_backward(total[j], middle[rows], norm[2:3])
            grad_out[rows] = grad[j] + back
            n_grad[2:3] += gain_grad
            n_grad[3:4] += shift_grad


def mlp_backward(
    weights, meta, place, begin, act, slope, normed, middle, norm, groups, split, after=()
):
    rows = normed.shape[0]
    const = lambda s, *_: (0, 0)
    full = pl.BlockSpec((rows, D), const)
    part = pl.BlockSpec((1, rows, D), lambda s, *_: (s, 0, 0))
    vec = pl.BlockSpec((4, D), const)
    (up_w, up_at), (down_w, down_at) = weights
    begin_specs = [full] * 6 + [vec]
    places = split * groups
    return pl.pallas_call(
        after_operands(
            functools.partial(mlp_backward_kernel, groups, split), 2, len(after)
        ),
        grid_spec=pltpu.PrefetchScalarGridSpec(
            num_scalar_prefetch=2,
            grid=(groups,),
            in_specs=[hbm()] * len(after)
            + begin_specs
            + [weight_spec(up_w, up_at), weight_spec(down_w, down_at)]
            + [part, part, full, full, vec],
            out_specs=[
                pl.BlockSpec((places, D // split, 2 * D), lambda s, *_: (0, 0, 0)),
                full,
                pl.BlockSpec((8, D), const),
            ],
            scratch_shapes=[
                pltpu.VMEM((3, CH, D), f32),
                pltpu.VMEM((rows, D), bf16),
                pltpu.VMEM((D, rows), bf16),
                pltpu.VMEM((D, rows), bf16),
                pltpu.VMEM((3, CH, D), f32),
            ],
        ),
        out_shape=[
            kept_out((places, D // split, 2 * D), bf16),
            kept_out((rows, D), f32),
            jax.ShapeDtypeStruct((8, D), f32),
        ],
        compiler_params=params(28),
        cost_estimate=pl.CostEstimate(
            flops=20_000_000_000, bytes_accessed=20_000_000, transcendentals=0
        ),
        name="mlp_backward",
    )(meta, place, *from_hbm(*after), *begin, *from_hbm(up_w, down_w, act, slope), normed, middle, norm)


def mlp_last_kernel(groups, split, meta, place, *refs):
    scale, cot, up_in, down_in, normed, middle, norm = refs[:7]
    after, w_grad, grad_out, n_grad = refs[7:11]
    low, low_t, norm_t, total, total_grad = refs[11:]
    step = pl.program_id(0)

    def start_grad(j):
        return cot[pl.ds(j * CH, CH)].astype(f32) * scale[meta[6 + j]]

    @pl.when(step == 0)
    def _():
        n_grad[...] = jnp.zeros_like(n_grad)
        for j in range(3):
            rows = pl.ds(j * CH, CH)
            rounded = start_grad(j).astype(bf16)
            low[rows] = rounded
            low_t[:, j * CH : (j + 1) * CH] = rounded.T
            norm_t[:, j * CH : (j + 1) * CH] = normed[rows].T
        total[...] = jnp.zeros_like(total)
        total_grad[...] = jnp.zeros_like(total_grad)

    up_w = up_in[:, 0].reshape(D, D)
    down_w = down_in[:, 0].reshape(D, D)
    acts, pieces = [], []
    for j in range(3):
        rows = pl.ds(j * CH, CH)
        act, slope = gelu_pair(mm(normed[rows], up_w))
        act = act.astype(bf16)
        acts.append(act)
        total[j] += mm(act, down_w, NT)
        piece = (mm(low[rows], down_w) * slope).astype(bf16)
        pieces.append(piece)
        total_grad[j] += mm(piece, up_w, NT)
    down_grad = mm(low_t[...], jnp.concatenate(acts, axis=0)).astype(bf16)
    put_blocks(w_grad, place, step, groups, split, D, down_grad)
    up_grad = mm(norm_t[...], jnp.concatenate(pieces, axis=0)).astype(bf16)
    put_blocks(w_grad, place, step, groups, split, 0, up_grad)

    @pl.when(step == groups - 1)
    def _():
        for j in range(3):
            rows = pl.ds(j * CH, CH)
            values = middle[rows]
            after[rows] = values + total[j]
            back, gain_grad, shift_grad = norm_backward(total_grad[j], values, norm[2:3])
            grad_out[rows] = start_grad(j) + back
            n_grad[2:3] += gain_grad
            n_grad[3:4] += shift_grad


def mlp_last(weights, meta, place, scale, cot, normed, middle, norm, groups, split):
    rows = normed.shape[0]
    const = lambda s, *_: (0, 0)
    full = pl.BlockSpec((rows, D), const)
    (up_w, up_at), (down_w, down_at) = weights
    places = split * groups
    return pl.pallas_call(
        functools.partial(mlp_last_kernel, groups, split),
        grid_spec=pltpu.PrefetchScalarGridSpec(
            num_scalar_prefetch=2,
            grid=(groups,),
            in_specs=[smem(), full]
            + [weight_spec(up_w, up_at), weight_spec(down_w, down_at)]
            + [full, full, pl.BlockSpec((4, D), const)],
            out_specs=[
                full,
                pl.BlockSpec((places, D // split, 2 * D), lambda s, *_: (0, 0, 0)),
                full,
                pl.BlockSpec((8, D), const),
            ],
            scratch_shapes=[
                pltpu.VMEM((rows, D), bf16),
                pltpu.VMEM((D, rows), bf16),
                pltpu.VMEM((D, rows), bf16),
                pltpu.VMEM((3, CH, D), f32),
                pltpu.VMEM((3, CH, D), f32),
            ],
        ),
        out_shape=[
            kept_out((rows, D), f32),
            kept_out((places, D // split, 2 * D), bf16),
            kept_out((rows, D), f32),
            jax.ShapeDtypeStruct((8, D), f32),
        ],
        compiler_params=params(28),
        cost_estimate=pl.CostEstimate(
            flops=30_000_000_000, bytes_accessed=18_000_000, transcendentals=0
        ),
        name="mlp_last",
    )(meta, place, scale, cot, *from_hbm(up_w, down_w, normed, middle), norm)


def head_rows(values, lane):
    zero = jnp.zeros_like(values)
    return [jnp.where(lane == h, values, zero) for h in range(2)]


def group_backward(keys, values, queries, grads, lse, delta):
    scores = mm(keys, queries, NT)
    grad_p = mm(values, grads, NT)
    probability = jnp.exp2(scores - lse)
    grad_s = (probability * (grad_p - delta)).astype(bf16)
    dv = mm(probability.astype(bf16), grads)
    dk = mm(grad_s, queries) * LN2
    both = jnp.concatenate([dk.astype(bf16), dv.astype(bf16)], axis=1)
    return both, mm(keys.T, grad_s)


def pick_heads(dq_t, index):
    begin = 2 * CH * index
    return jnp.concatenate(
        [dq_t[:HEAD_DIM, begin : begin + CH], dq_t[HEAD_DIM:, begin + CH : begin + 2 * CH]], axis=0
    )


def group_inputs(meta, q_i, lse_i, g_t, delta_t):
    lane = lax.broadcasted_iota(jnp.int32, (CH, PAIR), 1) // HEAD_DIM
    queries, grads, lse, delta = [], [], [], []
    for t in range(3):
        j = meta[9 + t]
        queries.append(head_rows(q_i[0, j], lane))
        grads.append(head_rows(g_t[t], lane))
        lse.append([lse_i[0, j, h : h + 1] for h in range(2)])
        delta.append([delta_t[t][h : h + 1] for h in range(2)])
    found = []
    for parts in ((0,), (1, 2)):
        found.append(
            tuple(
                jnp.concatenate([row for t in parts for row in rows[t]], axis=axis)
                for rows, axis in ((queries, 0), (grads, 0), (lse, 1), (delta, 1))
            )
        )
    return found


def key_range(ref, begin, count):
    return ref[0, pl.ds(begin, count)].reshape(count * CH, PAIR)


def attn_backward_far_kernel(groups, meta, *refs):
    w_in, grad_in, small, q_i, k_i, v_i, o_i, lse_i = refs[:8]
    d_left, d_own, d_right, dq_o, dkv_o, g_o, delta_o, small_o = refs[8:16]
    low, d_ext = refs[16:]
    step = pl.program_id(0)

    @pl.when(step == 0)
    def _():
        for t in range(3):
            rows = pl.ds(pl.multiple_of(meta[9 + t] * CH, CH), CH)
            low[t] = grad_in[rows].astype(bf16)
        d_ext[...] = jnp.zeros_like(d_ext)
        small_o[...] = small[...]

    def weight(begin, end):
        return w_in[:, 0, :, begin:end].reshape(D, end - begin)

    grad_low = mm(low[...].reshape(3 * CH, D), weight(3 * PAIR, D)).astype(bf16)
    g_t = [grad_low[t * CH : (t + 1) * CH] for t in range(3)]
    delta_t = []
    for t in range(3):
        g_o[0, t] = g_t[t]
        product = (g_t[t].astype(f32) * o_i[0, meta[9 + t]].astype(f32)).T
        rows = [
            jnp.sum(product[h * HEAD_DIM : (h + 1) * HEAD_DIM], axis=0, keepdims=True)
            for h in range(2)
        ]
        for h in range(2):
            delta_o[0, t, h : h + 1] = rows[h]
        delta_t.append(jnp.concatenate(rows, axis=0))
    one, two = group_inputs(meta, q_i, lse_i, g_t, delta_t)
    kv_w = weight(PAIR, 3 * PAIR)
    both, dq_t = group_backward(
        key_range(k_i, meta[12], 3), key_range(v_i, meta[12], 3), *one
    )
    dkv_o[0, 0:3] = both.reshape(3, CH, 2 * PAIR)
    d_ext[pl.ds(meta[16], 3)] += mm(both, kv_w, NT).reshape(3, CH, D)
    dq_o[0, 0] = pick_heads(dq_t, 0)
    both, dq_t = group_backward(
        key_range(k_i, meta[13], 2), key_range(v_i, meta[13], 2), *two
    )
    dkv_o[0, 3:5] = both.reshape(2, CH, 2 * PAIR)
    d_ext[pl.ds(meta[17], 2)] += mm(both, kv_w, NT).reshape(2, CH, D)
    dq_o[0, 1] = pick_heads(dq_t, 0)
    dq_o[0, 2] = pick_heads(dq_t, 1)

    @pl.when(step == groups - 1)
    def _():
        for j in range(3):
            rows = pl.ds(j * CH, CH)
            d_left[rows] = d_ext[j].astype(bf16)
            d_own[rows] = d_ext[3 + j]
            d_right[rows] = d_ext[6 + j].astype(bf16)


def attn_backward_near_kernel(groups, split, halves, meta, base, *refs):
    w_in, left, own, right, grad_in, q_i, k_i, v_i, o_i, lse_i = refs[:10]
    dq_i, dkv_i, g_i, delta_i, small = refs[10:15]
    w_grads = refs[15 : 15 + halves]
    d_own, small_o, ext_t, low_t, total, dq_all, w_all = refs[15 + halves :]
    step = pl.program_id(0)

    @pl.when(step == 0)
    def _():
        for index, part in enumerate((left, own, right)):
            for j in range(3):
                ext_t[3 * index + j] = part[pl.ds(j * CH, CH)].T
        for j in range(3):
            low_t[:, j * CH : (j + 1) * CH] = grad_in[pl.ds(j * CH, CH)].astype(bf16).T
        total[...] = jnp.zeros_like(total)
        small_o[...] = small[...]

    def weight(begin, end):
        return w_in[:, 0, :, begin:end].reshape(D, end - begin)

    def columns(begin, count):
        return jnp.concatenate([ext_t[begin + i] for i in range(count)], axis=1)

    g_t = [g_i[0, t] for t in range(3)]
    delta_t = [delta_i[0, t] for t in range(3)]
    one, two = group_inputs(meta, q_i, lse_i, g_t, delta_t)
    kv_w = weight(PAIR, 3 * PAIR)
    first, dq_one = group_backward(
        key_range(k_i, meta[14], 1), key_range(v_i, meta[14], 1), *one
    )
    second, dq_two = group_backward(
        key_range(k_i, meta[15], 2), key_range(v_i, meta[15], 2), *two
    )
    total[meta[18] - 3] += mm(first, kv_w, NT)
    total[pl.ds(meta[19] - 3, 2)] += mm(second, kv_w, NT).reshape(2, CH, D)
    for t, part in enumerate((pick_heads(dq_one, 0), pick_heads(dq_two, 0), pick_heads(dq_two, 1))):
        whole = ((dq_i[0, t] + part).T * (1.0 / math.sqrt(HEAD_DIM))).astype(bf16)
        j = meta[9 + t]
        dq_all[pl.ds(pl.multiple_of(j * CH, CH), CH)] = whole
        total[j] += mm(whole, weight(0, PAIR), NT)
    out_grad = mm(low_t[...], o_i[0].reshape(3 * CH, PAIR)).astype(bf16)
    w_all[:, 3 * PAIR :] = out_grad
    q_grad = mm(columns(3, 3), dq_all[...]).astype(bf16)
    w_all[:, :PAIR] = q_grad
    kv_grad = (
        mm(columns(meta[16], 3), dkv_i[0, 0:3].reshape(3 * CH, 2 * PAIR))
        + mm(columns(meta[17], 2), dkv_i[0, 3:5].reshape(2 * CH, 2 * PAIR))
        + mm(columns(meta[18], 1), first)
        + mm(columns(meta[19], 2), second)
    )
    w_all[:, PAIR : 3 * PAIR] = kv_grad.astype(bf16)
    high = D // split
    for apart in range(split):
        rows = pl.ds(pl.multiple_of((base[0] ^ apart) * high, high), high)
        w_grads[apart % halves][(apart // halves) * groups + step] = w_all[rows]

    @pl.when(step == groups - 1)
    def _():
        d_own[...] = total[...].reshape(3 * CH, D)


def attn_backward_far(weight, meta, grad_in, kept, groups, small, after=()):
    rows = grad_in.shape[0]
    const = lambda s, *_: (0, 0)
    pair = lambda s, *_: (s, 0, 0, 0)
    full = pl.BlockSpec((rows, D), const)
    three = pl.BlockSpec((1, 3, CH, PAIR), pair)
    eight = pl.BlockSpec((1, 2 * SLOT, CH, PAIR), pair)
    lines = pl.BlockSpec((1, 3, 8, CH), pair)
    tiny = pl.BlockSpec((8, D), const)
    return pl.pallas_call(
        after_operands(functools.partial(attn_backward_far_kernel, groups), 1, len(after)),
        grid_spec=pltpu.PrefetchScalarGridSpec(
            num_scalar_prefetch=1,
            grid=(groups,),
            in_specs=[hbm()] * len(after)
            + [weight_spec(*weight), full, tiny, three, eight, eight, three, lines],
            out_specs=[
                full,
                full,
                full,
                pl.BlockSpec((1, 3, PAIR, CH), pair),
                pl.BlockSpec((1, 5, CH, 2 * PAIR), pair),
                three,
                lines,
                tiny,
            ],
            scratch_shapes=[
                pltpu.VMEM((3, CH, D), bf16),
                pltpu.VMEM((9, CH, D), f32),
            ],
        ),
        out_shape=[
            jax.ShapeDtypeStruct((rows, D), bf16),
            jax.ShapeDtypeStruct((rows, D), f32),
            jax.ShapeDtypeStruct((rows, D), bf16),
            jax.ShapeDtypeStruct((groups, 3, PAIR, CH), f32),
            jax.ShapeDtypeStruct((groups, 5, CH, 2 * PAIR), bf16),
            jax.ShapeDtypeStruct((groups, 3, CH, PAIR), bf16),
            jax.ShapeDtypeStruct((groups, 3, 8, CH), f32),
            jax.ShapeDtypeStruct((8, D), f32),
        ],
        compiler_params=params(28),
        cost_estimate=pl.CostEstimate(
            flops=24_000_000_000, bytes_accessed=16_000_000, transcendentals=0
        ),
        name="attn_backward_far",
    )(meta, *from_hbm(*after, weight[0], grad_in), small, *from_hbm(*kept))


def attn_backward_near(weight, meta, base, ext, grad_in, kept, far, groups, split, small, halves):
    rows = grad_in.shape[0]
    const = lambda s, *_: (0, 0)
    pair = lambda s, *_: (s, 0, 0, 0)
    full = pl.BlockSpec((rows, D), const)
    three = pl.BlockSpec((1, 3, CH, PAIR), pair)
    eight = pl.BlockSpec((1, 2 * SLOT, CH, PAIR), pair)
    lines = pl.BlockSpec((1, 3, 8, CH), pair)
    tiny = pl.BlockSpec((8, D), const)
    places = split * groups
    return pl.pallas_call(
        functools.partial(attn_backward_near_kernel, groups, split, halves),
        grid_spec=pltpu.PrefetchScalarGridSpec(
            num_scalar_prefetch=2,
            grid=(groups,),
            in_specs=[weight_spec(*weight), full, full, full, full, three, eight, eight, three, lines]
            + [
                pl.BlockSpec((1, 3, PAIR, CH), pair),
                pl.BlockSpec((1, 5, CH, 2 * PAIR), pair),
                three,
                lines,
                tiny,
            ],
            out_specs=[pl.BlockSpec((places // halves, D // split, D), lambda s, *_: (0, 0, 0))]
            * halves
            + [full, tiny],
            scratch_shapes=[
                pltpu.VMEM((9, D, CH), bf16),
                pltpu.VMEM((D, rows), bf16),
                pltpu.VMEM((3, CH, D), f32),
                pltpu.VMEM((rows, PAIR), bf16),
                pltpu.VMEM((D, D), bf16),
            ],
        ),
        out_shape=[jax.ShapeDtypeStruct((places // halves, D // split, D), bf16)] * halves
        + [jax.ShapeDtypeStruct((rows, D), f32), jax.ShapeDtypeStruct((8, D), f32)],
        compiler_params=params(28),
        cost_estimate=pl.CostEstimate(
            flops=20_000_000_000, bytes_accessed=22_000_000, transcendentals=0
        ),
        name="attn_backward_near",
    )(meta, base, *from_hbm(weight[0], *ext), grad_in, *from_hbm(*kept), *far, small)


def entry_backward_kernel(
    grad_in, d_own, d_near, d_left, d_right, source, norm, ids, grad_out, small
):
    small[...] = jnp.zeros_like(small)
    for j in range(3):
        rows = pl.ds(j * CH, CH)
        arrived = d_own[rows] + d_near[rows] + d_left[rows].astype(f32) + d_right[rows].astype(f32)
        back, gain_grad, shift_grad = norm_backward(arrived, source[rows], norm[0:1])
        values = grad_in[rows] + back
        grad_out[rows] = values
        small[0:1] += gain_grad
        small[1:2] += shift_grad
        letter = lax.broadcasted_iota(jnp.int32, (32, CH), 0)
        chosen = (letter == ids[:, j * CH : (j + 1) * CH]).astype(bf16)
        high = values.astype(bf16)
        rest = values - high.astype(f32)
        middle = rest.astype(bf16)
        low = (rest - middle.astype(f32)).astype(bf16)
        small[8:40] += mm(chosen, high) + mm(chosen, middle) + mm(chosen, low)


def entry_backward(grad_in, d_own, d_near, d_left, d_right, source, norm, ids, after=()):
    rows = grad_in.shape[0]
    return pl.pallas_call(
        after_operands(entry_backward_kernel, 0, len(after)),
        in_specs=[hbm()] * len(after) + [vmem()] * 8,
        out_specs=[vmem()] * 2,
        out_shape=[
            kept_out((rows, D), f32),
            jax.ShapeDtypeStruct((40, D), f32),
        ],
        compiler_params=pltpu.CompilerParams(vmem_limit_bytes=40 * 1024 * 1024),
        cost_estimate=pl.CostEstimate(
            flops=100_000_000, bytes_accessed=9_000_000, transcendentals=0
        ),
        name="entry_backward",
    )(*after, grad_in, d_own, d_near, d_left, d_right, source, norm, ids)


def backward_plan(my_mp, row_start, first_seq, chunk_seq):
    lead = jnp.where(my_mp < 2, 0, 2)
    late_one = my_mp % 2 == 0
    late_two = my_mp < 2
    found = [lead, 1, 2 - lead]
    lead_seq = jnp.where(my_mp < 2, chunk_seq[0], chunk_seq[2])
    shifts = [
        (lead_seq, jnp.where(late_one, 1, 0)),
        (chunk_seq[1], jnp.where(late_two, 2, 0)),
        (lead_seq, jnp.where(late_one, 0, 3)),
        (chunk_seq[1], jnp.where(late_two, 0, 2)),
    ]
    found += [(seq - first_seq) * SLOT + shift for seq, shift in shifts]
    found += [3 + (seq * LEN - row_start) // CH + shift for seq, shift in shifts]
    return [jnp.asarray(entry) for entry in found]


def shards(
    token_ids,
    timesteps,
    importance,
    cotangent,
    qkv_weight,
    out_weight,
    up_weight,
    down_weight,
    norm_params,
    embed_table,
    qkv_first,
    qkv_second,
    out_first,
    out_second,
    up_first,
    up_second,
    down_first,
    down_second,
    norm_first,
    norm_second,
    embed_first,
    embed_second,
):
    dp, mp = lax.axis_size("dp"), lax.axis_size("mp")
    small = dp == 8 and mp == 4
    groups = mp
    split = dp if small else 1
    row_count = token_ids.shape[0]
    seq_here = timesteps.shape[0]
    high = D // dp
    my_mp = lax.axis_index("mp")
    my_dp = lax.axis_index("dp")
    row_start = my_mp * row_count

    first_seq = row_start // LEN
    last_seq = (row_start + row_count - 1) // LEN
    chunk_seq = [(row_start + CH * j) // LEN for j in range(3)]
    meta = jnp.stack(
        [
            3 + (first_seq * LEN - row_start) // CH,
            3 + (last_seq * LEN - row_start) // CH,
            last_seq - first_seq + 1,
        ]
        + [seq - first_seq for seq in chunk_seq]
        + chunk_seq
        + backward_plan(my_mp, row_start, first_seq, chunk_seq)
    ).astype(jnp.int32)
    in_order = jnp.arange(split * groups, dtype=jnp.int32)
    owner = block_owners(my_dp) if small else in_order
    base = jnp.where(small, my_dp, 0).astype(jnp.int32)[None]
    halves = 2 if small else 1

    attn_mine = []
    mlp_mine = []
    for layer in range(LAYERS):
        attn_mine.append(
            jnp.concatenate(
                [qkv_weight[layer].reshape(high, -1), out_weight[layer].T], axis=1
            ).astype(bf16)
        )
        mlp_mine.append(
            jnp.concatenate([up_weight[layer], down_weight[layer].T], axis=1).astype(bf16)
        )
    both_mine = jnp.concatenate([attn_mine[1], mlp_mine[1]], axis=1)
    if small:
        lines = row_count // D + (row_count % D > 0)
        ids_low = jnp.pad(token_ids.astype(bf16), (0, lines * D - row_count)).reshape(lines, D)
        first_mine = jnp.concatenate([attn_mine[0], ids_low], axis=0)
        first_z = gather_z(first_mine)
        attn_z = first_z[:, :high]
        ids_z = first_z[:, high:].reshape(4, lines * D)[:, :row_count].astype(jnp.int32)
        ids_left = ids_z[my_mp ^ jnp.maximum(my_mp - 1, 0)]
        ids_right = ids_z[my_mp ^ jnp.minimum(my_mp + 1, mp - 1)]
    else:
        ids_left, ids_right = shift_right(token_ids), shift_left(token_ids)
    ids_ext = jnp.concatenate([ids_left, token_ids, ids_right])
    seq_ext = (row_start - row_count + jnp.arange(3 * row_count, dtype=jnp.int32)) // LEN
    letters = (ids_ext[:, None] == jnp.arange(VOCAB, dtype=jnp.int32)[None, :]).astype(f32)
    member = (seq_ext[:, None] == jnp.arange(seq_here, dtype=jnp.int32)[None, :]).astype(f32)
    entry_ext = jnp.dot(letters, embed_table, precision=highest) + jnp.dot(
        member, time_features(timesteps), precision=highest
    )
    normed_ext = layer_norm(entry_ext, norm_params[0, 0], norm_params[0, 1]).astype(bf16)
    resid = entry_ext[row_count : 2 * row_count]
    ext = (
        normed_ext[:row_count],
        normed_ext[row_count : 2 * row_count],
        normed_ext[2 * row_count :],
    )

    if small:
        mlp_first, attn_z = tie(mlp_mine[0], attn_z)
        attn_sent = [flip(attn_z, bits) for bits in (8, 16, 24)]
        attn_sent, (ext, resid) = tie(attn_sent, (ext, resid))
        attn_xy = jnp.concatenate([attn_z] + list(attn_sent), axis=0)
        mlp_z = gather_z(mlp_first)
        mlp_z, attn_xy = tie(mlp_z, attn_xy)
        attn_w = [(attn_xy, flip(attn_xy, 4))]
        mlp_found = gather_dp(mlp_z)
        both_mine, mlp_z = tie(both_mine, mlp_z)
        both_sent = [flip(both_mine, bits) for bits in (1, 2, 3)]
    else:
        attn_w = [plain_gather(attn_mine[0])]
        mlp_found = plain_gather(mlp_mine[0])
        attn_w.append(plain_gather(both_mine))
        mlp_w = [((mlp_found, 0), (mlp_found, 1)), ((attn_w[1], 1), (attn_w[1], 2))]

    kept = []
    for layer in range(LAYERS):
        last = layer == LAYERS - 1
        outs, w_attn = attn_forward(
            attn_w[layer], meta, owner, *ext, resid, norm_params[layer], groups
        )
        middle, normed = outs[:2]
        if small and layer == 0:
            both_sent, normed = tie(both_sent, normed)
            both_z = jnp.stack([both_mine] + list(both_sent))
            last_found = gather_dp(both_z[:, :, D:])
            mlp_w = [((mlp_found, 0), (mlp_found, 1)), ((last_found, 0), (last_found, 1))]
            attn_z = both_z[:, :, :D]
            attn_z, (normed, mlp_found) = tie(attn_z, (normed, mlp_found))
            attn_sent = [flip(attn_z, bits) for bits in (8, 16, 24)]
            mlp_w[0] = ((mlp_found, 0), (mlp_found, 1))
        w_mlp = mlp_w[layer]
        if layer + 1 < LAYERS:
            mlp_outs, w_mlp = mlp_forward(
                w_mlp, owner, normed, middle, norm_params[layer + 1], groups
            )
        kept.append((ext, resid, middle, normed, outs[2:], mlp_outs[1:3], (w_attn, 0), w_mlp))
        if layer + 1 < LAYERS:
            resid, following = mlp_outs[0], mlp_outs[3]
            if small:
                attn_sent, following = tie(attn_sent, following)
                attn_xy = jnp.concatenate([attn_z] + list(attn_sent), axis=0)
                attn_w.append((attn_xy, flip(attn_xy, 4)))
            ext = (shift_right(following), following, shift_left(following))

    norm_grads = [[None] * 4 for _ in range(LAYERS)]
    attn_grads = [None] * LAYERS
    mlp_grads = [None] * LAYERS
    after = ()
    for layer in reversed(range(LAYERS)):
        ext, source, middle, normed, attn_kept, (act, slope), w_attn, w_mlp = kept[layer]
        norm = norm_params[layer]
        if layer + 1 == LAYERS:
            activations, mlp_grad, grad_mid, n_grad = mlp_last(
                w_mlp, meta, in_order, importance, cotangent, normed, middle, norm, groups, split
            )
        else:
            mlp_grad, grad_mid, n_grad = mlp_backward(
                w_mlp,
                meta,
                in_order,
                begin,
                act,
                slope,
                normed,
                middle,
                norm,
                groups,
                split,
                after,
            )
        after = ()
        if small:
            if layer + 1 < LAYERS:
                attn_found, (mlp_grad, grad_mid) = tie(attn_found, (mlp_grad, grad_mid))
            mlp_rows = scatter_dp(mlp_grad, dp)
            if layer + 1 < LAYERS:
                attn_rows = add_four(attn_mine_rows, attn_found, False)
                above = jnp.concatenate([attn_rows, above], axis=2)
                above_mine, above_found = scatter_four(above, 1)
                after = (attn_rows,)
        d_left, d_own, d_right, *far, n_grad = attn_backward_far(
            w_attn, meta, grad_mid, attn_kept, groups, n_grad, after
        )
        if small and layer + 1 < LAYERS:
            above_found, (d_left, d_right) = tie(above_found, (d_left, d_right))
        from_right = shift_left(d_left)
        from_left = shift_right(d_right)
        *attn_grad, d_near, n_grad = attn_backward_near(
            w_attn, meta, base, ext, grad_mid, attn_kept, far, groups, split, n_grad, halves
        )
        (from_left, from_right), (attn_grad, d_near) = tie(
            (from_left, from_right), (attn_grad, d_near)
        )
        after = ()
        if not small:
            mlp_grads[layer] = plain_scatter(mlp_grad, dp)
            attn_grads[layer] = plain_scatter(attn_grad[0], dp)
        elif layer + 1 == LAYERS:
            attn_held = scatter_core(*attn_grad)
            attn_mine_rows, attn_found = scatter_four(attn_held, 8)
            above = mlp_rows
            after = (attn_held,)
        else:
            above_total = add_four(above_mine, above_found, True)
            attn_grads[1] = above_total[:, :D]
            mlp_grads[1] = above_total[:, D:]
        norm_grads[layer][2:] = [n_grad[2], n_grad[3]]
        if layer + 1 < LAYERS:
            norm_grads[layer + 1][:2] = [n_grad[0], n_grad[1]]
        begin = (grad_mid, d_own, d_near, from_left, from_right, source, norm_params[layer])
    input_grad, reduced = entry_backward(*begin, token_ids[None, :])
    norm_grads[0][:2] = [reduced[0], reduced[1]]
    stacked = jnp.concatenate(
        [jnp.stack([row for rows in norm_grads for row in rows]), reduced[8:40]], axis=0
    )
    if small:
        rows = D // dp
        rest = stacked.astype(bf16)
        rest = (rest.astype(f32) + flip(rest, 4).astype(f32)).astype(bf16)
        held = scatter_core(*attn_grad).reshape(16 * rows, D)
        sent = [
            flip(jnp.concatenate([held[4 * rows * i : 4 * rows * (i + 1)], rest], axis=0), 8 * i)
            for i in (1, 2, 3)
        ]
        mlp_own, mlp_sent = scatter_four(mlp_rows, 1)
        mlp_sent, sent = tie(mlp_sent, sent)
        mine = add_four(jnp.concatenate([held[: 4 * rows], rest], axis=0)[None], [p[None] for p in sent], True)
        held, rest = mine[: 4 * rows].astype(bf16), mine[4 * rows :].astype(bf16)
        sent = [
            flip(jnp.concatenate([held[rows * i : rows * (i + 1)], rest], axis=0), i)
            for i in (1, 2, 3)
        ]
        total = add_four(
            jnp.concatenate([held[:rows], rest], axis=0)[None], [p[None] for p in sent], True
        )
        attn_grads[0] = total[:rows]
        stacked = total[rows:]
        mlp_grads[0] = add_four(mlp_own, mlp_sent, True)
    else:
        stacked = lax.psum(stacked, ALL)
    norm_grad = stacked[: 4 * LAYERS].reshape(LAYERS, 4, D)
    embed_grad = stacked[4 * LAYERS : 4 * LAYERS + VOCAB]

    qkv_grad = jnp.stack([g[:, : 3 * PAIR].reshape(high, 3, PAIR) for g in attn_grads])
    out_grad = jnp.stack([g[:, 3 * PAIR :].T for g in attn_grads])
    up_grad = jnp.stack([g[:, :D] for g in mlp_grads])
    down_grad = jnp.stack([g[:, D:].T for g in mlp_grads])
    qkv_master, qkv_mean, qkv_square = adamw(
        qkv_weight, qkv_first, qkv_second, qkv_grad, 2.0 / math.sqrt(D), decay_matrix
    )
    out_master, out_mean, out_square = adamw(
        out_weight, out_first, out_second, out_grad, 2.0 / math.sqrt(D), decay_matrix
    )
    up_master, up_mean, up_square = adamw(
        up_weight, up_first, up_second, up_grad, 2.0 / math.sqrt(D), decay_matrix
    )
    down_master, down_mean, down_square = adamw(
        down_weight, down_first, down_second, down_grad, 2.0 / math.sqrt(FF), decay_matrix
    )
    norm_master, norm_mean, norm_square = adamw(
        norm_params, norm_first, norm_second, norm_grad, vector_rate, 0.0
    )
    embed_master, embed_mean, embed_square = adamw(
        embed_table, embed_first, embed_second, embed_grad, embed_rate, 0.0
    )
    return (
        activations,
        input_grad,
        qkv_master,
        qkv_mean,
        qkv_square,
        qkv_master.astype(bf16),
        out_master,
        out_mean,
        out_square,
        out_master.astype(bf16),
        up_master,
        up_mean,
        up_square,
        up_master.astype(bf16),
        down_master,
        down_mean,
        down_square,
        down_master.astype(bf16),
        norm_master,
        norm_mean,
        norm_square,
        embed_master,
        embed_mean,
        embed_square,
    )


def solution(mesh):
    rows = P(("dp", "mp"), None)
    qkv = P(None, "dp", None, "mp")
    wide = P(None, "mp", "dp")
    tall = P(None, "dp", "mp")
    same = P()
    return jax.shard_map(
        shards,
        mesh=mesh,
        in_specs=(P(("dp", "mp")), P("dp"), P("dp"), rows, qkv, wide, tall, wide, same, same)
        + (qkv, qkv, wide, wide, tall, tall, wide, wide, same, same, same, same),
        out_specs=(rows, rows)
        + (qkv,) * 4
        + (wide,) * 4
        + (tall,) * 4
        + (wide,) * 4
        + (same,) * 6,
        check_vma=False,
    )
```
